128 devices in a mesh: fsdp: 32 (over y_hi, z, x), tensor: 4 (over y_lo, core).
Axes of the slice: x: 4, y: 4 (y_hi: 2, y_lo: 2; y = y_hi * 2 + y_lo), z: 4, core: 2. Of those that a mesh axis runs over, the one named last changes fastest.
Arguments:
- tokens: bfloat16 [2, 32, 256, 1024], P(None, 'fsdp', 'tensor'), may hold values from -6 to 6
- dealt: int32 [2, 32], P(None, 'fsdp'), may hold values 0 or 1
- cotangent: bfloat16 [2, 32, 256, 1024], P(None, 'fsdp', 'tensor'), may hold values from -6 to 6
- qkv_weight: bfloat16 [1, 1024, 3, 1024], P(None, 'fsdp', None, 'tensor'), may hold values from -0.1875 to 0.1875
- out_weight: bfloat16 [1, 1024, 1024], P(None, 'fsdp', 'tensor'), may hold values from -1.5 to 1.5
- up_weight: bfloat16 [1, 1024, 4096], P(None, 'fsdp', 'tensor'), may hold values from -0.1875 to 0.1875
- down_weight: bfloat16 [1, 1024, 4096], P(None, 'fsdp', 'tensor'), may hold values from -0.09375 to 0.09375
- norm1_gain: float32 [1, 1024], replicated, may hold values from 0.25 to 1.75
- norm1_bias: float32 [1, 1024], replicated, may hold values from -3 to 3
- query_bias: float32 [1, 1024], replicated, may hold values from -3 to 3
- value_bias: float32 [1, 1024], replicated, may hold values from -3 to 3
- out_bias: float32 [1, 1024], replicated, may hold values from -3 to 3
- norm2_gain: float32 [1, 1024], replicated, may hold values from 0.25 to 1.75
- norm2_bias: float32 [1, 1024], replicated, may hold values from -3 to 3
- up_bias: float32 [1, 4096], replicated, may hold values from -3 to 3
- down_bias: float32 [1, 1024], replicated, may hold values from -3 to 3
Outputs:
- block_out: bfloat16 [2, 32, 256, 1024], P(None, 'fsdp', 'tensor')
- input_grad: bfloat16 [2, 32, 256, 1024], P(None, 'fsdp', 'tensor')
- qkv_grad: float32 [1, 1024, 3, 1024], P(None, 'fsdp', None, 'tensor')
- out_grad: float32 [1, 1024, 1024], P(None, 'fsdp', 'tensor')
- up_grad: float32 [1, 1024, 4096], P(None, 'fsdp', 'tensor')
- down_grad: float32 [1, 1024, 4096], P(None, 'fsdp', 'tensor')
- norm1_gain_grad: float32 [1, 1024], replicated
- norm1_bias_grad: float32 [1, 1024], replicated
- query_bias_grad: float32 [1, 1024], replicated
- value_bias_grad: float32 [1, 1024], replicated
- out_bias_grad: float32 [1, 1024], replicated
- norm2_gain_grad: float32 [1, 1024], replicated
- norm2_bias_grad: float32 [1, 1024], replicated
- up_bias_grad: float32 [1, 4096], replicated
- down_bias_grad: float32 [1, 1024], replicated
The draws below stay inside these ranges and needn't reach their ends.
Inputs may be any that keep to these rules, and one draw needn't show every extreme that they name: `dealt`: 1 where the slot holds an image of that micro-batch, 0 where it is empty.
All inputs are finite; a program needn't handle non-finite values. No bound on the sum of `dealt` on one device may be relied on, other than what follows from the above.
Results may differ from the reference program's by a relative error of at most 0.024.
Values may be sent and summed in bfloat16 or wider, within the bound.
No kernel may reach another device: no remote copies, remote signals or barrier semaphores. Data moves between devices by JAX's collectives and lax.ppermute only.
A program may use at most 64 MiB of HBM per device.

```python
import jax
import jax.numpy as jnp
from jax import lax

D = 1024
HEADS = 16
HEAD_DIM = 64
FF = 4096
SEQ = 256
MB = 2
LAYERS = 1
SLOTS = 32


def place_ends(entries, own_key, low, largest):
    longest = entries.shape.index(max(entries.shape))
    spots = []
    for shift in (0, 1):
        where = [jax.random.randint(jax.random.fold_in(own_key, axis), (), 0, length) for axis, length in enumerate(entries.shape)]
        where[longest] = (where[longest] + shift) % entries.shape[longest]
        spots.append(tuple(where))
    return entries.at[spots[0]].set(low).at[spots[1]].set(largest)


def spiked(values, own_key, source, target, parts, factor):
    def block_of(dim):
        return (jnp.arange(values.shape[dim]) // (values.shape[dim] // parts)).reshape((-1,) + (1,) * (values.ndim - 1 - dim))

    one_side = jax.random.permutation(own_key, parts)[block_of(target)]
    other_side = (block_of(target) + parts // 2) % parts
    return jnp.where((block_of(source) == one_side) | (block_of(source) == other_side), factor * values, values)


def levels(rng, dims, cuts, smallest, high):
    loudness = 1.0
    for dim, parts in cuts:
        steps = jax.random.uniform(jax.random.fold_in(jax.random.fold_in(rng, 6), dim), (parts,), jnp.float32, smallest / len(cuts), high / len(cuts))
        loudness = loudness * jnp.repeat(jnp.exp(steps), dims[dim] // parts).reshape((-1,) + (1,) * (len(dims) - 1 - dim))
    return loudness


def centred(stream_key, shape, deviation, reach, pieces=(), kind=jnp.bfloat16):
    drawn = deviation * jax.random.normal(stream_key, shape, jnp.float32)
    if pieces:
        drawn = drawn * levels(stream_key, shape, pieces, -0.22, 0.18)
    return jnp.clip(drawn, -reach, reach).astype(kind)


def noise_with(rng, shape, scale, limit, split, heavy, held_as=jnp.bfloat16):
    drawn = scale * jax.random.normal(rng, shape, jnp.float32)
    if split:
        drawn = drawn * levels(rng, shape, split, -0.22, 0.18)
    return jnp.clip(spiked(drawn, jax.random.fold_in(rng, 3), *heavy), -limit, limit).astype(held_as)


def setup_inputs(seed: int = 0) -> dict:
    arg_keys = jax.random.split(jax.random.key(seed), 17)
    return {
        "tokens": noise_with(arg_keys[0], (MB, SLOTS, SEQ, D), 1.0, 6.0, ((1, 32), (2, 4)), (1, 3, 32, 2.75)),
        "dealt": place_ends((jax.random.randint(arg_keys[1], (MB, SLOTS), 0, 3) < 2).astype(jnp.int32), jax.random.fold_in(arg_keys[1], 1), 0, 1),
        "cotangent": noise_with(arg_keys[2], (MB, SLOTS, SEQ, D), 1.0, 6.0, ((1, 32), (2, 4)), (1, 3, 32, 2.75)),
        "qkv_weight": centred(arg_keys[3], (LAYERS, D, 3, D), D ** -0.5, 0.1875, ((1, 32), (3, 4))),
        "out_weight": centred(arg_keys[4], (LAYERS, D, D), (D // 64) ** -0.5, 1.5, ((1, 32), (2, 4))),
        "up_weight": centred(arg_keys[5], (LAYERS, D, FF), D ** -0.5, 0.1875, ((1, 32), (2, 4))),
        "down_weight": centred(arg_keys[6], (LAYERS, D, FF), FF ** -0.5, 0.09375, ((1, 32), (2, 4))),
        "norm1_gain": jnp.clip(1.0 + 0.15 * jax.random.normal(arg_keys[7], (LAYERS, D), jnp.float32), 0.25, 1.75),
        "norm1_bias": centred(arg_keys[8], (LAYERS, D), 0.5, 3.0, (), jnp.float32),
        "query_bias": centred(arg_keys[9], (LAYERS, D), 0.5, 3.0, (), jnp.float32),
        "value_bias": centred(arg_keys[10], (LAYERS, D), 0.5, 3.0, (), jnp.float32),
        "out_bias": centred(arg_keys[11], (LAYERS, D), 0.5, 3.0, (), jnp.float32),
        "norm2_gain": jnp.clip(1.0 + 0.15 * jax.random.normal(arg_keys[12], (LAYERS, D), jnp.float32), 0.25, 1.75),
        "norm2_bias": centred(arg_keys[13], (LAYERS, D), 0.5, 3.0, (), jnp.float32),
        "up_bias": centred(arg_keys[14], (LAYERS, FF), 0.5, 3.0, (), jnp.float32),
        "down_bias": centred(arg_keys[15], (LAYERS, D), 0.5, 3.0, (), jnp.float32),
    }


@jax.custom_vjp
def low(v):
    return lax.optimization_barrier(v.astype(jnp.bfloat16)).astype(jnp.float32)

@jax.custom_vjp
def low_back(v):
    return v

def low_keep(v):
    return (low(v), None)

def low_pass(kept, grad):
    return (grad,)

def back_keep(v):
    return (v, None)

def back_low(kept, grad):
    return (low(grad),)
low.defvjp(low_keep, low_pass)
low_back.defvjp(back_keep, back_low)
EPS_NORM = 1e-06
HIGH = lax.Precision.HIGHEST

def layer_norm(values, gain, shift):
    center = values - lax.optimization_barrier(jnp.mean(values, axis=-1, keepdims=True))
    spread = lax.optimization_barrier(jnp.mean(center * center, axis=-1, keepdims=True))
    return center * lax.rsqrt(spread + EPS_NORM) * gain + shift

def split_heads(values):
    return values.reshape(values.shape[0], values.shape[1], HEADS, HEAD_DIM)

def block(hidden, params):
    qkv_w, out_w, up_w, down_w, gain_one, shift_one, query_b, value_b, out_b, gain_two, shift_two, up_b, down_b = params
    normed = low(layer_norm(hidden, gain_one, shift_one))
    joined = jnp.einsum('gsd,dcf->gscf', normed, qkv_w, precision=HIGH)
    query = low_back(low(joined[:, :, 0] + query_b))
    keys = low_back(low(joined[:, :, 1]))
    values = low_back(low(joined[:, :, 2] + value_b))
    scores = jnp.einsum('gshe,gthe->ghst', split_heads(query), split_heads(keys), precision=HIGH) * HEAD_DIM ** (-0.5)
    scores = low_back(scores)
    probs = low(jax.nn.softmax(scores, axis=-1))
    mixed = jnp.einsum('ghst,gthe->gshe', probs, split_heads(values), precision=HIGH).reshape(hidden.shape)
    mixed = low_back(low(mixed))
    attended = low_back(jnp.einsum('gsd,ed->gse', mixed, out_w, precision=HIGH) + out_b)
    middle = hidden + attended
    normed_two = low(layer_norm(middle, gain_two, shift_two))
    upward = low_back(jnp.einsum('gsd,df->gsf', normed_two, up_w, precision=HIGH) + up_b)
    activated = low(jax.nn.gelu(upward, approximate=False))
    downward = low_back(jnp.einsum('gsf,ef->gse', activated, down_w, precision=HIGH) + down_b)
    return middle + downward

def reference(tokens, dealt, cotangent, qkv_weight, out_weight, up_weight, down_weight, norm1_gain, norm1_bias, query_bias, value_bias, out_bias, norm2_gain, norm2_bias, up_bias, down_bias):
    count = MB * SLOTS
    group = 1
    while count % (2 * group) == 0 and 2 * group * SEQ <= 4096:
        group = 2 * group
    flat_in = tokens.astype(jnp.float32).reshape(count // group, group, SEQ, D)
    flat_cot = cotangent.astype(jnp.float32).reshape(count // group, group, SEQ, D)
    flat_live = dealt.astype(jnp.float32).reshape(count // group, group)
    params = tuple((param.astype(jnp.float32) for param in (qkv_weight, out_weight, up_weight, down_weight, norm1_gain, norm1_bias, query_bias, value_bias, out_bias, norm2_gain, norm2_bias, up_bias, down_bias)))

    def forward(block_in, live_flags, *weights):
        hidden = block_in
        for layer in range(LAYERS):
            hidden = block(hidden, [weight[layer] for weight in weights])
        return hidden * live_flags[:, None, None]

    def step(totals, items):
        block_in, cot_in, live_flags = items
        result, pull = jax.vjp(lambda first, *rest: forward(first, live_flags, *rest), block_in, *params)
        grads = pull(cot_in)
        return (tuple((total + grad for total, grad in zip(totals, grads[1:]))), (result, grads[0]))
    start = tuple((jnp.zeros(param.shape, jnp.float32) for param in params))
    totals, outputs = lax.scan(step, start, (flat_in, flat_cot, flat_live))
    results, input_grads = outputs
    full_shape = (MB, SLOTS, SEQ, D)
    return (results.reshape(full_shape).astype(jnp.bfloat16), input_grads.reshape(full_shape).astype(jnp.bfloat16), totals[0], totals[1], totals[2], totals[3], totals[4], totals[5], totals[6], totals[7], totals[8], totals[9], totals[10], totals[11], totals[12])
```

```python
import jax
import jax.numpy as jnp
from jax import lax
from jax.sharding import PartitionSpec as P

HEAD_DIM = 64
EPS_NORM = 1e-06
BF = jnp.bfloat16
F32 = jnp.float32

YH, ZN, XN = 2, 4, 4


def fsdp_perm(dx, dz, dy):
    pairs = []
    for source in range(YH * ZN * XN):
        yh, z, x = source // (ZN * XN), (source // XN) % ZN, source % XN
        target = (((yh + dy) % YH) * ZN + (z + dz) % ZN) * XN + (x + dx) % XN
        pairs.append((source, target))
    return pairs


def hop(array, axis, step):
    move = {"x": (step, 0, 0), "z": (0, step, 0), "y": (0, 0, step)}[axis]
    return lax.ppermute(array, "fsdp", fsdp_perm(*move))


def swap(array, mask):
    return lax.ppermute(array, "tensor", [(i, i ^ mask) for i in range(4)])


def place(pieces, me, axis):
    shape = pieces[0].shape
    out = jnp.zeros(shape[:axis] + (len(pieces),) + shape[axis:], pieces[0].dtype)
    for step, piece in enumerate(pieces):
        out = lax.dynamic_update_index_in_dim(out, piece, (me + step) % len(pieces), axis)
    return out


def take(array, index, axis):
    return lax.dynamic_index_in_dim(array, index % array.shape[axis], axis, keepdims=False)


def ring_gather(block, axis, cut):
    left = hop(block, axis, 1)
    right = hop(block, axis, -1)
    half = block.shape[cut] // 2
    first = hop(lax.slice_in_dim(left, 0, half, axis=cut), axis, 1)
    second = hop(lax.slice_in_dim(right, half, 2 * half, axis=cut), axis, -1)
    return [block, right, jnp.concatenate([first, second], axis=cut), left]


def near_gather(block, axis):
    left = hop(block, axis, 1)
    right = hop(block, axis, -1)
    far = hop(block, axis, 2)
    return [block, right, far, left]


def gather_rows(half_a, half_b, where):
    yh, z, x = where
    width = half_a.shape[1]
    own = jnp.concatenate([half_a, half_b], axis=1)
    other = hop(own, "y", 1)
    both = jnp.stack([jnp.where(yh == 0, own, other), jnp.where(yh == 0, other, own)])
    part_a, part_b = both[..., :width], both[..., width:]
    part_a = place(near_gather(part_a, "x"), x, 1)
    part_b = place(near_gather(part_b, "z"), z, 1)
    full_a = place(ring_gather(part_a, "z", 1), z, 1)
    full_b = place(ring_gather(part_b, "x", 1), x, 2)
    return full_a.reshape(-1, width), full_b.reshape(-1, half_b.shape[1])


def ring_scatter(array, axis, me, dim, cut):
    far = take(array, me + 2, dim)
    half = far.shape[cut] // 2
    go_right = hop(lax.slice_in_dim(far, 0, half, axis=cut), axis, 1)
    go_left = hop(lax.slice_in_dim(far, half, 2 * half, axis=cut), axis, -1)
    nxt = take(array, me + 1, dim)
    prv = take(array, me + 3, dim)
    nxt_low, nxt_high = jnp.split(nxt, 2, axis=cut)
    prv_low, prv_high = jnp.split(prv, 2, axis=cut)
    to_right = jnp.concatenate([add(nxt_low, go_right), nxt_high], axis=cut)
    to_left = jnp.concatenate([prv_low, add(prv_high, go_left)], axis=cut)
    from_left = hop(to_right, axis, 1)
    from_right = hop(to_left, axis, -1)
    return add(take(array, me, dim), from_left, from_right)


def near_scatter(array, axis, me, dim):
    from_left = hop(take(array, me + 1, dim), axis, 1)
    from_right = hop(take(array, me + 3, dim), axis, -1)
    from_far = hop(take(array, me + 2, dim), axis, 2)
    return add(take(array, me, dim), from_left, from_right, from_far)


def add(*terms):
    total = terms[0].astype(F32)
    for term in terms[1:]:
        total = total + term.astype(F32)
    return total.astype(BF)


def scatter_rows(full_a, full_b, where):
    yh, z, x = where
    shape = (YH, ZN, XN, -1)
    part_a = ring_scatter(full_a.reshape(shape + (full_a.shape[1],)), "z", z, 1, 1)
    part_b = ring_scatter(full_b.reshape(shape + (full_b.shape[1],)), "x", x, 2, 1)
    part_a = near_scatter(part_a, "x", x, 1)
    part_b = near_scatter(part_b, "z", z, 1)
    both = jnp.concatenate([part_a, part_b], axis=-1)
    arrived = hop(take(both, yh + 1, 0), "y", 1)
    return take(both, yh, 0).astype(F32) + arrived.astype(F32)


def spread_rows(own):
    across = swap(own, 2)
    beside = swap(jnp.stack([own, across], axis=1), 1)
    return jnp.stack([own, beside[:, 0], across, beside[:, 1]], axis=1)


def collect_rows(partial):
    sent = jnp.stack([partial[:, 1], partial[:, 3]], axis=1).astype(BF)
    near = swap(sent, 1)
    kept = partial[:, 0] + near[:, 0].astype(F32)
    across = swap((partial[:, 2] + near[:, 1].astype(F32)).astype(BF), 2)
    return kept + across.astype(F32)


def normalize(values):
    center = values - jnp.mean(values, axis=-1, keepdims=True)
    scale = lax.rsqrt(jnp.mean(center * center, axis=-1, keepdims=True) + EPS_NORM)
    return center * scale, scale


def norm_back(grad, unit, scale, gain):
    inner = grad * gain
    first = jnp.mean(inner, axis=-1, keepdims=True)
    second = jnp.mean(inner * unit, axis=-1, keepdims=True)
    return scale * (inner - first - unit * second)


def heads(values):
    return values.reshape(values.shape[0], -1, 4, HEAD_DIM)


def dot(spec, left, right):
    return jnp.einsum(spec, left, right, preferred_element_type=F32)


def local(
    tokens,
    dealt,
    cotangent,
    qkv_weight,
    out_weight,
    up_weight,
    down_weight,
    norm1_gain,
    norm1_bias,
    query_bias,
    value_bias,
    out_bias,
    norm2_gain,
    norm2_bias,
    up_bias,
    down_bias,
):
    position = lax.axis_index("fsdp")
    tensor = lax.axis_index("tensor")
    where = (position // (ZN * XN), (position // XN) % ZN, position % XN)
    score_scale = HEAD_DIM ** (-0.5)
    rows = tokens.shape[2]
    width = tokens.shape[3]

    def own_part(vector, size):
        return lax.dynamic_slice_in_dim(vector[0], tensor * size, size, 0)

    qkv_own = qkv_weight[0].reshape(rows // 2, 3 * 256)
    half_a = jnp.concatenate([qkv_own[:, :512], up_weight[0]], axis=1)
    half_b = jnp.concatenate([qkv_own[:, 512:], out_weight[0], down_weight[0]], axis=1)
    full_a, full_b = gather_rows(half_a, half_b, where)
    query_w, keys_w, up_w = full_a[:, :256], full_a[:, 256:512], full_a[:, 512:]
    values_w, out_w, down_w = full_b[:, :256], full_b[:, 256:512], full_b[:, 512:]
    qkv_w = jnp.concatenate([full_a[:, :512], values_w], axis=1)

    out_across = swap(out_w, 2)
    out_beside = swap(jnp.stack([out_w, out_across]), 1)
    out_all = jnp.concatenate([out_w, out_beside[0], out_across, out_beside[1]], axis=1)

    live = dealt.astype(F32).reshape(2, 1, 1)
    own_tokens = tokens[:, 0]
    grad_own = cotangent[:, 0].astype(F32) * live
    hidden = spread_rows(own_tokens).astype(F32).reshape(2, 4 * rows, width)
    down_all = spread_rows(grad_own.astype(BF)).reshape(2, 4 * rows, width)
    unit_one, scale_one = normalize(hidden)
    normed = (unit_one * norm1_gain[0] + norm1_bias[0]).astype(BF)
    joined = dot("msd,df->msf", normed, qkv_w)
    query = heads((joined[..., :256] + own_part(query_bias, 256)).astype(BF))
    keys = heads(joined[..., 256:512].astype(BF))
    values = heads((joined[..., 512:] + own_part(value_bias, 256)).astype(BF))
    scores = dot("mshe,mthe->mhst", query, keys) * score_scale
    probs = jax.nn.softmax(scores, axis=-1)
    probs_low = probs.astype(BF)
    mixed = dot("mhst,mthe->mshe", probs_low, values).astype(BF).reshape(2, 4 * rows, 256)
    blocks = mixed.reshape(2, 4, rows, 256)
    mixed_across = swap(jnp.concatenate([blocks[:, 2:], blocks[:, :2]], axis=1), 2)
    pair = jnp.stack([blocks, mixed_across])
    pair = jnp.stack([pair[:, :, 1], pair[:, :, 0], pair[:, :, 3], pair[:, :, 2]], axis=2)
    mixed_beside = swap(pair, 1)
    mixed_all = jnp.concatenate(
        [blocks, mixed_beside[0], mixed_across, mixed_beside[1]], axis=-1
    ).reshape(2, 4 * rows, width)
    middle = hidden + (dot("msd,ed->mse", mixed_all, out_all) + out_bias[0])
    unit_two, scale_two = normalize(middle)
    normed_two = (unit_two * norm2_gain[0] + norm2_bias[0]).astype(BF)
    upward = dot("msd,df->msf", normed_two, up_w) + own_part(up_bias, 1024)
    share = 0.5 * (1.0 + lax.erf(upward * (0.5**0.5)))
    activated = (upward * share).astype(BF)
    slope = share + upward * (jnp.exp(-0.5 * upward * upward) * (0.5 / jnp.pi) ** 0.5)

    grad_up = (dot("mse,ef->msf", down_all, down_w) * slope).astype(BF)
    norm_two_part = dot("msf,df->msd", grad_up, up_w).reshape(2, 4, rows, width)
    grad_norm_two = collect_rows(norm_two_part)
    down_grad = dot("mse,msf->ef", down_all, activated).astype(BF)
    up_grad = dot("msd,msf->df", normed_two, grad_up).astype(BF)
    up_shard, down_shard = jnp.split(scatter_rows(up_grad, down_grad, where), 2, axis=1)
    up_b_grad = jnp.sum(grad_up.astype(F32), axis=(0, 1))
    down_b_grad = jnp.sum(grad_own, axis=(0, 1))

    down_part = dot("msf,ef->mse", activated, down_w).reshape(2, 4, rows, width)
    block_out = (
        (middle[:, :rows] + (collect_rows(down_part) + down_bias[0])) * live
    ).astype(BF)[:, None]

    own_unit_two = unit_two[:, :rows]
    gain_two_grad = jnp.sum(grad_norm_two * own_unit_two, axis=(0, 1))
    shift_two_grad = jnp.sum(grad_norm_two, axis=(0, 1))
    grad_middle = grad_own + norm_back(
        grad_norm_two, own_unit_two, scale_two[:, :rows], norm2_gain[0]
    )
    grad_att = grad_middle.astype(BF)
    out_b_grad = jnp.sum(grad_att.astype(F32), axis=(0, 1))
    att_all = spread_rows(grad_att).reshape(2, 4 * rows, width)

    out_grad = dot("mse,msd->ed", att_all, mixed).astype(BF)
    grad_mixed = heads(dot("mse,ed->msd", att_all, out_w).astype(BF))
    grad_values = dot("mhst,mshe->mthe", probs_low, grad_mixed).astype(BF)
    grad_prob = dot("mshe,mthe->mhst", grad_mixed, values)
    grad_score = (
        probs * (grad_prob - jnp.sum(grad_prob * probs, axis=-1, keepdims=True))
    ).astype(BF)
    grad_query = (dot("mhst,mthe->mshe", grad_score, keys) * score_scale).astype(BF)
    grad_keys = (dot("mhst,mshe->mthe", grad_score, query) * score_scale).astype(BF)
    grad_joined = jnp.concatenate(
        [item.reshape(2, 4 * rows, 256) for item in (grad_query, grad_keys, grad_values)], axis=-1
    )
    query_b_grad = jnp.sum(grad_joined[..., :256].astype(F32), axis=(0, 1))
    value_b_grad = jnp.sum(grad_joined[..., 512:].astype(F32), axis=(0, 1))
    qkv_grad = dot("msd,msf->df", normed, grad_joined).astype(BF)
    att_a = qkv_grad[:, :512]
    att_b = jnp.concatenate([qkv_grad[:, 512:], out_grad], axis=1)
    att_shard = scatter_rows(att_a, att_b, where)

    norm_one_part = dot("msf,df->msd", grad_joined, qkv_w).reshape(2, 4, rows, width)
    grad_norm_one = collect_rows(norm_one_part)
    own_unit_one = unit_one[:, :rows]
    gain_one_grad = jnp.sum(grad_norm_one * own_unit_one, axis=(0, 1))
    shift_one_grad = jnp.sum(grad_norm_one, axis=(0, 1))
    input_grad = grad_middle + norm_back(
        grad_norm_one, own_unit_one, scale_one[:, :rows], norm1_gain[0]
    )
    input_grad = input_grad.astype(BF)[:, None]

    def whole(part, size):
        return lax.dynamic_update_slice_in_dim(jnp.zeros((size,), F32), part, tensor * part.size, 0)

    packed = jnp.concatenate(
        [
            gain_one_grad,
            shift_one_grad,
            whole(query_b_grad, width),
            whole(value_b_grad, width),
            out_b_grad,
            gain_two_grad,
            shift_two_grad,
            down_b_grad,
            whole(up_b_grad, 4 * width),
        ]
    ).reshape(-1, 128)
    packed = packed + swap(packed, 1) + swap(packed, 2) + swap(packed, 3)
    packed = packed + hop(packed, "x", 1) + hop(packed, "x", 2) + hop(packed, "x", 3)
    packed = packed + hop(packed, "z", 1) + hop(packed, "z", 2) + hop(packed, "z", 3)
    packed = packed + hop(packed, "y", 1)
    packed = packed.reshape(1, -1)
    vectors = [packed[:, k * width : (k + 1) * width] for k in range(8)]
    return (
        block_out,
        input_grad,
        att_shard[:, :768].reshape(1, -1, 3, 256),
        att_shard[:, 768:][None],
        up_shard[None],
        down_shard[None],
        vectors[0],
        vectors[1],
        vectors[2],
        vectors[3],
        vectors[4],
        vectors[5],
        vectors[6],
        packed[:, 8 * width :],
        vectors[7],
    )


def solution(mesh):
    rows = P(None, "fsdp", "tensor", None)
    matrix = P(None, "fsdp", "tensor")
    qkv = P(None, "fsdp", None, "tensor")
    return jax.shard_map(
        local,
        mesh=mesh,
        in_specs=(rows, P(None, "fsdp"), rows, qkv, matrix, matrix, matrix) + (P(),) * 9,
        out_specs=(rows, rows, qkv, matrix, matrix, matrix) + (P(),) * 9,
        check_vma=False,
    )
```

```python
import jax
import jax.numpy as jnp
from jax import lax
from jax.sharding import PartitionSpec as P

HEAD_DIM = 64
EPS_NORM = 1e-06
BF = jnp.bfloat16
F32 = jnp.float32

YH, ZN, XN = 2, 4, 4


def fsdp_perm(dx, dz, dy):
    pairs = []
    for source in range(YH * ZN * XN):
        yh, z, x = source // (ZN * XN), (source // XN) % ZN, source % XN
        target = (((yh + dy) % YH) * ZN + (z + dz) % ZN) * XN + (x + dx) % XN
        pairs.append((source, target))
    return pairs


def hop(array, axis, step):
    move = {"x": (step, 0, 0), "z": (0, step, 0), "y": (0, 0, step)}[axis]
    return lax.ppermute(array, "fsdp", fsdp_perm(*move))


def swap(array, mask):
    return lax.ppermute(array, "tensor", [(i, i ^ mask) for i in range(4)])


def place(pieces, me, axis):
    shape = pieces[0].shape
    out = jnp.zeros(shape[:axis] + (len(pieces),) + shape[axis:], pieces[0].dtype)
    for step, piece in enumerate(pieces):
        out = lax.dynamic_update_index_in_dim(out, piece, (me + step) % len(pieces), axis)
    return out


def take(array, index, axis):
    return lax.dynamic_index_in_dim(array, index % array.shape[axis], axis, keepdims=False)


def ring_gather(block, axis, cut):
    left = hop(block, axis, 1)
    right = hop(block, axis, -1)
    half = block.shape[cut] // 2
    first = hop(lax.slice_in_dim(left, 0, half, axis=cut), axis, 1)
    second = hop(lax.slice_in_dim(right, half, 2 * half, axis=cut), axis, -1)
    return [block, right, jnp.concatenate([first, second], axis=cut), left]


def near_gather(block, axis):
    left = hop(block, axis, 1)
    right = hop(block, axis, -1)
    far = hop(block, axis, 2)
    return [block, right, far, left]


def after(value, *others):
    return lax.optimization_barrier((value,) + others)[0]


def gather_rows(half_a, half_b, first, where):
    yh, z, x = where
    width = half_a.shape[1]
    own = jnp.concatenate([half_a, half_b], axis=1)
    other = hop(own, "y", 1)
    both = jnp.stack([jnp.where(yh == 0, own, other), jnp.where(yh == 0, other, own)])
    part_a, part_b = both[..., :width], both[..., width:]
    part_a = place(near_gather(part_a, "x"), x, 1)
    part_b = place(near_gather(part_b, "z"), z, 1)
    early_a = near_gather(part_a[..., :first], "z")
    early_b = near_gather(part_b[..., :first], "x")
    late_a = after(part_a[..., first:], early_a[1])
    late_b = after(part_b[..., first:], early_b[1])
    late_a = place(ring_gather(late_a, "z", 1), z, 1)
    late_b = place(ring_gather(late_b, "x", 1), x, 2)
    early_a, early_b = place(early_a, z, 1), place(early_b, x, 2)
    return [part.reshape(YH * ZN * XN * 32, -1) for part in (early_a, early_b, late_a, late_b)]


def ring_scatter(array, axis, me, dim, cut):
    far = take(array, me + 2, dim)
    half = far.shape[cut] // 2
    go_right = hop(lax.slice_in_dim(far, 0, half, axis=cut), axis, 1)
    go_left = hop(lax.slice_in_dim(far, half, 2 * half, axis=cut), axis, -1)
    nxt = take(array, me + 1, dim)
    prv = take(array, me + 3, dim)
    nxt_low, nxt_high = jnp.split(nxt, 2, axis=cut)
    prv_low, prv_high = jnp.split(prv, 2, axis=cut)
    to_right = jnp.concatenate([add(nxt_low, go_right), nxt_high], axis=cut)
    to_left = jnp.concatenate([prv_low, add(prv_high, go_left)], axis=cut)
    from_left = hop(to_right, axis, 1)
    from_right = hop(to_left, axis, -1)
    return add(take(array, me, dim), from_left, from_right)


def near_scatter(array, axis, me, dim):
    from_left = hop(take(array, me + 1, dim), axis, 1)
    from_right = hop(take(array, me + 3, dim), axis, -1)
    from_far = hop(take(array, me + 2, dim), axis, 2)
    return add(take(array, me, dim), from_left, from_right, from_far)


def add(*terms):
    total = terms[0].astype(F32)
    for term in terms[1:]:
        total = total + term.astype(F32)
    return total.astype(BF)


def scatter_rows(full_a, full_b, where):
    yh, z, x = where
    shape = (YH, ZN, XN, -1)
    part_a = ring_scatter(full_a.reshape(shape + (full_a.shape[1],)), "z", z, 1, 1)
    part_b = ring_scatter(full_b.reshape(shape + (full_b.shape[1],)), "x", x, 2, 1)
    part_a = near_scatter(part_a, "x", x, 1)
    part_b = near_scatter(part_b, "z", z, 1)
    both = jnp.concatenate([part_a, part_b], axis=-1)
    arrived = hop(take(both, yh + 1, 0), "y", 1)
    return take(both, yh, 0).astype(F32) + arrived.astype(F32)


def spread_rows(own):
    across = swap(own, 2)
    beside = swap(jnp.stack([own, across], axis=1), 1)
    return jnp.stack([own, beside[:, 0], across, beside[:, 1]], axis=1)


def collect_near(partial):
    near = swap(jnp.stack([partial[:, 1], partial[:, 3]], axis=1).astype(BF), 1)
    return partial[:, 0] + near[:, 0].astype(F32), (partial[:, 2] + near[:, 1].astype(F32)).astype(BF)


def collect_far(kept, sent):
    return kept + swap(sent, 2).astype(F32)


def normalize(values):
    center = values - jnp.mean(values, axis=-1, keepdims=True)
    scale = lax.rsqrt(jnp.mean(center * center, axis=-1, keepdims=True) + EPS_NORM)
    return center * scale, scale


def norm_back(grad, unit, scale, gain):
    inner = grad * gain
    first = jnp.mean(inner, axis=-1, keepdims=True)
    second = jnp.mean(inner * unit, axis=-1, keepdims=True)
    return scale * (inner - first - unit * second)


def heads(values):
    return values.reshape(values.shape[0], -1, 4, HEAD_DIM)


def dot(spec, left, right):
    return jnp.einsum(spec, left, right, preferred_element_type=F32)


def local(
    tokens,
    dealt,
    cotangent,
    qkv_weight,
    out_weight,
    up_weight,
    down_weight,
    norm1_gain,
    norm1_bias,
    query_bias,
    value_bias,
    out_bias,
    norm2_gain,
    norm2_bias,
    up_bias,
    down_bias,
):
    position = lax.axis_index("fsdp")
    tensor = lax.axis_index("tensor")
    where = (position // (ZN * XN), (position // XN) % ZN, position % XN)
    score_scale = HEAD_DIM ** (-0.5)
    rows = tokens.shape[2]
    width = tokens.shape[3]

    def own_part(vector, size):
        return lax.dynamic_slice_in_dim(vector[0], tensor * size, size, 0)

    qkv_own = qkv_weight[0].reshape(rows // 2, 3 * 256)
    half_a = jnp.concatenate([qkv_own[:, :512], up_weight[0]], axis=1)
    half_b = jnp.concatenate([qkv_own[:, 512:], out_weight[0], down_weight[0]], axis=1)
    qk_w, vo_w, up_w, down_w = gather_rows(half_a, half_b, 512, where)
    values_w, out_w = vo_w[:, :256], vo_w[:, 256:]

    out_across = swap(out_w, 2)
    out_beside = swap(jnp.stack([out_w, out_across]), 1)
    out_all = jnp.concatenate([out_w, out_beside[0], out_across, out_beside[1]], axis=1)

    live = dealt.astype(F32).reshape(2, 1, 1)
    own_tokens = tokens[:, 0]
    grad_own = cotangent[:, 0].astype(F32) * live
    hidden = spread_rows(own_tokens).astype(F32).reshape(2, 4 * rows, width)
    down_all = spread_rows(grad_own.astype(BF)).reshape(2, 4 * rows, width)
    unit_one, scale_one = normalize(hidden)
    normed = (unit_one * norm1_gain[0] + norm1_bias[0]).astype(BF)
    joined = dot("msd,df->msf", normed, qk_w)
    query = heads((joined[..., :256] + own_part(query_bias, 256)).astype(BF))
    keys = heads(joined[..., 256:].astype(BF))
    values = heads((dot("msd,df->msf", normed, values_w) + own_part(value_bias, 256)).astype(BF))
    scores = dot("mshe,mthe->mhst", query, keys) * score_scale
    probs = jax.nn.softmax(scores, axis=-1)
    probs_low = probs.astype(BF)
    mixed = dot("mhst,mthe->mshe", probs_low, values).astype(BF).reshape(2, 4 * rows, 256)
    blocks = mixed.reshape(2, 4, rows, 256)
    mixed_across = swap(jnp.concatenate([blocks[:, 2:], blocks[:, :2]], axis=1), 2)
    pair = jnp.stack([blocks, mixed_across])
    pair = jnp.stack([pair[:, :, 1], pair[:, :, 0], pair[:, :, 3], pair[:, :, 2]], axis=2)
    mixed_beside = swap(pair, 1)
    mixed_all = jnp.concatenate(
        [blocks, mixed_beside[0], mixed_across, mixed_beside[1]], axis=-1
    ).reshape(2, 4 * rows, width)
    middle = hidden + (dot("msd,ed->mse", mixed_all, out_all) + out_bias[0])
    unit_two, scale_two = normalize(middle)
    normed_two = (unit_two * norm2_gain[0] + norm2_bias[0]).astype(BF)
    upward = dot("msd,df->msf", normed_two, up_w) + own_part(up_bias, 1024)
    share = 0.5 * (1.0 + lax.erf(upward * (0.5**0.5)))
    activated = (upward * share).astype(BF)
    slope = share + upward * (jnp.exp(-0.5 * upward * upward) * (0.5 / jnp.pi) ** 0.5)

    grad_up = (dot("mse,ef->msf", down_all, down_w) * slope).astype(BF)
    norm_two_part = dot("msf,df->msd", grad_up, up_w).reshape(2, 4, rows, width)
    kept_two, sent_two = collect_near(norm_two_part)
    grad_norm_two = collect_far(kept_two, sent_two)
    down_grad = dot("mse,msf->ef", down_all, activated).astype(BF)
    up_grad = dot("msd,msf->df", normed_two, grad_up).astype(BF)
    up_grad, down_grad = after(up_grad, sent_two), after(down_grad, sent_two)
    up_shard, down_shard = jnp.split(scatter_rows(up_grad, down_grad, where), 2, axis=1)
    up_b_grad = jnp.sum(grad_up.astype(F32), axis=(0, 1))
    down_b_grad = jnp.sum(grad_own, axis=(0, 1))

    down_part = dot("msf,ef->mse", activated, down_w).reshape(2, 4, rows, width)
    down_part = after(down_part, grad_norm_two)
    block_out = (
        (middle[:, :rows] + (collect_far(*collect_near(down_part)) + down_bias[0])) * live
    ).astype(BF)[:, None]

    own_unit_two = unit_two[:, :rows]
    gain_two_grad = jnp.sum(grad_norm_two * own_unit_two, axis=(0, 1))
    shift_two_grad = jnp.sum(grad_norm_two, axis=(0, 1))
    grad_middle = grad_own + norm_back(
        grad_norm_two, own_unit_two, scale_two[:, :rows], norm2_gain[0]
    )
    grad_att = grad_middle.astype(BF)
    out_b_grad = jnp.sum(grad_att.astype(F32), axis=(0, 1))
    att_all = spread_rows(grad_att).reshape(2, 4 * rows, width)

    out_grad = dot("mse,msd->ed", att_all, mixed).astype(BF)
    grad_mixed = heads(dot("mse,ed->msd", att_all, out_w).astype(BF))
    grad_values = dot("mhst,mshe->mthe", probs_low, grad_mixed).astype(BF)
    grad_prob = dot("mshe,mthe->mhst", grad_mixed, values)
    grad_score = (
        probs * (grad_prob - jnp.sum(grad_prob * probs, axis=-1, keepdims=True))
    ).astype(BF)
    grad_query = (dot("mhst,mthe->mshe", grad_score, keys) * score_scale).astype(BF)
    grad_keys = (dot("mhst,mshe->mthe", grad_score, query) * score_scale).astype(BF)
    grad_joined = jnp.concatenate(
        [item.reshape(2, 4 * rows, 256) for item in (grad_query, grad_keys, grad_values)], axis=-1
    )
    query_b_grad = jnp.sum(grad_joined[..., :256].astype(F32), axis=(0, 1))
    value_b_grad = jnp.sum(grad_joined[..., 512:].astype(F32), axis=(0, 1))
    qkv_grad = dot("msd,msf->df", normed, grad_joined).astype(BF)
    att_a = qkv_grad[:, :512]
    att_b = jnp.concatenate([qkv_grad[:, 512:], out_grad], axis=1)
    att_shard = scatter_rows(att_a, att_b, where)

    norm_one_part = dot("msf,df->msd", grad_joined[..., :512], qk_w) + dot(
        "msf,df->msd", grad_joined[..., 512:], values_w
    )
    gain_one_grad = jnp.sum(norm_one_part * unit_one, axis=(0, 1))
    shift_one_grad = jnp.sum(norm_one_part, axis=(0, 1))
    grad_norm_one = collect_far(*collect_near(norm_one_part.reshape(2, 4, rows, width)))
    input_grad = grad_middle + norm_back(
        grad_norm_one, unit_one[:, :rows], scale_one[:, :rows], norm1_gain[0]
    )
    input_grad = input_grad.astype(BF)[:, None]

    def whole(part, size):
        return lax.dynamic_update_slice_in_dim(jnp.zeros((size,), F32), part, tensor * part.size, 0)

    packed = jnp.concatenate(
        [
            gain_one_grad,
            shift_one_grad,
            whole(query_b_grad, width),
            whole(value_b_grad, width),
            out_b_grad,
            gain_two_grad,
            shift_two_grad,
            down_b_grad,
            whole(up_b_grad, 4 * width),
        ]
    ).reshape(-1, 128)
    packed = packed + swap(packed, 1) + swap(packed, 2) + swap(packed, 3)
    packed = packed + hop(packed, "x", 1) + hop(packed, "x", 2) + hop(packed, "x", 3)
    packed = packed + hop(packed, "z", 1) + hop(packed, "z", 2) + hop(packed, "z", 3)
    packed = packed + hop(packed, "y", 1)
    packed = packed.reshape(1, -1)
    vectors = [packed[:, k * width : (k + 1) * width] for k in range(8)]
    return (
        block_out,
        input_grad,
        att_shard[:, :768].reshape(1, -1, 3, 256),
        att_shard[:, 768:][None],
        up_shard[None],
        down_shard[None],
        vectors[0],
        vectors[1],
        vectors[2],
        vectors[3],
        vectors[4],
        vectors[5],
        vectors[6],
        packed[:, 8 * width :],
        vectors[7],
    )


def solution(mesh):
    rows = P(None, "fsdp", "tensor", None)
    matrix = P(None, "fsdp", "tensor")
    qkv = P(None, "fsdp", None, "tensor")
    return jax.shard_map(
        local,
        mesh=mesh,
        in_specs=(rows, P(None, "fsdp"), rows, qkv, matrix, matrix, matrix) + (P(),) * 9,
        out_specs=(rows, rows, qkv, matrix, matrix, matrix) + (P(),) * 9,
        check_vma=False,
    )
```

```python
import jax
import jax.numpy as jnp
from jax import lax
from jax.experimental import pallas as pl
from jax.experimental.pallas import tpu as pltpu
from jax.sharding import PartitionSpec as P

HEAD_DIM = 64
EPS_NORM = 1e-06
BF = jnp.bfloat16
F32 = jnp.float32

YH, ZN, XN = 2, 4, 4


def fsdp_perm(dx, dz, dy):
    pairs = []
    for source in range(YH * ZN * XN):
        yh, z, x = source // (ZN * XN), (source // XN) % ZN, source % XN
        target = (((yh + dy) % YH) * ZN + (z + dz) % ZN) * XN + (x + dx) % XN
        pairs.append((source, target))
    return pairs


def hop(array, axis, step):
    move = {"x": (step, 0, 0), "z": (0, step, 0), "y": (0, 0, step)}[axis]
    return lax.ppermute(array, "fsdp", fsdp_perm(*move))


def swap(array, mask):
    return lax.ppermute(array, "tensor", [(i, i ^ mask) for i in range(4)])


def here():
    index = lax.axis_index("fsdp")
    plane = ZN * XN
    return lax.div(index, plane), lax.rem(lax.div(index, XN), ZN), lax.rem(index, XN)


def turn(index, step):
    return lax.rem(index + step, 4)


def shaped(*shape, kind=BF):
    return jax.ShapeDtypeStruct(shape, kind)


def limit(mebibytes):
    return pltpu.CompilerParams(vmem_limit_bytes=mebibytes << 20)


def move(plan, arrays, shapes, count):
    def body(*refs):
        inputs, outputs, done = refs[: len(arrays)], refs[len(arrays) : -1], refs[-1]
        pairs = plan(inputs, outputs)
        copies = [
            pltpu.make_async_copy(source, target, done.at[spot])
            for spot, (source, target) in enumerate(pairs)
        ]
        for copy in copies:
            copy.start()
        for copy in copies:
            copy.wait()

    size = sum(item.size * 2 for item in shapes)
    return pl.pallas_call(
        body,
        out_shape=shapes,
        in_specs=[pl.BlockSpec(memory_space=pl.ANY)] * len(arrays),
        out_specs=[pl.BlockSpec(memory_space=pl.ANY)] * len(shapes),
        scratch_shapes=[pltpu.SemaphoreType.DMA((count,))],
        cost_estimate=pl.CostEstimate(flops=0, bytes_accessed=2 * size, transcendentals=0),
    )(*arrays)


def whole_call(body, arrays, shapes, mebibytes, flops=0, scratch=()):
    size = sum(item.size * item.dtype.itemsize for item in list(shapes) + list(arrays))
    return pl.pallas_call(
        body,
        out_shape=shapes,
        scratch_shapes=scratch,
        compiler_params=limit(mebibytes),
        cost_estimate=pl.CostEstimate(flops=flops, bytes_accessed=size, transcendentals=0),
    )(*arrays)


def after(value, *others):
    return lax.optimization_barrier((value,) + others)[0]


def near_gather(block, axis):
    left = hop(block, axis, 1)
    right = hop(block, axis, -1)
    far = hop(block, axis, 2)
    return [block, right, far, left]


def ring_gather(block, axis):
    left = hop(block, axis, 1)
    right = hop(block, axis, -1)
    first = hop(left[0], axis, 1)
    second = hop(right[1], axis, -1)
    return [block, right, left, first, second]


def pack_body(qkv, out, up, down, own):
    own[:, 0:256] = qkv[0]
    own[:, 256:512] = qkv[1]
    own[:, 512:1536] = up[...]
    own[:, 1536:1792] = qkv[2]
    own[:, 1792:2048] = out[...]
    own[:, 2048:3072] = down[...]


def pair_body(own, other, part_a, part_b):
    yh, _, _ = here()
    part_a[yh] = own[:, :1536]
    part_b[yh] = own[:, 1536:]
    part_a[1 - yh] = other[:, :1536]
    part_b[1 - yh] = other[:, 1536:]


def first_plan(inputs, outputs):
    _, z, x = here()
    att_a, att_b, mlp_a, mlp_b = outputs
    pairs = []
    for step in range(4):
        piece_a, piece_b = inputs[step], inputs[4 + step]
        pairs.append((piece_a.at[:, :, 0:512], att_a.at[:, turn(x, step)]))
        pairs.append((piece_b.at[:, :, 0:512], att_b.at[:, turn(z, step)]))
        pairs.append((piece_a.at[:, :, 512:1536], mlp_a.at[:, turn(x, step)]))
        pairs.append((piece_b.at[:, :, 512:1536], mlp_b.at[:, turn(z, step)]))
    return pairs


def att_plan(inputs, outputs):
    _, z, x = here()
    qk_w, values_w, out_w = outputs
    pairs = []
    for step in range(4):
        piece_a, piece_b = inputs[step], inputs[4 + step]
        pairs.append((piece_a, qk_w.at[:, turn(z, step)]))
        pairs.append((piece_b.at[:, :, :, 0:256], values_w.at[:, :, turn(x, step)]))
        pairs.append((piece_b.at[:, :, :, 256:512], out_w.at[:, :, turn(x, step)]))
    return pairs


def mlp_plan(inputs, outputs):
    _, z, x = here()
    up_w, down_w = outputs
    pairs = []
    for spot, step in enumerate((0, 1, 3)):
        pairs.append((inputs[spot], up_w.at[:, turn(z, step)]))
        pairs.append((inputs[5 + spot], down_w.at[:, :, turn(x, step)]))
    for half in range(2):
        pairs.append((inputs[3 + half], up_w.at[half, turn(z, 2)]))
        pairs.append((inputs[8 + half], down_w.at[half, :, turn(x, 2)]))
    return pairs


def far_plan(inputs, outputs):
    _, z, x = here()
    grad_a, grad_b = inputs
    pairs = []
    for half in range(2):
        pairs.append((grad_a.at[half, turn(z, 2)], outputs[half]))
        pairs.append((grad_b.at[half, :, turn(x, 2)], outputs[2 + half]))
    return pairs


def fetch(pairs, done):
    copies = [
        pltpu.make_async_copy(source, target, done.at[spot])
        for spot, (source, target) in enumerate(pairs)
    ]
    for copy in copies:
        copy.start()
    for copy in copies:
        copy.wait()


def pass_body(grad_a, grad_b, low_a, high_a, low_b, high_b, ra, la, rb, lb, held, done):
    _, z, x = here()
    fetch(
        [
            (grad_a.at[:, turn(z, 1)], held.at[0]),
            (grad_a.at[:, turn(z, 3)], held.at[1]),
            (grad_b.at[:, :, turn(x, 1)], held.at[2]),
            (grad_b.at[:, :, turn(x, 3)], held.at[3]),
        ],
        done,
    )
    for spot, (right, left, low, high) in enumerate(
        ((ra, la, low_a, high_a), (rb, lb, low_b, high_b))
    ):
        right[0] = add(held[2 * spot, 0], low[...])
        right[1] = held[2 * spot, 1]
        left[0] = held[2 * spot + 1, 0]
        left[1] = add(held[2 * spot + 1, 1], high[...])


def rest_body(grad_a, grad_b, la, ra, lb, rb, total_a, total_b, held, done):
    _, z, x = here()
    fetch(
        [(grad_a.at[:, turn(z, 0)], held.at[0]), (grad_b.at[:, :, turn(x, 0)], held.at[1])],
        done,
    )
    total_a[...] = add(held[0], la[...], ra[...])
    total_b[...] = add(held[1], lb[...], rb[...])


VMEM = pl.BlockSpec(memory_space=pltpu.VMEM)
ANY = pl.BlockSpec(memory_space=pl.ANY)


def held_call(body, whole, arrays, shapes, slots, block, mebibytes):
    size = sum(item.size * 2 for item in shapes) + sum(item.size * 2 for item in arrays)
    return pl.pallas_call(
        body,
        out_shape=shapes,
        in_specs=[ANY] * len(whole) + [VMEM] * len(arrays),
        out_specs=[VMEM] * len(shapes),
        scratch_shapes=[pltpu.VMEM((slots,) + block, BF), pltpu.SemaphoreType.DMA((slots,))],
        compiler_params=limit(mebibytes),
        cost_estimate=pl.CostEstimate(flops=0, bytes_accessed=2 * size, transcendentals=0),
    )(*whole, *arrays)


def mlp_scatter(grad_a, grad_b):
    block = (2, 4, 32, 1024)
    half = shaped(4, 32, 1024)
    low_a, high_a, low_b, high_b = move(far_plan, (grad_a, grad_b), [half] * 4, 4)
    recv = (hop(low_a, "z", 1), hop(high_a, "z", -1), hop(low_b, "x", 1), hop(high_b, "x", -1))
    ra, la, rb, lb = held_call(
        pass_body, (grad_a, grad_b), recv, [shaped(*block)] * 4, 4, block, 40
    )
    recv = (hop(ra, "z", 1), hop(la, "z", -1), hop(rb, "x", 1), hop(lb, "x", -1))
    return held_call(rest_body, (grad_a, grad_b), recv, [shaped(*block)] * 2, 2, block, 40)


def add(*terms):
    total = terms[0].astype(F32)
    for term in terms[1:]:
        total = total + term.astype(F32)
    return total.astype(BF)


def contract(left, right, dims):
    return lax.dot_general(left, right, (dims, ((), ())), preferred_element_type=F32)


ROWS = ((1,), (0,))
BOTH = ((1,), (1,))
TOPS = ((0,), (0,))
SCALE = HEAD_DIM ** (-0.5)


def probabilities(query, keys):
    scores = contract(query, keys, BOTH) * SCALE
    weight = jnp.exp(scores - jnp.max(scores, axis=-1, keepdims=True))
    return weight / jnp.sum(weight, axis=-1, keepdims=True)


def att_body(normed, qk_w, values_w, query_b, value_b, joined, mixed):
    spot = pl.ds(pl.multiple_of(lax.axis_index("tensor") * 256, 256), 256)
    rows = normed[...]
    pair = contract(rows, qk_w[...].reshape(1024, 512), ROWS)
    joined[:, 0:256] = (pair[:, 0:256] + query_b[:, spot]).astype(BF)
    joined[:, 256:512] = pair[:, 256:].astype(BF)
    last = contract(rows, values_w[...].reshape(1024, 256), ROWS)
    joined[:, 512:768] = (last + value_b[:, spot]).astype(BF)
    for image in range(2):
        line = slice(image * 256, image * 256 + 256)
        parts = []
        for head in range(4):
            query, keys, values = (
                joined[line, base + head * 64 : base + head * 64 + 64] for base in (0, 256, 512)
            )
            probs = probabilities(query, keys).astype(BF)
            parts.append(contract(probs, values, ROWS).astype(BF))
        mixed[line, :] = jnp.concatenate(parts, axis=1)


def mid_body(hidden, m0, m1, m2, m3, w0, w1, w2, w3, out_b, gain, shift, normed, own):
    for image in range(2):
        line = slice(image * 256, image * 256 + 256)
        total = hidden[line, :].astype(F32) + out_b[...]
        for mask, (mixed, weight) in enumerate(((m0, w0), (m1, w1), (m2, w2), (m3, w3))):
            rows = jnp.concatenate(
                [
                    mixed[image * 256 + (spot ^ mask) * 64 : image * 256 + (spot ^ mask) * 64 + 64]
                    for spot in range(4)
                ],
                axis=0,
            )
            total = total + contract(rows, weight[...].reshape(1024, 256), BOTH)
        own[image] = total[:64]
        unit, _ = normalize(total)
        normed[line, :] = (unit * gain[...] + shift[...]).astype(BF)


def spread_rows(own):
    across = swap(own, 2)
    beside = swap(own, 1)
    diagonal = swap(across, 1)
    return jnp.stack([own, beside, across, diagonal], axis=1)


def collect_near(partial):
    near = swap(jnp.stack([partial[:, 1], partial[:, 3]], axis=1).astype(BF), 1)
    return near_total(partial[:, 0], partial[:, 2], near)


def near_total(first, second, near):
    return first + near[:, 0].astype(F32), (second + near[:, 1].astype(F32)).astype(BF)


def collect_far(kept, sent):
    return kept + swap(sent, 2).astype(F32)


def normalize(values):
    center = values - jnp.mean(values, axis=-1, keepdims=True)
    scale = lax.rsqrt(jnp.mean(center * center, axis=-1, keepdims=True) + EPS_NORM)
    return center * scale, scale


def norm_back(grad, unit, scale, gain):
    inner = grad * gain
    first = jnp.mean(inner, axis=-1, keepdims=True)
    second = jnp.mean(inner * unit, axis=-1, keepdims=True)
    return scale * (inner - first - unit * second)


def back_body(
    a0, a1, a2, a3, joined, qk_w, values_w, out_w, hidden, gain_two, shift_two, out_b, down_b, up_b,
    grads, att, sent, kept, vector,
):
    tensor = lax.axis_index("tensor")
    for image in range(2):
        for spot, piece in enumerate((a0, a1, a2, a3)):
            first = image * 256 + spot * 64
            att[first : first + 64, :] = piece[image]
    pair_w = qk_w[...].reshape(1024, 512)
    last_w = values_w[...].reshape(1024, 256)
    mixer = out_w[...].reshape(1024, 256)
    gain = jnp.zeros((1, 1024), F32)
    shift = jnp.zeros((1, 1024), F32)
    for image in range(2):
        line = slice(image * 256, image * 256 + 256)
        grad_mixed = contract(att[line, :], mixer, ROWS).astype(BF)
        parts = ([], [], [])
        for head in range(4):
            query, keys, values = (
                joined[line, base + head * 64 : base + head * 64 + 64] for base in (0, 256, 512)
            )
            grad = grad_mixed[:, head * 64 : head * 64 + 64]
            probs = probabilities(query, keys)
            grad_prob = contract(grad, values, BOTH)
            inner = jnp.sum(grad_prob * probs, axis=-1, keepdims=True)
            score = (probs * (grad_prob - inner)).astype(BF)
            parts[0].append((contract(score, keys, ROWS) * SCALE).astype(BF))
            parts[1].append((contract(score, query, TOPS) * SCALE).astype(BF))
            parts[2].append(contract(probs.astype(BF), grad, TOPS).astype(BF))
        for kind in range(3):
            grads[line, kind * 256 : kind * 256 + 256] = jnp.concatenate(parts[kind], axis=1)
        norm_grad = contract(grads[line, :512], pair_w, BOTH) + contract(
            grads[line, 512:], last_w, BOTH
        )
        unit, _ = normalize(hidden[line, :].astype(F32))
        gain = gain + jnp.sum(norm_grad * unit, axis=0, keepdims=True)
        shift = shift + jnp.sum(norm_grad, axis=0, keepdims=True)
        kept[image, 0] = norm_grad[0:64]
        sent[image, 0] = norm_grad[64:128].astype(BF)
        kept[image, 1] = norm_grad[128:192]
        sent[image, 1] = norm_grad[192:256].astype(BF)
    vector[...] = jnp.zeros(vector.shape, F32)
    rows = (
        (0, gain), (2, shift), (8, out_b[...]), (10, gain_two[...]), (12, shift_two[...]),
        (14, down_b[...]),
    )
    for row, value in rows:
        vector[row : row + 1, :] = value[:, :512]
        vector[row + 1 : row + 2, :] = value[:, 512:]
    spot = pl.ds(pl.multiple_of(lax.rem(tensor, 2) * 256, 256), 256)
    for row, base in ((4, 0), (6, 512)):
        part = jnp.sum(grads[:, base : base + 256].astype(F32), axis=0, keepdims=True)
        vector[pl.ds(row + lax.div(tensor, 2), 1), spot] = part
    vector[pl.ds(16 + 2 * tensor, 1), :] = up_b[:, :512]
    vector[pl.ds(17 + 2 * tensor, 1), :] = up_b[:, 512:]


def grads_body(normed, grads, att, mixed, vector, *rest):
    sends_a, sends_b, own_a, own_b = rest[0:3], rest[3:6], rest[6], rest[7]
    grad_a, grad_b, low, done = rest[8:]
    _, z, x = here()
    grad_a[...] = contract(normed[...], grads[:, 0:512], TOPS).astype(BF).reshape(grad_a.shape)
    pairs = [(grad_a.at[:, turn(z, 0)], own_a)]
    low[...] = vector[...].astype(BF)
    for step in range(1, 4):
        target = sends_a[step - 1]
        for half in range(2):
            pairs.append((grad_a.at[half, turn(z, step)], target.at[pl.ds(4 * half, 4)]))
        pairs.append((low, target.at[8]))
    copies = [
        pltpu.make_async_copy(source, target, done.at[spot])
        for spot, (source, target) in enumerate(pairs)
    ]
    for copy in copies:
        copy.start()
    last = contract(normed[...], grads[:, 512:768], TOPS).astype(BF)
    grad_b[:, :, :, :, 0:256] = last.reshape(2, 4, 4, 32, 256)
    last = contract(att[...], mixed[...], TOPS).astype(BF)
    grad_b[:, :, :, :, 256:512] = last.reshape(2, 4, 4, 32, 256)
    others = [(grad_b.at[:, :, turn(x, 0)], own_b)]
    for step in range(1, 4):
        others.append((grad_b.at[:, :, turn(x, step)], sends_b[step - 1]))
    more = [
        pltpu.make_async_copy(source, target, done.at[len(pairs) + spot])
        for spot, (source, target) in enumerate(others)
    ]
    for copy in more:
        copy.start()
    for copy in copies + more:
        copy.wait()


def second_body(*refs):
    a1, a2, a3, own_a, b1, b2, b3, own_b, vector, mlp_a, mlp_b = refs[:11]
    outs_a, outs_b, sum_a, sum_b = refs[11:15], refs[15:19], refs[19], refs[20]
    _, z, x = here()
    for yh in range(2):
        part = slice(4 * yh, 4 * yh + 4)
        sum_a[yh] = add(own_a[yh], a1[part], a2[part], a3[part])
        sum_b[yh] = add(own_b[yh], b1[yh], b2[yh], b3[yh])
    low = add(vector[...], a1[8], a2[8], a3[8])
    for step in range(4):
        for out, total, mlp, index in (
            (outs_a[step], sum_a, mlp_a, turn(x, step)),
            (outs_b[step], sum_b, mlp_b, turn(z, step)),
        ):
            for yh in range(2):
                out[yh] = total[yh, index]
                out[2 + yh] = mlp[yh, index, :, 0:512]
                out[4 + yh] = mlp[yh, index, :, 512:1024]
        outs_a[step][6] = low


def third_body(a0, a1, a2, a3, b0, b1, b2, b3, send, own):
    yh, _, _ = here()
    for spot in range(3):
        for base, pieces in ((0, (a0, a1, a2, a3)), (3, (b0, b1, b2, b3))):
            mine = [piece[2 * spot + yh].astype(F32) for piece in pieces]
            other = [piece[2 * spot + 1 - yh].astype(F32) for piece in pieces]
            own[base + spot] = (mine[0] + mine[1]) + (mine[2] + mine[3])
            send[base + spot] = ((other[0] + other[1]) + (other[2] + other[3])).astype(BF)
    total = [piece[6].astype(F32) for piece in (a0, a1, a2, a3)]
    total = (total[0] + total[1]) + (total[2] + total[3])
    own[6] = total
    send[6] = total.astype(BF)


def last_body(own, came, qkv, out, up, down, vector):
    def total(spot):
        return own[spot] + came[spot].astype(F32)

    att_a, att_b = total(0), total(3)
    qkv[0] = att_a[:, 0:256]
    qkv[1] = att_a[:, 256:512]
    qkv[2] = att_b[:, 0:256]
    out[...] = att_b[:, 256:512]
    up[:, 0:512] = total(1)
    up[:, 512:1024] = total(2)
    down[:, 0:512] = total(4)
    down[:, 512:1024] = total(5)
    vector[...] = total(6)


def att_scatter(normed, grads, att, mixed, vector, mlp_a, mlp_b):
    block = (2, 4, 32, 512)
    shapes = [shaped(9, 32, 512)] * 3 + [shaped(*block)] * 5
    arrays = (normed, grads, att, mixed, vector)
    size = sum(item.size * 2 for item in shapes) + sum(item.size * 2 for item in arrays)
    results = pl.pallas_call(
        grads_body,
        out_shape=shapes,
        in_specs=[VMEM] * 5,
        out_specs=[ANY] * 8,
        scratch_shapes=[
            pltpu.VMEM((2, 4, 4, 32, 512), BF),
            pltpu.VMEM((2, 4, 4, 32, 512), BF),
            pltpu.VMEM((32, 512), BF),
            pltpu.SemaphoreType.DMA((14,)),
        ],
        compiler_params=limit(40),
        cost_estimate=pl.CostEstimate(
            flops=2 * 512 * 1024 * 1024, bytes_accessed=size, transcendentals=0
        ),
    )(*arrays)
    came_a = [hop(results[step - 1], "z", step) for step in (1, 2, 3)]
    came_b = [hop(results[2 + step], "x", step) for step in (1, 2, 3)]
    pieces = whole_call(
        second_body,
        (*came_a, results[6], *came_b, results[7], vector, mlp_a, mlp_b),
        [shaped(7, 32, 512)] * 4 + [shaped(6, 32, 512)] * 4,
        40,
        scratch=[pltpu.VMEM(block, BF), pltpu.VMEM(block, BF)],
    )
    came_a = [hop(pieces[step], "x", step) for step in (1, 2, 3)]
    came_b = [hop(pieces[4 + step], "z", step) for step in (1, 2, 3)]
    send, own = whole_call(
        third_body,
        (pieces[0], *came_a, pieces[4], *came_b),
        [shaped(7, 32, 512), shaped(7, 32, 512, kind=F32)],
        40,
    )
    shapes = [(3, 32, 256), (32, 256), (32, 1024), (32, 1024), (32, 512)]
    return whole_call(
        last_body, (own, hop(send, "y", 1)), [shaped(*shape, kind=F32) for shape in shapes], 40
    )


def dot(spec, left, right):
    return jnp.einsum(spec, left, right, preferred_element_type=F32)


def local(
    tokens,
    dealt,
    cotangent,
    qkv_weight,
    out_weight,
    up_weight,
    down_weight,
    norm1_gain,
    norm1_bias,
    query_bias,
    value_bias,
    out_bias,
    norm2_gain,
    norm2_bias,
    up_bias,
    down_bias,
):
    tensor = lax.axis_index("tensor")
    rows = tokens.shape[2]
    width = tokens.shape[3]
    count = 8 * rows
    weight_rows = (YH, ZN, XN, 32)

    def own_part(vector, size):
        return lax.dynamic_slice_in_dim(vector[0], tensor * size, size, 0)

    (own,) = whole_call(
        pack_body,
        (jnp.transpose(qkv_weight[0], (1, 0, 2)), out_weight[0], up_weight[0], down_weight[0]),
        [shaped(32, 3072)],
        16,
    )
    part_a, part_b = whole_call(
        pair_body, (own, hop(own, "y", 1)), [shaped(2, 32, 1536)] * 2, 16
    )
    pieces = near_gather(part_a, "x") + near_gather(part_b, "z")
    shapes = [shaped(2, 4, 32, 512)] * 2 + [shaped(2, 4, 32, 1024)] * 2
    att_a, att_b, mlp_a, mlp_b = move(first_plan, pieces, shapes, 16)
    att_a, att_b = near_gather(att_a, "z"), near_gather(att_b, "x")
    mlp_a = ring_gather(after(mlp_a, att_a[1]), "z")
    mlp_b = ring_gather(after(mlp_b, att_b[1]), "x")
    shapes = [shaped(*weight_rows, 512), shaped(*weight_rows, 256), shaped(*weight_rows, 256)]
    qk_w, values_w, out_w = move(att_plan, att_a + att_b, shapes, 12)
    up_w, down_w = move(mlp_plan, mlp_a + mlp_b, [shaped(*weight_rows, 1024)] * 2, 10)
    up_w, down_w = up_w.reshape(width, -1), down_w.reshape(width, -1)
    out_across = swap(out_w, 2)
    out_beside, out_diagonal = swap(out_w, 1), swap(out_across, 1)

    live = dealt.astype(F32).reshape(2, 1, 1)
    own_tokens = tokens[:, 0]
    grad_own = cotangent[:, 0].astype(F32) * live
    hidden = spread_rows(own_tokens).reshape(count, width)
    down_all = spread_rows(grad_own.astype(BF)).reshape(count, width)
    unit_one, _ = normalize(hidden.astype(F32))
    normed = (unit_one * norm1_gain[0] + norm1_bias[0]).astype(BF)
    joined, mixed = whole_call(
        att_body,
        (normed, qk_w, values_w, query_bias, value_bias),
        [shaped(count, 768), shaped(count, 256)],
        48,
        flops=2 * 512 * 1024 * 1024,
    )
    mixed_across = swap(mixed, 2)
    mixed_beside, mixed_diagonal = swap(mixed, 1), swap(mixed_across, 1)
    normed_two, middle_own = whole_call(
        mid_body,
        (
            hidden,
            mixed,
            mixed_beside,
            mixed_across,
            mixed_diagonal,
            out_w,
            out_beside,
            out_across,
            out_diagonal,
            out_bias,
            norm2_gain,
            norm2_bias,
        ),
        [shaped(count, width), shaped(2, rows, width, kind=F32)],
        48,
        flops=2 * 512 * 1024 * 1024,
    )
    upward = dot("sd,df->sf", normed_two, up_w) + own_part(up_bias, 1024)
    share = 0.5 * (1.0 + lax.erf(upward * (0.5**0.5)))
    activated = (upward * share).astype(BF)
    slope = share + upward * (jnp.exp(-0.5 * upward * upward) * (0.5 / jnp.pi) ** 0.5)

    grad_up = (dot("se,ef->sf", down_all, down_w) * slope).astype(BF)
    norm_two_part = dot("sf,df->sd", grad_up, up_w).reshape(2, 4, rows, width)
    kept_two, sent_two = collect_near(norm_two_part)
    grad_norm_two = collect_far(kept_two, sent_two)
    up_grad = dot("sd,sf->df", normed_two, grad_up).astype(BF)
    down_grad = dot("se,sf->ef", down_all, activated).astype(BF)
    up_grad, down_grad = after(up_grad, sent_two), after(down_grad, sent_two)
    mlp_a, mlp_b = mlp_scatter(
        up_grad.reshape(*weight_rows, -1), down_grad.reshape(*weight_rows, -1)
    )
    up_b_grad = jnp.sum(grad_up.astype(F32), axis=0, keepdims=True)
    down_b_grad = jnp.sum(grad_own, axis=(0, 1))[None]

    unit_two, scale_two = normalize(middle_own)
    gain_two_grad = jnp.sum(grad_norm_two * unit_two, axis=(0, 1))[None]
    shift_two_grad = jnp.sum(grad_norm_two, axis=(0, 1))[None]
    grad_middle = grad_own + norm_back(grad_norm_two, unit_two, scale_two, norm2_gain[0])
    grad_att = grad_middle.astype(BF)
    out_b_grad = jnp.sum(grad_att.astype(F32), axis=(0, 1))[None]
    att_across = swap(grad_att, 2)
    att_beside, att_diagonal = swap(grad_att, 1), swap(att_across, 1)

    down_part = dot("sf,ef->se", activated, down_w).reshape(2, 4, rows, width)
    down_part = after(down_part, grad_norm_two)
    block_out = (
        (middle_own + (collect_far(*collect_near(down_part)) + down_bias[0])) * live
    ).astype(BF)[:, None]

    grads, att_all, sent, kept, vector = whole_call(
        back_body,
        (
            grad_att,
            att_beside,
            att_across,
            att_diagonal,
            joined,
            qk_w,
            values_w,
            out_w,
            hidden,
            gain_two_grad,
            shift_two_grad,
            out_b_grad,
            down_b_grad,
            up_b_grad,
        ),
        [
            shaped(count, 768),
            shaped(count, width),
            shaped(2, 2, rows, width),
            shaped(2, 2, rows, width, kind=F32),
            shaped(32, 512, kind=F32),
        ],
        56,
        flops=3 * 512 * 1024 * 1024,
    )
    qkv_grad, out_grad, up_grad, down_grad, vector = att_scatter(
        normed, grads, att_all, mixed, vector, mlp_a, mlp_b
    )
    near = swap(sent, 1)
    grad_norm_one = collect_far(*near_total(kept[:, 0], kept[:, 1], near))
    unit_own, scale_own = normalize(own_tokens.astype(F32))
    input_grad = grad_middle + norm_back(grad_norm_one, unit_own, scale_own, norm1_gain[0])
    input_grad = input_grad.astype(BF)[:, None]

    vector = vector + swap(vector, 1)
    vector = (vector + swap(vector, 2))[:24].reshape(1, -1)
    parts = [vector[:, k * width : (k + 1) * width] for k in range(8)]
    return (
        block_out,
        input_grad,
        jnp.transpose(qkv_grad, (1, 0, 2))[None],
        out_grad[None],
        up_grad[None],
        down_grad[None],
        *parts[:7],
        vector[:, 8 * width :],
        parts[7],
    )


def solution(mesh):
    rows = P(None, "fsdp", "tensor", None)
    matrix = P(None, "fsdp", "tensor")
    qkv = P(None, "fsdp", None, "tensor")
    return jax.shard_map(
        local,
        mesh=mesh,
        in_specs=(rows, P(None, "fsdp"), rows, qkv, matrix, matrix, matrix) + (P(),) * 9,
        out_specs=(rows, rows, qkv, matrix, matrix, matrix) + (P(),) * 9,
        check_vma=False,
    )
```

```python
import jax
import jax.numpy as jnp
from jax import lax
from jax.experimental import pallas as pl
from jax.experimental.pallas import tpu as pltpu
from jax.sharding import PartitionSpec as P

HEAD_DIM = 64
EPS_NORM = 1e-06
BF = jnp.bfloat16
F32 = jnp.float32

YH, ZN, XN = 2, 4, 4


def fsdp_perm(dx, dz, dy):
    pairs = []
    for source in range(YH * ZN * XN):
        yh, z, x = source // (ZN * XN), (source // XN) % ZN, source % XN
        target = (((yh + dy) % YH) * ZN + (z + dz) % ZN) * XN + (x + dx) % XN
        pairs.append((source, target))
    return pairs


def hop(array, axis, step):
    move = {"x": (step, 0, 0), "z": (0, step, 0), "y": (0, 0, step)}[axis]
    return lax.ppermute(array, "fsdp", fsdp_perm(*move))


def swap(array, mask):
    return lax.ppermute(array, "tensor", [(i, i ^ mask) for i in range(4)])


def here():
    index = lax.axis_index("fsdp")
    plane = ZN * XN
    return lax.div(index, plane), lax.rem(lax.div(index, XN), ZN), lax.rem(index, XN)


def turn(index, step):
    return lax.rem(index + step, 4)


def shaped(*shape, kind=BF):
    return jax.ShapeDtypeStruct(shape, kind)


def limit(mebibytes):
    return pltpu.CompilerParams(vmem_limit_bytes=mebibytes << 20)


VMEM = pl.BlockSpec(memory_space=pltpu.VMEM)
ANY = pl.BlockSpec(memory_space=pl.ANY)


def move(plan, arrays, shapes, count):
    def body(*refs):
        inputs, outputs, done = refs[: len(arrays)], refs[len(arrays) : -1], refs[-1]
        pairs = plan(inputs, outputs)
        copies = [
            pltpu.make_async_copy(source, target, done.at[spot])
            for spot, (source, target) in enumerate(pairs)
        ]
        for copy in copies:
            copy.start()
        for copy in copies:
            copy.wait()

    size = sum(item.size * 2 for item in shapes)
    return pl.pallas_call(
        body,
        out_shape=shapes,
        in_specs=[ANY] * len(arrays),
        out_specs=[VMEM] * len(shapes),
        scratch_shapes=[pltpu.SemaphoreType.DMA((count,))],
        compiler_params=limit(16),
        cost_estimate=pl.CostEstimate(flops=0, bytes_accessed=2 * size, transcendentals=0),
    )(*arrays)


def whole_call(body, arrays, shapes, mebibytes, flops=0, scratch=()):
    size = sum(item.size * item.dtype.itemsize for item in list(shapes) + list(arrays))
    return pl.pallas_call(
        body,
        out_shape=shapes,
        scratch_shapes=scratch,
        compiler_params=limit(mebibytes),
        cost_estimate=pl.CostEstimate(flops=flops, bytes_accessed=size, transcendentals=0),
    )(*arrays)


def after(value, *others):
    return lax.optimization_barrier((value,) + others)[0]


def near_gather(block, axis):
    left = hop(block, axis, 1)
    right = hop(block, axis, -1)
    far = hop(block, axis, 2)
    return [block, right, far, left]


def ring_gather(block, axis):
    left = hop(block, axis, 1)
    right = hop(block, axis, -1)
    first = hop(left[0], axis, 1)
    second = hop(right[1], axis, -1)
    return [block, right, left, first, second]


def pack_body(qkv, out, up, down, own):
    own[:, 0:256] = qkv[0]
    own[:, 256:512] = qkv[1]
    own[:, 512:1536] = up[...]
    own[:, 1536:1792] = qkv[2]
    own[:, 1792:2048] = out[...]
    own[:, 2048:3072] = down[...]


def pair_body(own, other, part_a, part_b):
    yh, _, _ = here()
    part_a[yh] = own[:, :1536]
    part_b[yh] = own[:, 1536:]
    part_a[1 - yh] = other[:, :1536]
    part_b[1 - yh] = other[:, 1536:]


def first_plan(inputs, outputs):
    _, z, x = here()
    att_a, att_b, mlp_a, mlp_b = outputs
    pairs = []
    for step in range(4):
        piece_a, piece_b = inputs[step], inputs[4 + step]
        pairs.append((piece_a.at[:, :, 0:512], att_a.at[:, turn(x, step)]))
        pairs.append((piece_b.at[:, :, 0:512], att_b.at[:, turn(z, step)]))
        pairs.append((piece_a.at[:, :, 512:1536], mlp_a.at[:, turn(x, step)]))
        pairs.append((piece_b.at[:, :, 512:1536], mlp_b.at[:, turn(z, step)]))
    return pairs


def att_plan(inputs, outputs):
    _, z, x = here()
    qk_w, values_w, out_w = outputs
    pairs = []
    for step in range(4):
        piece_a, piece_b = inputs[step], inputs[4 + step]
        pairs.append((piece_a, qk_w.at[:, turn(z, step)]))
        pairs.append((piece_b.at[:, :, :, 0:256], values_w.at[:, :, turn(x, step)]))
        pairs.append((piece_b.at[:, :, :, 256:512], out_w.at[:, :, turn(x, step)]))
    return pairs


def mlp_plan(inputs, outputs):
    _, z, x = here()
    up_w, down_w = outputs
    pairs = []
    for spot, step in enumerate((0, 1, 3)):
        pairs.append((inputs[spot], up_w.at[:, turn(z, step)]))
        pairs.append((inputs[5 + spot], down_w.at[:, :, turn(x, step)]))
    for half in range(2):
        pairs.append((inputs[3 + half], up_w.at[half, turn(z, 2)]))
        pairs.append((inputs[8 + half], down_w.at[half, :, turn(x, 2)]))
    return pairs


def far_plan(inputs, outputs):
    _, z, x = here()
    grad_a, grad_b = inputs
    pairs = []
    for half in range(2):
        pairs.append((grad_a.at[half, turn(z, 2)], outputs[half]))
        pairs.append((grad_b.at[half, :, turn(x, 2)], outputs[2 + half]))
    return pairs


def fetch(pairs, done):
    copies = [
        pltpu.make_async_copy(source, target, done.at[spot])
        for spot, (source, target) in enumerate(pairs)
    ]
    for copy in copies:
        copy.start()
    for copy in copies:
        copy.wait()


def pass_body(grad_a, grad_b, low_a, high_a, low_b, high_b, ra, la, rb, lb, held, done):
    _, z, x = here()
    fetch(
        [
            (grad_a.at[:, turn(z, 1)], held.at[0]),
            (grad_a.at[:, turn(z, 3)], held.at[1]),
            (grad_b.at[:, :, turn(x, 1)], held.at[2]),
            (grad_b.at[:, :, turn(x, 3)], held.at[3]),
        ],
        done,
    )
    for spot, (right, left, low, high) in enumerate(
        ((ra, la, low_a, high_a), (rb, lb, low_b, high_b))
    ):
        right[0] = add(held[2 * spot, 0], low[...])
        right[1] = held[2 * spot, 1]
        left[0] = held[2 * spot + 1, 0]
        left[1] = add(held[2 * spot + 1, 1], high[...])


def rest_body(grad_a, grad_b, la, ra, lb, rb, total_a, total_b, held, done):
    _, z, x = here()
    fetch(
        [(grad_a.at[:, turn(z, 0)], held.at[0]), (grad_b.at[:, :, turn(x, 0)], held.at[1])],
        done,
    )
    total_a[...] = add(held[0], la[...], ra[...])
    total_b[...] = add(held[1], lb[...], rb[...])


def held_call(body, whole, arrays, shapes, slots, block, mebibytes):
    size = sum(item.size * 2 for item in shapes) + sum(item.size * 2 for item in arrays)
    return pl.pallas_call(
        body,
        out_shape=shapes,
        in_specs=[ANY] * len(whole) + [VMEM] * len(arrays),
        out_specs=[VMEM] * len(shapes),
        scratch_shapes=[pltpu.VMEM((slots,) + block, BF), pltpu.SemaphoreType.DMA((slots,))],
        compiler_params=limit(mebibytes),
        cost_estimate=pl.CostEstimate(flops=0, bytes_accessed=2 * size, transcendentals=0),
    )(*whole, *arrays)


def mlp_scatter(grad_a, grad_b):
    block = (2, 4, 32, 1024)
    half = shaped(4, 32, 1024)
    low_a, high_a, low_b, high_b = move(far_plan, (grad_a, grad_b), [half] * 4, 4)
    recv = (hop(low_a, "z", 1), hop(high_a, "z", -1), hop(low_b, "x", 1), hop(high_b, "x", -1))
    ra, la, rb, lb = held_call(
        pass_body, (grad_a, grad_b), recv, [shaped(*block)] * 4, 4, block, 40
    )
    recv = (hop(ra, "z", 1), hop(la, "z", -1), hop(rb, "x", 1), hop(lb, "x", -1))
    return held_call(rest_body, (grad_a, grad_b), recv, [shaped(*block)] * 2, 2, block, 40)


def add(*terms):
    total = terms[0].astype(F32)
    for term in terms[1:]:
        total = total + term.astype(F32)
    return total.astype(BF)


def contract(left, right, dims):
    return lax.dot_general(left, right, (dims, ((), ())), preferred_element_type=F32)


ROWS = ((1,), (0,))
BOTH = ((1,), (1,))
TOPS = ((0,), (0,))
SCALE = HEAD_DIM ** (-0.5)


def probabilities(query, keys):
    scores = contract(query, keys, BOTH) * SCALE
    weight = jnp.exp(scores - jnp.max(scores, axis=-1, keepdims=True))
    return weight / jnp.sum(weight, axis=-1, keepdims=True)


def att_body(normed, qk_w, values_w, query_b, value_b, joined, mixed):
    spot = pl.ds(pl.multiple_of(lax.axis_index("tensor") * 256, 256), 256)
    rows = normed[...]
    pair = contract(rows, qk_w[...].reshape(1024, 512), ROWS)
    joined[:, 0:256] = (pair[:, 0:256] + query_b[:, spot]).astype(BF)
    joined[:, 256:512] = pair[:, 256:].astype(BF)
    last = contract(rows, values_w[...].reshape(1024, 256), ROWS)
    joined[:, 512:768] = (last + value_b[:, spot]).astype(BF)
    for image in range(2):
        line = slice(image * 256, image * 256 + 256)
        parts = []
        for head in range(4):
            query, keys, values = (
                joined[line, base + head * 64 : base + head * 64 + 64] for base in (0, 256, 512)
            )
            probs = probabilities(query, keys).astype(BF)
            parts.append(contract(probs, values, ROWS).astype(BF))
        mixed[line, :] = jnp.concatenate(parts, axis=1)


def mid_body(hidden, m0, m1, m2, m3, w0, w1, w2, w3, out_b, gain, shift, normed, own):
    for image in range(2):
        line = slice(image * 256, image * 256 + 256)
        total = hidden[line, :].astype(F32) + out_b[...]
        for mask, (mixed, weight) in enumerate(((m0, w0), (m1, w1), (m2, w2), (m3, w3))):
            rows = jnp.concatenate(
                [
                    mixed[image * 256 + (spot ^ mask) * 64 : image * 256 + (spot ^ mask) * 64 + 64]
                    for spot in range(4)
                ],
                axis=0,
            )
            total = total + contract(rows, weight[...].reshape(1024, 256), BOTH)
        own[image] = total[:64]
        unit, _ = normalize(total)
        normed[line, :] = (unit * gain[...] + shift[...]).astype(BF)


def spread_rows(own):
    across = swap(own, 2)
    beside = swap(own, 1)
    diagonal = swap(across, 1)
    return jnp.stack([own, beside, across, diagonal], axis=1)


def collect_near(partial):
    near = swap(jnp.stack([partial[:, 1], partial[:, 3]], axis=1).astype(BF), 1)
    return near_total(partial[:, 0], partial[:, 2], near)


def near_total(first, second, near):
    return first + near[:, 0].astype(F32), (second + near[:, 1].astype(F32)).astype(BF)


def collect_far(kept, sent):
    return kept + swap(sent, 2).astype(F32)


def normalize(values):
    center = values - jnp.mean(values, axis=-1, keepdims=True)
    scale = lax.rsqrt(jnp.mean(center * center, axis=-1, keepdims=True) + EPS_NORM)
    return center * scale, scale


def norm_back(grad, unit, scale, gain):
    inner = grad * gain
    first = jnp.mean(inner, axis=-1, keepdims=True)
    second = jnp.mean(inner * unit, axis=-1, keepdims=True)
    return scale * (inner - first - unit * second)


def back_body(
    a0, a1, a2, a3, joined, qk_w, values_w, out_w, hidden, gain_two, shift_two, out_b, down_b, up_b,
    grads, att, sent, kept, vector,
):
    tensor = lax.axis_index("tensor")
    for image in range(2):
        for spot, piece in enumerate((a0, a1, a2, a3)):
            first = image * 256 + spot * 64
            att[first : first + 64, :] = piece[image]
    pair_w = qk_w[...].reshape(1024, 512)
    last_w = values_w[...].reshape(1024, 256)
    mixer = out_w[...].reshape(1024, 256)
    gain = jnp.zeros((1, 1024), F32)
    shift = jnp.zeros((1, 1024), F32)
    for image in range(2):
        line = slice(image * 256, image * 256 + 256)
        grad_mixed = contract(att[line, :], mixer, ROWS).astype(BF)
        parts = ([], [], [])
        for head in range(4):
            query, keys, values = (
                joined[line, base + head * 64 : base + head * 64 + 64] for base in (0, 256, 512)
            )
            grad = grad_mixed[:, head * 64 : head * 64 + 64]
            probs = probabilities(query, keys)
            grad_prob = contract(grad, values, BOTH)
            inner = jnp.sum(grad_prob * probs, axis=-1, keepdims=True)
            score = (probs * (grad_prob - inner)).astype(BF)
            parts[0].append((contract(score, keys, ROWS) * SCALE).astype(BF))
            parts[1].append((contract(score, query, TOPS) * SCALE).astype(BF))
            parts[2].append(contract(probs.astype(BF), grad, TOPS).astype(BF))
        for kind in range(3):
            grads[line, kind * 256 : kind * 256 + 256] = jnp.concatenate(parts[kind], axis=1)
        norm_grad = contract(grads[line, :512], pair_w, BOTH) + contract(
            grads[line, 512:], last_w, BOTH
        )
        unit, _ = normalize(hidden[line, :].astype(F32))
        gain = gain + jnp.sum(norm_grad * unit, axis=0, keepdims=True)
        shift = shift + jnp.sum(norm_grad, axis=0, keepdims=True)
        kept[image, 0] = norm_grad[0:64]
        sent[image, 0] = norm_grad[64:128].astype(BF)
        kept[image, 1] = norm_grad[128:192]
        sent[image, 1] = norm_grad[192:256].astype(BF)
    vector[...] = jnp.zeros(vector.shape, F32)
    rows = (
        (0, gain), (2, shift), (8, out_b[...]), (10, gain_two[...]), (12, shift_two[...]),
        (14, down_b[...]),
    )
    for row, value in rows:
        vector[row : row + 1, :] = value[:, :512]
        vector[row + 1 : row + 2, :] = value[:, 512:]
    spot = pl.ds(pl.multiple_of(lax.rem(tensor, 2) * 256, 256), 256)
    for row, base in ((4, 0), (6, 512)):
        part = jnp.sum(grads[:, base : base + 256].astype(F32), axis=0, keepdims=True)
        vector[pl.ds(row + lax.div(tensor, 2), 1), spot] = part
    vector[pl.ds(16 + 2 * tensor, 1), :] = up_b[:, :512]
    vector[pl.ds(17 + 2 * tensor, 1), :] = up_b[:, 512:]


def grads_body(normed, grads, att, mixed, vector, *rest):
    sends_a, sends_b, own_a, own_b = rest[0:3], rest[3:6], rest[6], rest[7]
    grad_a, grad_b, low, done = rest[8:]
    _, z, x = here()
    grad_a[...] = contract(normed[...], grads[:, 0:512], TOPS).astype(BF).reshape(grad_a.shape)
    pairs = [(grad_a.at[:, turn(z, 0)], own_a)]
    low[...] = vector[...].astype(BF)
    for step in range(1, 4):
        target = sends_a[step - 1]
        for half in range(2):
            pairs.append((grad_a.at[half, turn(z, step)], target.at[pl.ds(4 * half, 4)]))
        pairs.append((low, target.at[8]))
    copies = [
        pltpu.make_async_copy(source, target, done.at[spot])
        for spot, (source, target) in enumerate(pairs)
    ]
    for copy in copies:
        copy.start()
    last = contract(normed[...], grads[:, 512:768], TOPS).astype(BF)
    grad_b[:, :, :, :, 0:256] = last.reshape(2, 4, 4, 32, 256)
    last = contract(att[...], mixed[...], TOPS).astype(BF)
    grad_b[:, :, :, :, 256:512] = last.reshape(2, 4, 4, 32, 256)
    others = [(grad_b.at[:, :, turn(x, 0)], own_b)]
    for step in range(1, 4):
        others.append((grad_b.at[:, :, turn(x, step)], sends_b[step - 1]))
    more = [
        pltpu.make_async_copy(source, target, done.at[len(pairs) + spot])
        for spot, (source, target) in enumerate(others)
    ]
    for copy in more:
        copy.start()
    for copy in copies + more:
        copy.wait()


def second_body(*refs):
    a1, a2, a3, own_a, b1, b2, b3, own_b, vector, mlp_a, mlp_b = refs[:11]
    outs_a, outs_b, sum_a, sum_b = refs[11:15], refs[15:19], refs[19], refs[20]
    _, z, x = here()
    for yh in range(2):
        part = slice(4 * yh, 4 * yh + 4)
        sum_a[yh] = add(own_a[yh], a1[part], a2[part], a3[part])
        sum_b[yh] = add(own_b[yh], b1[yh], b2[yh], b3[yh])
    low = add(vector[...], a1[8], a2[8], a3[8])
    for step in range(4):
        for out, total, mlp, index in (
            (outs_a[step], sum_a, mlp_a, turn(x, step)),
            (outs_b[step], sum_b, mlp_b, turn(z, step)),
        ):
            for yh in range(2):
                out[yh] = total[yh, index]
                out[2 + yh] = mlp[yh, index, :, 0:512]
                out[4 + yh] = mlp[yh, index, :, 512:1024]
        outs_a[step][6] = low


def third_body(a0, a1, a2, a3, b0, b1, b2, b3, send, own):
    yh, _, _ = here()
    for spot in range(3):
        for base, pieces in ((0, (a0, a1, a2, a3)), (3, (b0, b1, b2, b3))):
            mine = [piece[2 * spot + yh].astype(F32) for piece in pieces]
            other = [piece[2 * spot + 1 - yh].astype(F32) for piece in pieces]
            own[base + spot] = (mine[0] + mine[1]) + (mine[2] + mine[3])
            send[base + spot] = ((other[0] + other[1]) + (other[2] + other[3])).astype(BF)
    total = [piece[6].astype(F32) for piece in (a0, a1, a2, a3)]
    total = (total[0] + total[1]) + (total[2] + total[3])
    own[6] = total
    send[6] = total.astype(BF)


def last_body(own, came, qkv, out, up, down, vector):
    def total(spot):
        return own[spot] + came[spot].astype(F32)

    att_a, att_b = total(0), total(3)
    qkv[0] = att_a[:, 0:256]
    qkv[1] = att_a[:, 256:512]
    qkv[2] = att_b[:, 0:256]
    out[...] = att_b[:, 256:512]
    up[:, 0:512] = total(1)
    up[:, 512:1024] = total(2)
    down[:, 0:512] = total(4)
    down[:, 512:1024] = total(5)
    vector[...] = total(6)


def att_scatter(normed, grads, att, mixed, vector, mlp_a, mlp_b):
    block = (2, 4, 32, 512)
    shapes = [shaped(9, 32, 512)] * 3 + [shaped(*block)] * 5
    arrays = (normed, grads, att, mixed, vector)
    size = sum(item.size * 2 for item in shapes) + sum(item.size * 2 for item in arrays)
    results = pl.pallas_call(
        grads_body,
        out_shape=shapes,
        in_specs=[VMEM] * 5,
        out_specs=[ANY] * 8,
        scratch_shapes=[
            pltpu.VMEM((2, 4, 4, 32, 512), BF),
            pltpu.VMEM((2, 4, 4, 32, 512), BF),
            pltpu.VMEM((32, 512), BF),
            pltpu.SemaphoreType.DMA((14,)),
        ],
        compiler_params=limit(40),
        cost_estimate=pl.CostEstimate(
            flops=2 * 512 * 1024 * 1024, bytes_accessed=size, transcendentals=0
        ),
    )(*arrays)
    came_a = [hop(results[step - 1], "z", step) for step in (1, 2, 3)]
    came_b = [hop(results[2 + step], "x", step) for step in (1, 2, 3)]
    pieces = whole_call(
        second_body,
        (*came_a, results[6], *came_b, results[7], vector, mlp_a, mlp_b),
        [shaped(7, 32, 512)] * 4 + [shaped(6, 32, 512)] * 4,
        40,
        scratch=[pltpu.VMEM(block, BF), pltpu.VMEM(block, BF)],
    )
    came_a = [hop(pieces[step], "x", step) for step in (1, 2, 3)]
    came_b = [hop(pieces[4 + step], "z", step) for step in (1, 2, 3)]
    send, own = whole_call(
        third_body,
        (pieces[0], *came_a, pieces[4], *came_b),
        [shaped(7, 32, 512), shaped(7, 32, 512, kind=F32)],
        40,
    )
    shapes = [(3, 32, 256), (32, 256), (32, 1024), (32, 1024), (32, 512)]
    return whole_call(
        last_body, (own, hop(send, "y", 1)), [shaped(*shape, kind=F32) for shape in shapes], 40
    )


def dot(spec, left, right):
    return jnp.einsum(spec, left, right, preferred_element_type=F32)


def local(
    tokens,
    dealt,
    cotangent,
    qkv_weight,
    out_weight,
    up_weight,
    down_weight,
    norm1_gain,
    norm1_bias,
    query_bias,
    value_bias,
    out_bias,
    norm2_gain,
    norm2_bias,
    up_bias,
    down_bias,
):
    tensor = lax.axis_index("tensor")
    rows = tokens.shape[2]
    width = tokens.shape[3]
    count = 8 * rows
    weight_rows = (YH, ZN, XN, 32)

    def own_part(vector, size):
        return lax.dynamic_slice_in_dim(vector[0], tensor * size, size, 0)

    (own,) = whole_call(
        pack_body,
        (jnp.transpose(qkv_weight[0], (1, 0, 2)), out_weight[0], up_weight[0], down_weight[0]),
        [shaped(32, 3072)],
        16,
    )
    part_a, part_b = whole_call(
        pair_body, (own, hop(own, "y", 1)), [shaped(2, 32, 1536)] * 2, 16
    )
    pieces = near_gather(part_a, "x") + near_gather(part_b, "z")
    shapes = [shaped(2, 4, 32, 512)] * 2 + [shaped(2, 4, 32, 1024)] * 2
    att_a, att_b, mlp_a, mlp_b = move(first_plan, pieces, shapes, 16)
    att_a, att_b = near_gather(att_a, "z"), near_gather(att_b, "x")
    mlp_a = ring_gather(after(mlp_a, att_a[1]), "z")
    mlp_b = ring_gather(after(mlp_b, att_b[1]), "x")
    shapes = [shaped(*weight_rows, 512), shaped(*weight_rows, 256), shaped(*weight_rows, 256)]
    qk_w, values_w, out_w = move(att_plan, att_a + att_b, shapes, 12)
    up_w, down_w = move(mlp_plan, mlp_a + mlp_b, [shaped(*weight_rows, 1024)] * 2, 10)
    up_w, down_w = up_w.reshape(width, -1), down_w.reshape(width, -1)
    out_across = swap(out_w, 2)
    out_beside, out_diagonal = swap(out_w, 1), swap(out_across, 1)

    live = dealt.astype(F32).reshape(2, 1, 1)
    own_tokens = tokens[:, 0]
    grad_own = cotangent[:, 0].astype(F32) * live
    hidden = spread_rows(own_tokens).reshape(count, width)
    down_all = spread_rows(grad_own.astype(BF)).reshape(count, width)
    unit_one, _ = normalize(hidden.astype(F32))
    normed = (unit_one * norm1_gain[0] + norm1_bias[0]).astype(BF)
    joined, mixed = whole_call(
        att_body,
        (normed, qk_w, values_w, query_bias, value_bias),
        [shaped(count, 768), shaped(count, 256)],
        48,
        flops=2 * 512 * 1024 * 1024,
    )
    mixed_across = swap(mixed, 2)
    mixed_beside, mixed_diagonal = swap(mixed, 1), swap(mixed_across, 1)
    normed_two, middle_own = whole_call(
        mid_body,
        (
            hidden,
            mixed,
            mixed_beside,
            mixed_across,
            mixed_diagonal,
            out_w,
            out_beside,
            out_across,
            out_diagonal,
            out_bias,
            norm2_gain,
            norm2_bias,
        ),
        [shaped(count, width), shaped(2, rows, width, kind=F32)],
        48,
        flops=2 * 512 * 1024 * 1024,
    )
    upward = dot("sd,df->sf", normed_two, up_w) + own_part(up_bias, 1024)
    share = 0.5 * (1.0 + lax.erf(upward * (0.5**0.5)))
    activated = (upward * share).astype(BF)
    slope = share + upward * (jnp.exp(-0.5 * upward * upward) * (0.5 / jnp.pi) ** 0.5)

    grad_up = (dot("se,ef->sf", down_all, down_w) * slope).astype(BF)
    norm_two_part = dot("sf,df->sd", grad_up, up_w).reshape(2, 4, rows, width)
    kept_two, sent_two = collect_near(norm_two_part)
    grad_norm_two = collect_far(kept_two, sent_two)
    up_grad = dot("sd,sf->df", normed_two, grad_up).astype(BF)
    down_grad = dot("se,sf->ef", down_all, activated).astype(BF)
    up_grad, down_grad = after(up_grad, sent_two), after(down_grad, sent_two)
    mlp_a, mlp_b = mlp_scatter(
        up_grad.reshape(*weight_rows, -1), down_grad.reshape(*weight_rows, -1)
    )
    up_b_grad = jnp.sum(grad_up.astype(F32), axis=0, keepdims=True)
    down_b_grad = jnp.sum(grad_own, axis=(0, 1))[None]

    unit_two, scale_two = normalize(middle_own)
    gain_two_grad = jnp.sum(grad_norm_two * unit_two, axis=(0, 1))[None]
    shift_two_grad = jnp.sum(grad_norm_two, axis=(0, 1))[None]
    grad_middle = grad_own + norm_back(grad_norm_two, unit_two, scale_two, norm2_gain[0])
    grad_att = grad_middle.astype(BF)
    out_b_grad = jnp.sum(grad_att.astype(F32), axis=(0, 1))[None]
    att_across = swap(grad_att, 2)
    att_beside, att_diagonal = swap(grad_att, 1), swap(att_across, 1)

    down_part = dot("sf,ef->se", activated, down_w).reshape(2, 4, rows, width)
    down_part = after(down_part, grad_norm_two)
    block_out = (
        (middle_own + (collect_far(*collect_near(down_part)) + down_bias[0])) * live
    ).astype(BF)[:, None]

    grads, att_all, sent, kept, vector = whole_call(
        back_body,
        (
            grad_att,
            att_beside,
            att_across,
            att_diagonal,
            joined,
            qk_w,
            values_w,
            out_w,
            hidden,
            gain_two_grad,
            shift_two_grad,
            out_b_grad,
            down_b_grad,
            up_b_grad,
        ),
        [
            shaped(count, 768),
            shaped(count, width),
            shaped(2, 2, rows, width),
            shaped(2, 2, rows, width, kind=F32),
            shaped(32, 512, kind=F32),
        ],
        56,
        flops=3 * 512 * 1024 * 1024,
    )
    qkv_grad, out_grad, up_grad, down_grad, vector = att_scatter(
        normed, grads, att_all, mixed, vector, mlp_a, mlp_b
    )
    near = swap(sent, 1)
    grad_norm_one = collect_far(*near_total(kept[:, 0], kept[:, 1], near))
    unit_own, scale_own = normalize(own_tokens.astype(F32))
    input_grad = grad_middle + norm_back(grad_norm_one, unit_own, scale_own, norm1_gain[0])
    input_grad = input_grad.astype(BF)[:, None]

    vector = vector + swap(vector, 1)
    vector = (vector + swap(vector, 2))[:24].reshape(1, -1)
    parts = [vector[:, k * width : (k + 1) * width] for k in range(8)]
    return (
        block_out,
        input_grad,
        jnp.transpose(qkv_grad, (1, 0, 2))[None],
        out_grad[None],
        up_grad[None],
        down_grad[None],
        *parts[:7],
        vector[:, 8 * width :],
        parts[7],
    )


def solution(mesh):
    rows = P(None, "fsdp", "tensor", None)
    matrix = P(None, "fsdp", "tensor")
    qkv = P(None, "fsdp", None, "tensor")
    return jax.shard_map(
        local,
        mesh=mesh,
        in_specs=(rows, P(None, "fsdp"), rows, qkv, matrix, matrix, matrix) + (P(),) * 9,
        out_specs=(rows, rows, qkv, matrix, matrix, matrix) + (P(),) * 9,
        check_vma=False,
    )
```

```python
import jax
import jax.numpy as jnp
from jax import lax
from jax.experimental import pallas as pl
from jax.experimental.pallas import tpu as pltpu
from jax.sharding import PartitionSpec as P

HEAD_DIM = 64
EPS_NORM = 1e-06
BF = jnp.bfloat16
F32 = jnp.float32

YH, ZN, XN = 2, 4, 4


def fsdp_perm(dx, dz, dy):
    pairs = []
    for source in range(YH * ZN * XN):
        yh, z, x = source // (ZN * XN), (source // XN) % ZN, source % XN
        target = (((yh + dy) % YH) * ZN + (z + dz) % ZN) * XN + (x + dx) % XN
        pairs.append((source, target))
    return pairs


def hop(array, axis, step):
    move = {"x": (step, 0, 0), "z": (0, step, 0), "y": (0, 0, step)}[axis]
    return lax.ppermute(array, "fsdp", fsdp_perm(*move))


def swap(array, mask):
    return lax.ppermute(array, "tensor", [(i, i ^ mask) for i in range(4)])


def here():
    index = lax.axis_index("fsdp")
    plane = ZN * XN
    return lax.div(index, plane), lax.rem(lax.div(index, XN), ZN), lax.rem(index, XN)


def turn(index, step):
    return lax.rem(index + step, 4)


def shaped(*shape, kind=BF):
    return jax.ShapeDtypeStruct(shape, kind)


def limit(mebibytes):
    return pltpu.CompilerParams(vmem_limit_bytes=mebibytes << 20)


VMEM = pl.BlockSpec(memory_space=pltpu.VMEM)
ANY = pl.BlockSpec(memory_space=pl.ANY)


def move(plan, arrays, shapes, count):
    def body(*refs):
        inputs, outputs, done = refs[: len(arrays)], refs[len(arrays) : -1], refs[-1]
        pairs = plan(inputs, outputs)
        copies = [
            pltpu.make_async_copy(source, target, done.at[spot])
            for spot, (source, target) in enumerate(pairs)
        ]
        for copy in copies:
            copy.start()
        for copy in copies:
            copy.wait()

    size = sum(item.size * 2 for item in shapes)
    return pl.pallas_call(
        body,
        out_shape=shapes,
        in_specs=[ANY] * len(arrays),
        out_specs=[VMEM] * len(shapes),
        scratch_shapes=[pltpu.SemaphoreType.DMA((count,))],
        compiler_params=limit(16),
        cost_estimate=pl.CostEstimate(flops=0, bytes_accessed=2 * size, transcendentals=0),
    )(*arrays)


def whole_call(body, arrays, shapes, mebibytes, flops=0, scratch=()):
    size = sum(item.size * item.dtype.itemsize for item in list(shapes) + list(arrays))
    return pl.pallas_call(
        body,
        out_shape=shapes,
        scratch_shapes=scratch,
        compiler_params=limit(mebibytes),
        cost_estimate=pl.CostEstimate(flops=flops, bytes_accessed=size, transcendentals=0),
    )(*arrays)


def after(value, *others):
    return lax.optimization_barrier((value,) + others)[0]


def near_gather(block, axis):
    left = hop(block, axis, 1)
    right = hop(block, axis, -1)
    far = hop(block, axis, 2)
    return [block, right, far, left]


def ring_gather(block, axis):
    left = hop(block, axis, 1)
    right = hop(block, axis, -1)
    first = hop(left[0], axis, 1)
    second = hop(right[1], axis, -1)
    return [block, right, left, first, second]


def pack_body(qkv, out, up, down, own):
    own[:, 0:256] = qkv[0]
    own[:, 256:512] = qkv[1]
    own[:, 512:1536] = up[...]
    own[:, 1536:1792] = qkv[2]
    own[:, 1792:2048] = out[...]
    own[:, 2048:3072] = down[...]


def pair_body(own, other, part_a, part_b):
    yh, _, _ = here()
    part_a[yh] = own[:, :1536]
    part_b[yh] = own[:, 1536:]
    part_a[1 - yh] = other[:, :1536]
    part_b[1 - yh] = other[:, 1536:]


def first_plan(inputs, outputs):
    _, z, x = here()
    att_a, att_b, mlp_a, mlp_b = outputs
    pairs = []
    for step in range(4):
        piece_a, piece_b = inputs[step], inputs[4 + step]
        pairs.append((piece_a.at[:, :, 0:512], att_a.at[:, turn(x, step)]))
        pairs.append((piece_b.at[:, :, 0:512], att_b.at[:, turn(z, step)]))
        pairs.append((piece_a.at[:, :, 512:1536], mlp_a.at[:, turn(x, step)]))
        pairs.append((piece_b.at[:, :, 512:1536], mlp_b.at[:, turn(z, step)]))
    return pairs


def att_plan(inputs, outputs):
    _, z, x = here()
    qk_w, values_w, out_w = outputs
    pairs = []
    for step in range(4):
        piece_a, piece_b = inputs[step], inputs[4 + step]
        pairs.append((piece_a, qk_w.at[:, turn(z, step)]))
        pairs.append((piece_b.at[:, :, :, 0:256], values_w.at[:, :, turn(x, step)]))
        pairs.append((piece_b.at[:, :, :, 256:512], out_w.at[:, :, turn(x, step)]))
    return pairs


def mlp_plan(inputs, outputs):
    _, z, x = here()
    up_w, down_w = outputs
    pairs = []
    for spot, step in enumerate((0, 1, 3)):
        pairs.append((inputs[spot], up_w.at[:, turn(z, step)]))
        pairs.append((inputs[5 + spot], down_w.at[:, :, turn(x, step)]))
    for half in range(2):
        pairs.append((inputs[3 + half], up_w.at[half, turn(z, 2)]))
        pairs.append((inputs[8 + half], down_w.at[half, :, turn(x, 2)]))
    return pairs


def far_plan(inputs, outputs):
    _, z, x = here()
    grad_a, grad_b = inputs
    pairs = []
    for half in range(2):
        pairs.append((grad_a.at[half, turn(z, 2)], outputs[half]))
        pairs.append((grad_b.at[half, :, turn(x, 2)], outputs[2 + half]))
    return pairs


def fetch(pairs, done):
    copies = [
        pltpu.make_async_copy(source, target, done.at[spot])
        for spot, (source, target) in enumerate(pairs)
    ]
    for copy in copies:
        copy.start()
    for copy in copies:
        copy.wait()


def pass_body(grad_a, grad_b, low_a, high_a, low_b, high_b, ra, la, rb, lb, held, done):
    _, z, x = here()
    fetch(
        [
            (grad_a.at[:, turn(z, 1)], held.at[0]),
            (grad_a.at[:, turn(z, 3)], held.at[1]),
            (grad_b.at[:, :, turn(x, 1)], held.at[2]),
            (grad_b.at[:, :, turn(x, 3)], held.at[3]),
        ],
        done,
    )
    for spot, (right, left, low, high) in enumerate(
        ((ra, la, low_a, high_a), (rb, lb, low_b, high_b))
    ):
        right[0] = add(held[2 * spot, 0], low[...])
        right[1] = held[2 * spot, 1]
        left[0] = held[2 * spot + 1, 0]
        left[1] = add(held[2 * spot + 1, 1], high[...])


def rest_body(grad_a, grad_b, la, ra, lb, rb, total_a, total_b, held, done):
    _, z, x = here()
    fetch(
        [(grad_a.at[:, turn(z, 0)], held.at[0]), (grad_b.at[:, :, turn(x, 0)], held.at[1])],
        done,
    )
    total_a[...] = add(held[0], la[...], ra[...])
    total_b[...] = add(held[1], lb[...], rb[...])


def held_call(body, whole, arrays, shapes, slots, block, mebibytes):
    size = sum(item.size * 2 for item in shapes) + sum(item.size * 2 for item in arrays)
    return pl.pallas_call(
        body,
        out_shape=shapes,
        in_specs=[ANY] * len(whole) + [VMEM] * len(arrays),
        out_specs=[VMEM] * len(shapes),
        scratch_shapes=[pltpu.VMEM((slots,) + block, BF), pltpu.SemaphoreType.DMA((slots,))],
        compiler_params=limit(mebibytes),
        cost_estimate=pl.CostEstimate(flops=0, bytes_accessed=2 * size, transcendentals=0),
    )(*whole, *arrays)


def mlp_scatter(grad_a, grad_b):
    block = (2, 4, 32, 1024)
    half = shaped(4, 32, 1024)
    low_a, high_a, low_b, high_b = move(far_plan, (grad_a, grad_b), [half] * 4, 4)
    recv = (hop(low_a, "z", 1), hop(high_a, "z", -1), hop(low_b, "x", 1), hop(high_b, "x", -1))
    ra, la, rb, lb = held_call(
        pass_body, (grad_a, grad_b), recv, [shaped(*block)] * 4, 4, block, 40
    )
    recv = (hop(ra, "z", 1), hop(la, "z", -1), hop(rb, "x", 1), hop(lb, "x", -1))
    return held_call(rest_body, (grad_a, grad_b), recv, [shaped(*block)] * 2, 2, block, 40)


def add(*terms):
    total = terms[0].astype(F32)
    for term in terms[1:]:
        total = total + term.astype(F32)
    return total.astype(BF)


def contract(left, right, dims):
    return lax.dot_general(left, right, (dims, ((), ())), preferred_element_type=F32)


ROWS = ((1,), (0,))
BOTH = ((1,), (1,))
TOPS = ((0,), (0,))
SCALE = HEAD_DIM ** (-0.5)


def probabilities(query, keys):
    scores = contract(query, keys, BOTH) * SCALE
    weight = jnp.exp(scores - jnp.max(scores, axis=-1, keepdims=True))
    return weight / jnp.sum(weight, axis=-1, keepdims=True)


def att_body(normed, qk_w, values_w, out_w, query_b, value_b, joined, mixed, sent, kept):
    spot = pl.ds(pl.multiple_of(lax.axis_index("tensor") * 256, 256), 256)
    rows = normed[...]
    mixer = out_w[...].reshape(1024, 256)
    pair = contract(rows, qk_w[...].reshape(1024, 512), ROWS)
    joined[:, 0:256] = (pair[:, 0:256] + query_b[:, spot]).astype(BF)
    joined[:, 256:512] = pair[:, 256:].astype(BF)
    last = contract(rows, values_w[...].reshape(1024, 256), ROWS)
    joined[:, 512:768] = (last + value_b[:, spot]).astype(BF)
    for image in range(2):
        line = slice(image * 256, image * 256 + 256)
        parts = []
        for head in range(4):
            query, keys, values = (
                joined[line, base + head * 64 : base + head * 64 + 64] for base in (0, 256, 512)
            )
            probs = probabilities(query, keys).astype(BF)
            parts.append(contract(probs, values, ROWS).astype(BF))
        whole = jnp.concatenate(parts, axis=1)
        mixed[line, :] = whole
        split_blocks(image, contract(whole, mixer, BOTH), sent, kept)


def split_blocks(image, part, sent, kept):
    kept[image, 0] = part[0:64]
    sent[image, 0] = part[64:128].astype(BF)
    kept[image, 1] = part[128:192]
    sent[image, 1] = part[192:256].astype(BF)


def spread_rows(own, *wait):
    beside = swap(own, 1)
    across = swap(after(own, *wait) if wait else own, 2)
    return own, beside, across, swap(across, 1)


def collect_near(partial):
    near = swap(jnp.stack([partial[:, 1], partial[:, 3]], axis=1).astype(BF), 1)
    return near_total(partial[:, 0], partial[:, 2], near)


def near_total(first, second, near):
    return first + near[:, 0].astype(F32), (second + near[:, 1].astype(F32)).astype(BF)


def collect_far(kept, sent):
    return kept + swap(sent, 2).astype(F32)


def normalize(values):
    center = values - jnp.mean(values, axis=-1, keepdims=True)
    scale = lax.rsqrt(jnp.mean(center * center, axis=-1, keepdims=True) + EPS_NORM)
    return center * scale, scale


def norm_back(grad, unit, scale, gain):
    inner = grad * gain
    first = jnp.mean(inner, axis=-1, keepdims=True)
    second = jnp.mean(inner * unit, axis=-1, keepdims=True)
    return scale * (inner - first - unit * second)


def back_body(
    a0, a1, a2, a3, joined, qk_w, values_w, out_w, hidden, gain_two, shift_two, out_b, down_b, up_b,
    grads, att, sent, kept, vector,
):
    tensor = lax.axis_index("tensor")
    for image in range(2):
        for spot, piece in enumerate((a0, a1, a2, a3)):
            first = image * 256 + spot * 64
            att[first : first + 64, :] = piece[image]
    pair_w = qk_w[...].reshape(1024, 512)
    last_w = values_w[...].reshape(1024, 256)
    mixer = out_w[...].reshape(1024, 256)
    gain = jnp.zeros((1, 1024), F32)
    shift = jnp.zeros((1, 1024), F32)
    for image in range(2):
        line = slice(image * 256, image * 256 + 256)
        grad_mixed = contract(att[line, :], mixer, ROWS).astype(BF)
        parts = ([], [], [])
        for head in range(4):
            query, keys, values = (
                joined[line, base + head * 64 : base + head * 64 + 64] for base in (0, 256, 512)
            )
            grad = grad_mixed[:, head * 64 : head * 64 + 64]
            probs = probabilities(query, keys)
            grad_prob = contract(grad, values, BOTH)
            inner = jnp.sum(grad_prob * probs, axis=-1, keepdims=True)
            score = (probs * (grad_prob - inner)).astype(BF)
            parts[0].append((contract(score, keys, ROWS) * SCALE).astype(BF))
            parts[1].append((contract(score, query, TOPS) * SCALE).astype(BF))
            parts[2].append(contract(probs.astype(BF), grad, TOPS).astype(BF))
        for kind in range(3):
            grads[line, kind * 256 : kind * 256 + 256] = jnp.concatenate(parts[kind], axis=1)
        norm_grad = contract(grads[line, :512], pair_w, BOTH) + contract(
            grads[line, 512:], last_w, BOTH
        )
        unit, _ = normalize(hidden[line, :].astype(F32))
        gain = gain + jnp.sum(norm_grad * unit, axis=0, keepdims=True)
        shift = shift + jnp.sum(norm_grad, axis=0, keepdims=True)
        split_blocks(image, norm_grad, sent, kept)
    vector[...] = jnp.zeros(vector.shape, F32)
    rows = (
        (0, gain), (2, shift), (8, out_b[...]), (10, gain_two[...]), (12, shift_two[...]),
        (14, down_b[...]),
    )
    for row, value in rows:
        vector[row : row + 1, :] = value[:, :512]
        vector[row + 1 : row + 2, :] = value[:, 512:]
    spot = pl.ds(pl.multiple_of(lax.rem(tensor, 2) * 256, 256), 256)
    for row, base in ((4, 0), (6, 512)):
        part = jnp.sum(grads[:, base : base + 256].astype(F32), axis=0, keepdims=True)
        vector[pl.ds(row + lax.div(tensor, 2), 1), spot] = part
    vector[pl.ds(16 + 2 * tensor, 1), :] = up_b[:, :512]
    vector[pl.ds(17 + 2 * tensor, 1), :] = up_b[:, 512:]


def grads_body(normed, grads, att, mixed, vector, *rest):
    sends_a, sends_b, own_a, own_b = rest[0:3], rest[3:6], rest[6], rest[7]
    grad_a, grad_b, low, done = rest[8:]
    _, z, x = here()
    grad_a[...] = contract(normed[...], grads[:, 0:512], TOPS).astype(BF).reshape(grad_a.shape)
    pairs = [(grad_a.at[:, turn(z, 0)], own_a)]
    low[...] = vector[...].astype(BF)
    for step in range(1, 4):
        target = sends_a[step - 1]
        for half in range(2):
            pairs.append((grad_a.at[half, turn(z, step)], target.at[pl.ds(4 * half, 4)]))
        pairs.append((low, target.at[8]))
    copies = [
        pltpu.make_async_copy(source, target, done.at[spot])
        for spot, (source, target) in enumerate(pairs)
    ]
    for copy in copies:
        copy.start()
    last = contract(normed[...], grads[:, 512:768], TOPS).astype(BF)
    grad_b[:, :, :, :, 0:256] = last.reshape(2, 4, 4, 32, 256)
    last = contract(att[...], mixed[...], TOPS).astype(BF)
    grad_b[:, :, :, :, 256:512] = last.reshape(2, 4, 4, 32, 256)
    others = [(grad_b.at[:, :, turn(x, 0)], own_b)]
    for step in range(1, 4):
        others.append((grad_b.at[:, :, turn(x, step)], sends_b[step - 1]))
    more = [
        pltpu.make_async_copy(source, target, done.at[len(pairs) + spot])
        for spot, (source, target) in enumerate(others)
    ]
    for copy in more:
        copy.start()
    for copy in copies + more:
        copy.wait()


def second_body(*refs):
    a1, a2, a3, own_a, b1, b2, b3, own_b, vector, mlp_a, mlp_b = refs[:11]
    outs_a, outs_b, sum_a, sum_b = refs[11:15], refs[15:19], refs[19], refs[20]
    _, z, x = here()
    for yh in range(2):
        part = slice(4 * yh, 4 * yh + 4)
        sum_a[yh] = add(own_a[yh], a1[part], a2[part], a3[part])
        sum_b[yh] = add(own_b[yh], b1[yh], b2[yh], b3[yh])
    low = add(vector[...], a1[8], a2[8], a3[8])
    for step in range(4):
        for out, total, mlp, index in (
            (outs_a[step], sum_a, mlp_a, turn(x, step)),
            (outs_b[step], sum_b, mlp_b, turn(z, step)),
        ):
            for yh in range(2):
                out[yh] = total[yh, index]
                out[2 + yh] = mlp[yh, index, :, 0:512]
                out[4 + yh] = mlp[yh, index, :, 512:1024]
        outs_a[step][6] = low


def third_body(a0, a1, a2, a3, b0, b1, b2, b3, send, own):
    yh, _, _ = here()
    for spot in range(3):
        for base, pieces in ((0, (a0, a1, a2, a3)), (3, (b0, b1, b2, b3))):
            mine = [piece[2 * spot + yh].astype(F32) for piece in pieces]
            other = [piece[2 * spot + 1 - yh].astype(F32) for piece in pieces]
            own[base + spot] = (mine[0] + mine[1]) + (mine[2] + mine[3])
            send[base + spot] = ((other[0] + other[1]) + (other[2] + other[3])).astype(BF)
    total = [piece[6].astype(F32) for piece in (a0, a1, a2, a3)]
    total = (total[0] + total[1]) + (total[2] + total[3])
    own[6] = total
    send[6] = total.astype(BF)


def last_body(own, came, qkv, out, up, down, vector):
    def total(spot):
        return own[spot] + came[spot].astype(F32)

    att_a, att_b = total(0), total(3)
    qkv[0] = att_a[:, 0:256]
    qkv[1] = att_a[:, 256:512]
    qkv[2] = att_b[:, 0:256]
    out[...] = att_b[:, 256:512]
    up[:, 0:512] = total(1)
    up[:, 512:1024] = total(2)
    down[:, 0:512] = total(4)
    down[:, 512:1024] = total(5)
    vector[...] = total(6)


def att_scatter(normed, grads, att, mixed, vector, mlp_a, mlp_b):
    block = (2, 4, 32, 512)
    shapes = [shaped(9, 32, 512)] * 3 + [shaped(*block)] * 5
    arrays = (normed, grads, att, mixed, vector)
    size = sum(item.size * 2 for item in shapes) + sum(item.size * 2 for item in arrays)
    results = pl.pallas_call(
        grads_body,
        out_shape=shapes,
        in_specs=[VMEM] * 5,
        out_specs=[ANY] * 8,
        scratch_shapes=[
            pltpu.VMEM((2, 4, 4, 32, 512), BF),
            pltpu.VMEM((2, 4, 4, 32, 512), BF),
            pltpu.VMEM((32, 512), BF),
            pltpu.SemaphoreType.DMA((14,)),
        ],
        compiler_params=limit(40),
        cost_estimate=pl.CostEstimate(
            flops=2 * 512 * 1024 * 1024, bytes_accessed=size, transcendentals=0
        ),
    )(*arrays)
    came_a = [hop(results[step - 1], "z", step) for step in (1, 2, 3)]
    came_b = [hop(results[2 + step], "x", step) for step in (1, 2, 3)]
    pieces = whole_call(
        second_body,
        (*came_a, results[6], *came_b, results[7], vector, mlp_a, mlp_b),
        [shaped(7, 32, 512)] * 4 + [shaped(6, 32, 512)] * 4,
        40,
        scratch=[pltpu.VMEM(block, BF), pltpu.VMEM(block, BF)],
    )
    came_a = [hop(pieces[step], "x", step) for step in (1, 2, 3)]
    came_b = [hop(pieces[4 + step], "z", step) for step in (1, 2, 3)]
    send, own = whole_call(
        third_body,
        (pieces[0], *came_a, pieces[4], *came_b),
        [shaped(7, 32, 512), shaped(7, 32, 512, kind=F32)],
        40,
    )
    shapes = [(3, 32, 256), (32, 256), (32, 1024), (32, 1024), (32, 512)]
    return whole_call(
        last_body, (own, hop(send, "y", 1)), [shaped(*shape, kind=F32) for shape in shapes], 40
    )


def dot(spec, left, right):
    return jnp.einsum(spec, left, right, preferred_element_type=F32)


def local(
    tokens,
    dealt,
    cotangent,
    qkv_weight,
    out_weight,
    up_weight,
    down_weight,
    norm1_gain,
    norm1_bias,
    query_bias,
    value_bias,
    out_bias,
    norm2_gain,
    norm2_bias,
    up_bias,
    down_bias,
):
    tensor = lax.axis_index("tensor")
    rows = tokens.shape[2]
    width = tokens.shape[3]
    count = 8 * rows
    weight_rows = (YH, ZN, XN, 32)

    def own_part(vector, size):
        return lax.dynamic_slice_in_dim(vector[0], tensor * size, size, 0)

    (own,) = whole_call(
        pack_body,
        (jnp.transpose(qkv_weight[0], (1, 0, 2)), out_weight[0], up_weight[0], down_weight[0]),
        [shaped(32, 3072)],
        16,
    )
    other = hop(own, "y", 1)
    part_a, part_b = whole_call(pair_body, (own, other), [shaped(2, 32, 1536)] * 2, 16)
    pieces = near_gather(part_a, "x") + near_gather(part_b, "z")
    shapes = [shaped(2, 4, 32, 512)] * 2 + [shaped(2, 4, 32, 1024)] * 2
    att_a, att_b, mlp_a, mlp_b = move(first_plan, pieces, shapes, 16)
    att_a, att_b = near_gather(att_a, "z"), near_gather(att_b, "x")
    mlp_a = ring_gather(after(mlp_a, *att_a), "z")
    mlp_b = ring_gather(after(mlp_b, *att_b), "x")
    shapes = [shaped(*weight_rows, 512), shaped(*weight_rows, 256), shaped(*weight_rows, 256)]
    qk_w, values_w, out_w = move(att_plan, att_a + att_b, shapes, 12)
    up_w, down_w = move(mlp_plan, mlp_a + mlp_b, [shaped(*weight_rows, 1024)] * 2, 10)
    up_w, down_w = up_w.reshape(width, -1), down_w.reshape(width, -1)

    live = dealt.astype(F32).reshape(2, 1, 1)
    own_tokens = tokens[:, 0]
    grad_own = cotangent[:, 0].astype(F32) * live
    both = spread_rows(jnp.stack([own_tokens, grad_own.astype(BF)]), other)
    hidden = jnp.stack([item[0] for item in both], axis=1).reshape(count, width)
    down_all = jnp.stack([item[1] for item in both], axis=1).reshape(count, width)
    unit_one, _ = normalize(hidden.astype(F32))
    normed = (unit_one * norm1_gain[0] + norm1_bias[0]).astype(BF)
    joined, mixed, sent, kept = whole_call(
        att_body,
        (normed, qk_w, values_w, out_w, query_bias, value_bias),
        [
            shaped(count, 768),
            shaped(count, 256),
            shaped(2, 2, rows, width),
            shaped(2, 2, rows, width, kind=F32),
        ],
        48,
        flops=2 * 512 * 1024 * 1024,
    )
    branch = collect_far(*near_total(kept[:, 0], kept[:, 1], swap(sent, 1)))
    middle_own = own_tokens.astype(F32) + (branch + out_bias[0])
    unit_two, scale_two = normalize(middle_own)
    normed_two = spread_rows((unit_two * norm2_gain[0] + norm2_bias[0]).astype(BF))
    normed_two = jnp.stack(normed_two, axis=1).reshape(count, width)
    upward = dot("sd,df->sf", normed_two, up_w) + own_part(up_bias, 1024)
    share = 0.5 * (1.0 + lax.erf(upward * (0.5**0.5)))
    activated = (upward * share).astype(BF)
    slope = share + upward * (jnp.exp(-0.5 * upward * upward) * (0.5 / jnp.pi) ** 0.5)

    grad_up = (dot("se,ef->sf", down_all, down_w) * slope).astype(BF)
    norm_two_part = dot("sf,df->sd", grad_up, up_w).reshape(2, 4, rows, width)
    kept_two, sent_two = collect_near(norm_two_part)
    grad_norm_two = collect_far(kept_two, sent_two)
    up_grad = dot("sd,sf->df", normed_two, grad_up).astype(BF)
    down_grad = dot("se,sf->ef", down_all, activated).astype(BF)
    up_grad, down_grad = after(up_grad, sent_two), after(down_grad, sent_two)
    mlp_a, mlp_b = mlp_scatter(
        up_grad.reshape(*weight_rows, -1), down_grad.reshape(*weight_rows, -1)
    )
    up_b_grad = jnp.sum(grad_up.astype(F32), axis=0, keepdims=True)
    down_b_grad = jnp.sum(grad_own, axis=(0, 1))[None]

    gain_two_grad = jnp.sum(grad_norm_two * unit_two, axis=(0, 1))[None]
    shift_two_grad = jnp.sum(grad_norm_two, axis=(0, 1))[None]
    grad_middle = grad_own + norm_back(grad_norm_two, unit_two, scale_two, norm2_gain[0])
    grad_att = grad_middle.astype(BF)
    out_b_grad = jnp.sum(grad_att.astype(F32), axis=(0, 1))[None]
    att_pieces = spread_rows(grad_att)

    down_part = dot("sf,ef->se", activated, down_w).reshape(2, 4, rows, width)
    down_part = after(down_part, att_pieces[3])
    block_out = (
        (middle_own + (collect_far(*collect_near(down_part)) + down_bias[0])) * live
    ).astype(BF)[:, None]

    grads, att_all, sent, kept, vector = whole_call(
        back_body,
        (
            *att_pieces,
            joined,
            qk_w,
            values_w,
            out_w,
            hidden,
            gain_two_grad,
            shift_two_grad,
            out_b_grad,
            down_b_grad,
            up_b_grad,
        ),
        [
            shaped(count, 768),
            shaped(count, width),
            shaped(2, 2, rows, width),
            shaped(2, 2, rows, width, kind=F32),
            shaped(32, 512, kind=F32),
        ],
        56,
        flops=3 * 512 * 1024 * 1024,
    )
    qkv_grad, out_grad, up_grad, down_grad, vector = att_scatter(
        normed, grads, att_all, mixed, vector, mlp_a, mlp_b
    )
    near = swap(sent, 1)
    grad_norm_one = collect_far(*near_total(kept[:, 0], kept[:, 1], near))
    unit_own, scale_own = normalize(own_tokens.astype(F32))
    input_grad = grad_middle + norm_back(grad_norm_one, unit_own, scale_own, norm1_gain[0])
    input_grad = input_grad.astype(BF)[:, None]

    vector = vector + swap(vector, 1) + swap(vector, 2) + swap(vector, 3)
    vector = vector[:24].reshape(1, -1)
    parts = [vector[:, k * width : (k + 1) * width] for k in range(8)]
    return (
        block_out,
        input_grad,
        jnp.transpose(qkv_grad, (1, 0, 2))[None],
        out_grad[None],
        up_grad[None],
        down_grad[None],
        *parts[:7],
        vector[:, 8 * width :],
        parts[7],
    )


def solution(mesh):
    rows = P(None, "fsdp", "tensor", None)
    matrix = P(None, "fsdp", "tensor")
    qkv = P(None, "fsdp", None, "tensor")
    return jax.shard_map(
        local,
        mesh=mesh,
        in_specs=(rows, P(None, "fsdp"), rows, qkv, matrix, matrix, matrix) + (P(),) * 9,
        out_specs=(rows, rows, qkv, matrix, matrix, matrix) + (P(),) * 9,
        check_vma=False,
    )
```

```python
import jax
import jax.numpy as jnp
from jax import lax
from jax.experimental import pallas as pl
from jax.experimental.pallas import tpu as pltpu
from jax.sharding import PartitionSpec as P

HEAD_DIM = 64
EPS_NORM = 1e-06
BF = jnp.bfloat16
F32 = jnp.float32

YH, ZN, XN = 2, 4, 4


def fsdp_perm(dx, dz, dy):
    pairs = []
    for source in range(YH * ZN * XN):
        yh, z, x = source // (ZN * XN), (source // XN) % ZN, source % XN
        target = (((yh + dy) % YH) * ZN + (z + dz) % ZN) * XN + (x + dx) % XN
        pairs.append((source, target))
    return pairs


def hop(array, axis, step):
    move = {"x": (step, 0, 0), "z": (0, step, 0), "y": (0, 0, step)}[axis]
    return lax.ppermute(array, "fsdp", fsdp_perm(*move))


def swap(array, mask):
    return lax.ppermute(array, "tensor", [(i, i ^ mask) for i in range(4)])


def here():
    index = lax.axis_index("fsdp")
    plane = ZN * XN
    return lax.div(index, plane), lax.rem(lax.div(index, XN), ZN), lax.rem(index, XN)


def turn(index, step):
    return lax.rem(index + step, 4)


def shaped(*shape, kind=BF):
    return jax.ShapeDtypeStruct(shape, kind)


def limit(mebibytes):
    return pltpu.CompilerParams(vmem_limit_bytes=mebibytes << 20)


VMEM = pl.BlockSpec(memory_space=pltpu.VMEM)
ANY = pl.BlockSpec(memory_space=pl.ANY)


def move(plan, arrays, shapes, count):
    def body(*refs):
        inputs, outputs, done = refs[: len(arrays)], refs[len(arrays) : -1], refs[-1]
        pairs = plan(inputs, outputs)
        copies = [
            pltpu.make_async_copy(source, target, done.at[spot])
            for spot, (source, target) in enumerate(pairs)
        ]
        for copy in copies:
            copy.start()
        for copy in copies:
            copy.wait()

    size = sum(item.size * 2 for item in shapes)
    return pl.pallas_call(
        body,
        out_shape=shapes,
        in_specs=[ANY] * len(arrays),
        out_specs=[VMEM] * len(shapes),
        scratch_shapes=[pltpu.SemaphoreType.DMA((count,))],
        compiler_params=limit(16),
        cost_estimate=pl.CostEstimate(flops=0, bytes_accessed=2 * size, transcendentals=0),
    )(*arrays)


def whole_call(body, arrays, shapes, mebibytes, scratch=(), cost=None):
    size = sum(item.size * item.dtype.itemsize for item in list(shapes) + list(arrays))
    cost = cost or pl.CostEstimate(flops=0, bytes_accessed=size, transcendentals=0)
    return pl.pallas_call(
        body,
        out_shape=shapes,
        scratch_shapes=scratch,
        compiler_params=limit(mebibytes),
        cost_estimate=cost,
    )(*arrays)


def after(value, *others):
    return lax.optimization_barrier((value,) + others)[0]


def near_gather(block_a, axis_a, block_b, axis_b):
    right_a, right_b = hop(block_a, axis_a, -1), hop(block_b, axis_b, -1)
    left_a, left_b = hop(block_a, axis_a, 1), hop(block_b, axis_b, 1)
    late_a, late_b = lax.optimization_barrier(
        (block_a, block_b, right_a, right_b, left_a, left_b)
    )[:2]
    far_a, far_b = hop(late_a, axis_a, 2), hop(late_b, axis_b, 2)
    return [block_a, right_a, far_a, left_a], [block_b, right_b, far_b, left_b]


def wide_gather(block, first, axis):
    right, left = hop(block, axis, -1), hop(block, axis, 1)
    far = hop(first, axis, 2)
    low, high = hop(left[0, :, :, 512:], axis, 1), hop(right[1, :, :, 512:], axis, -1)
    return (block, right, left, far), (block, right, left, low, high)


def pack_plan(inputs, outputs):
    qkv, out, up, down = inputs
    own = outputs[0]
    return [
        (qkv.at[0], own.at[:, 0:256]),
        (qkv.at[1], own.at[:, 256:512]),
        (up, own.at[:, 512:1536]),
        (qkv.at[2], own.at[:, 1536:1792]),
        (out, own.at[:, 1792:2048]),
        (down, own.at[:, 2048:3072]),
    ]


def pair_body(own, other, part_a, part_b):
    yh, _, _ = here()
    part_a[yh] = own[:, :1536]
    part_b[yh] = own[:, 1536:]
    part_a[1 - yh] = other[:, :1536]
    part_b[1 - yh] = other[:, 1536:]


def first_plan(inputs, outputs):
    _, z, x = here()
    all_a, all_b, att_a, att_b = outputs
    pairs = []
    for step in range(4):
        piece_a, piece_b = inputs[step], inputs[4 + step]
        pairs.append((piece_a, all_a.at[:, turn(x, step)]))
        pairs.append((piece_b, all_b.at[:, turn(z, step)]))
        pairs.append((piece_a.at[:, :, 0:512], att_a.at[:, turn(x, step)]))
        pairs.append((piece_b.at[:, :, 0:512], att_b.at[:, turn(z, step)]))
    return pairs


def att_plan(inputs, outputs):
    _, z, x = here()
    qk_w, values_w, out_w = outputs
    pairs = []
    for spot, step in enumerate((0, 1, 3, 2)):
        piece_a, piece_b = inputs[spot], inputs[4 + spot]
        pairs.append((piece_a.at[:, :, :, 0:512], qk_w.at[:, turn(z, step)]))
        pairs.append((piece_b.at[:, :, :, 0:256], values_w.at[:, :, turn(x, step)]))
        pairs.append((piece_b.at[:, :, :, 256:512], out_w.at[:, :, turn(x, step)]))
    return pairs


def mlp_plan(inputs, outputs):
    _, z, x = here()
    up_w, down_w = outputs
    pairs = []
    for spot, step in enumerate((0, 1, 3)):
        pairs.append((inputs[spot].at[:, :, :, 512:1536], up_w.at[:, turn(z, step)]))
        pairs.append((inputs[5 + spot].at[:, :, :, 512:1536], down_w.at[:, :, turn(x, step)]))
    for half in range(2):
        pairs.append((inputs[3 + half], up_w.at[half, turn(z, 2)]))
        pairs.append((inputs[8 + half], down_w.at[half, :, turn(x, 2)]))
    return pairs


def far_plan(inputs, outputs):
    _, z, x = here()
    grad_a, grad_b = inputs
    pairs = []
    for half in range(2):
        pairs.append((grad_a.at[half, turn(z, 2)], outputs[half]))
        pairs.append((grad_b.at[half, :, turn(x, 2)], outputs[2 + half]))
    return pairs


def fetch(pairs, done):
    copies = [
        pltpu.make_async_copy(source, target, done.at[spot])
        for spot, (source, target) in enumerate(pairs)
    ]
    for copy in copies:
        copy.start()
    for copy in copies:
        copy.wait()


def pass_body(grad_a, grad_b, low_a, high_a, low_b, high_b, ra, la, rb, lb, held, done):
    _, z, x = here()
    fetch(
        [
            (grad_a.at[:, turn(z, 1)], held.at[0]),
            (grad_a.at[:, turn(z, 3)], held.at[1]),
            (grad_b.at[:, :, turn(x, 1)], held.at[2]),
            (grad_b.at[:, :, turn(x, 3)], held.at[3]),
        ],
        done,
    )
    for spot, (right, left, low, high) in enumerate(
        ((ra, la, low_a, high_a), (rb, lb, low_b, high_b))
    ):
        right[0] = add(held[2 * spot, 0], low[...])
        right[1] = held[2 * spot, 1]
        left[0] = held[2 * spot + 1, 0]
        left[1] = add(held[2 * spot + 1, 1], high[...])


def rest_body(grad_a, grad_b, la, ra, lb, rb, total_a, total_b, held, done):
    _, z, x = here()
    fetch(
        [(grad_a.at[:, turn(z, 0)], held.at[0]), (grad_b.at[:, :, turn(x, 0)], held.at[1])],
        done,
    )
    total_a[...] = add(held[0], la[...], ra[...])
    total_b[...] = add(held[1], lb[...], rb[...])


def held_call(body, whole, arrays, shapes, slots, block, mebibytes):
    size = sum(item.size * 2 for item in shapes) + sum(item.size * 2 for item in arrays)
    return pl.pallas_call(
        body,
        out_shape=shapes,
        in_specs=[ANY] * len(whole) + [VMEM] * len(arrays),
        out_specs=[VMEM] * len(shapes),
        scratch_shapes=[pltpu.VMEM((slots,) + block, BF), pltpu.SemaphoreType.DMA((slots,))],
        compiler_params=limit(mebibytes),
        cost_estimate=pl.CostEstimate(flops=0, bytes_accessed=2 * size, transcendentals=0),
    )(*whole, *arrays)


def mlp_scatter(grad_a, grad_b):
    block = (2, 4, 32, 1024)
    half = shaped(4, 32, 1024)
    low_a, high_a, low_b, high_b = move(far_plan, (grad_a, grad_b), [half] * 4, 4)
    recv = (hop(low_a, "z", 1), hop(high_a, "z", -1), hop(low_b, "x", 1), hop(high_b, "x", -1))
    ra, la, rb, lb = held_call(
        pass_body, (grad_a, grad_b), recv, [shaped(*block)] * 4, 4, block, 40
    )
    recv = (hop(ra, "z", 1), hop(la, "z", -1), hop(rb, "x", 1), hop(lb, "x", -1))
    return held_call(rest_body, (grad_a, grad_b), recv, [shaped(*block)] * 2, 2, block, 40)


def add(*terms):
    total = terms[0].astype(F32)
    for term in terms[1:]:
        total = total + term.astype(F32)
    return total.astype(BF)


def contract(left, right, dims):
    return lax.dot_general(left, right, (dims, ((), ())), preferred_element_type=F32)


ROWS = ((1,), (0,))
BOTH = ((1,), (1,))
TOPS = ((0,), (0,))
SCALE = HEAD_DIM ** (-0.5)


def probabilities(query, keys):
    scores = contract(query, keys, BOTH) * SCALE
    weight = jnp.exp(scores - jnp.max(scores, axis=-1, keepdims=True))
    return weight / jnp.sum(weight, axis=-1, keepdims=True)


def att_body(normed, qk_w, values_w, out_w, query_b, value_b, joined, mixed, sent, kept):
    spot = pl.ds(pl.multiple_of(lax.axis_index("tensor") * 256, 256), 256)
    rows = normed[...]
    mixer = out_w[...].reshape(1024, 256)
    pair = contract(rows, qk_w[...].reshape(1024, 512), ROWS)
    joined[:, 0:256] = (pair[:, 0:256] + query_b[:, spot]).astype(BF)
    joined[:, 256:512] = pair[:, 256:].astype(BF)
    last = contract(rows, values_w[...].reshape(1024, 256), ROWS)
    joined[:, 512:768] = (last + value_b[:, spot]).astype(BF)
    for image in range(2):
        line = slice(image * 256, image * 256 + 256)
        parts = []
        for head in range(4):
            query, keys, values = (
                joined[line, base + head * 64 : base + head * 64 + 64] for base in (0, 256, 512)
            )
            probs = probabilities(query, keys).astype(BF)
            parts.append(contract(probs, values, ROWS).astype(BF))
        whole = jnp.concatenate(parts, axis=1)
        mixed[line, :] = whole
        split_blocks(image, contract(whole, mixer, BOTH), sent, kept)


def split_blocks(image, part, sent, kept):
    for spot in range(2):
        kept[image, spot] = part[spot * 64 : spot * 64 + 64]
        sent[image, spot] = part[128 + spot * 64 : 192 + spot * 64].astype(BF)


def middle_body(half, came, own, across, out_b, gain, shift, normed, middle):
    for image in range(2):
        for spot, piece in enumerate((own, across)):
            total = half[image, spot].astype(F32) + came[image, 1 - spot].astype(F32)
            value = piece[image].astype(F32) + (total + out_b[...])
            middle[image, spot] = value
            unit, _ = normalize(value)
            normed[image, spot] = (unit * gain[...] + shift[...]).astype(BF)


def middle_back_body(
    half, came, own, across, middle, gain, att, grad, gain_grad, shift_grad, out_b_grad
):
    sums = [jnp.zeros((1, 1024), F32) for _ in range(3)]
    for image in range(2):
        for spot, piece in enumerate((own, across)):
            total = half[image, spot].astype(F32) + came[image, 1 - spot].astype(F32)
            unit, scale = normalize(middle[image, spot])
            value = piece[image].astype(F32) + norm_back(total, unit, scale, gain[...])
            low = value.astype(BF)
            att[image, spot] = low
            if spot == 0:
                grad[image] = value
                for place, item in enumerate((total * unit, total, low.astype(F32))):
                    sums[place] = sums[place] + jnp.sum(item, axis=0, keepdims=True)
    gain_grad[...], shift_grad[...], out_b_grad[...] = sums


def collect_far(kept, sent):
    return kept + swap(sent, 2).astype(F32)


def normalize(values):
    center = values - jnp.mean(values, axis=-1, keepdims=True)
    scale = lax.rsqrt(jnp.mean(center * center, axis=-1, keepdims=True) + EPS_NORM)
    return center * scale, scale


def norm_back(grad, unit, scale, gain):
    inner = grad * gain
    first = jnp.mean(inner, axis=-1, keepdims=True)
    second = jnp.mean(inner * unit, axis=-1, keepdims=True)
    return scale * (inner - first - unit * second)


def back_body(
    pair, beside, normed, mixed, joined, qk_w, values_w, out_w, hidden, gain_two, shift_two,
    out_b, down_b, up_b, sent, kept, vector, *rest,
):
    sends_a, sends_b, own_a, own_b = rest[0:3], rest[3:6], rest[6], rest[7]
    grads, att, grad_a, grad_b, low, done = rest[8:]
    tensor = lax.axis_index("tensor")
    for image in range(2):
        for spot, piece in enumerate((pair, beside)):
            first = image * 256 + spot * 128
            att[first : first + 128, :] = piece[image].reshape(128, 1024)
    pair_w = qk_w[...].reshape(1024, 512)
    last_w = values_w[...].reshape(1024, 256)
    mixer = out_w[...].reshape(1024, 256)
    gain = jnp.zeros((1, 1024), F32)
    shift = jnp.zeros((1, 1024), F32)
    for image in range(2):
        line = slice(image * 256, image * 256 + 256)
        grad_mixed = contract(att[line, :], mixer, ROWS).astype(BF)
        parts = ([], [], [])
        for head in range(4):
            query, keys, values = (
                joined[line, base + head * 64 : base + head * 64 + 64] for base in (0, 256, 512)
            )
            grad = grad_mixed[:, head * 64 : head * 64 + 64]
            probs = probabilities(query, keys)
            grad_prob = contract(grad, values, BOTH)
            inner = jnp.sum(grad_prob * probs, axis=-1, keepdims=True)
            score = (probs * (grad_prob - inner)).astype(BF)
            parts[0].append((contract(score, keys, ROWS) * SCALE).astype(BF))
            parts[1].append((contract(score, query, TOPS) * SCALE).astype(BF))
            parts[2].append(contract(probs.astype(BF), grad, TOPS).astype(BF))
        for kind in range(3):
            grads[line, kind * 256 : kind * 256 + 256] = jnp.concatenate(parts[kind], axis=1)
        norm_grad = contract(grads[line, :512], pair_w, BOTH) + contract(
            grads[line, 512:], last_w, BOTH
        )
        unit, _ = normalize(hidden[line, :].astype(F32))
        gain = gain + jnp.sum(norm_grad * unit, axis=0, keepdims=True)
        shift = shift + jnp.sum(norm_grad, axis=0, keepdims=True)
        split_blocks(image, norm_grad, sent, kept)
    vector[...] = jnp.zeros(vector.shape, F32)
    rows = (
        (0, gain), (2, shift), (8, out_b[...]), (10, gain_two[...]), (12, shift_two[...]),
        (14, down_b[...]),
    )
    for row, value in rows:
        vector[row : row + 1, :] = value[:, :512]
        vector[row + 1 : row + 2, :] = value[:, 512:]
    spot = pl.ds(pl.multiple_of(lax.rem(tensor, 2) * 256, 256), 256)
    for row, base in ((4, 0), (6, 512)):
        part = jnp.sum(grads[:, base : base + 256].astype(F32), axis=0, keepdims=True)
        vector[pl.ds(row + lax.div(tensor, 2), 1), spot] = part
    vector[pl.ds(16 + 2 * tensor, 1), :] = up_b[:, :512]
    vector[pl.ds(17 + 2 * tensor, 1), :] = up_b[:, 512:]
    _, z, x = here()
    grad_a[...] = contract(normed[...], grads[:, 0:512], TOPS).astype(BF).reshape(grad_a.shape)
    pairs = [(grad_a.at[:, turn(z, 0)], own_a)]
    low[...] = vector[...].astype(BF)
    for step in range(1, 4):
        target = sends_a[step - 1]
        for half in range(2):
            pairs.append((grad_a.at[half, turn(z, step)], target.at[pl.ds(4 * half, 4)]))
        pairs.append((low, target.at[8]))
    copies = [
        pltpu.make_async_copy(source, target, done.at[spot])
        for spot, (source, target) in enumerate(pairs)
    ]
    for copy in copies:
        copy.start()
    last = contract(normed[...], grads[:, 512:768], TOPS).astype(BF)
    grad_b[:, :, :, :, 0:256] = last.reshape(2, 4, 4, 32, 256)
    last = contract(att[...], mixed[...], TOPS).astype(BF)
    grad_b[:, :, :, :, 256:512] = last.reshape(2, 4, 4, 32, 256)
    others = [(grad_b.at[:, :, turn(x, 0)], own_b)]
    for step in range(1, 4):
        others.append((grad_b.at[:, :, turn(x, step)], sends_b[step - 1]))
    more = [
        pltpu.make_async_copy(source, target, done.at[len(pairs) + spot])
        for spot, (source, target) in enumerate(others)
    ]
    for copy in more:
        copy.start()
    for copy in copies + more:
        copy.wait()


def second_body(*refs):
    a1, a2, a3, own_a, b1, b2, b3, own_b, vector, mlp_a, mlp_b = refs[:11]
    outs_a, outs_b, sum_a, sum_b = refs[11:15], refs[15:19], refs[19], refs[20]
    _, z, x = here()
    for yh in range(2):
        part = slice(4 * yh, 4 * yh + 4)
        sum_a[yh] = add(own_a[yh], a1[part], a2[part], a3[part])
        sum_b[yh] = add(own_b[yh], b1[yh], b2[yh], b3[yh])
    low = add(vector[...], a1[8], a2[8], a3[8])
    for step in range(4):
        for out, total, mlp, index in (
            (outs_a[step], sum_a, mlp_a, turn(x, step)),
            (outs_b[step], sum_b, mlp_b, turn(z, step)),
        ):
            for yh in range(2):
                out[yh] = total[yh, index]
                out[2 + yh] = mlp[yh, index, :, 0:512]
                out[4 + yh] = mlp[yh, index, :, 512:1024]
        outs_a[step][6] = low


def third_body(a0, a1, a2, a3, b0, b1, b2, b3, send, own):
    yh, _, _ = here()
    for spot in range(3):
        for base, pieces in ((0, (a0, a1, a2, a3)), (3, (b0, b1, b2, b3))):
            mine = [piece[2 * spot + yh].astype(F32) for piece in pieces]
            other = [piece[2 * spot + 1 - yh].astype(F32) for piece in pieces]
            own[base + spot] = (mine[0] + mine[1]) + (mine[2] + mine[3])
            send[base + spot] = ((other[0] + other[1]) + (other[2] + other[3])).astype(BF)
    total = [piece[6].astype(F32) for piece in (a0, a1, a2, a3)]
    total = (total[0] + total[1]) + (total[2] + total[3])
    own[6] = total
    send[6] = total.astype(BF)


def last_body(own, came, qkv, out, up, down, vector):
    def total(spot):
        return own[spot] + came[spot].astype(F32)

    att_a, att_b = total(0), total(3)
    qkv[0] = att_a[:, 0:256]
    qkv[1] = att_a[:, 256:512]
    qkv[2] = att_b[:, 0:256]
    out[...] = att_b[:, 256:512]
    up[:, 0:512] = total(1)
    up[:, 512:1024] = total(2)
    down[:, 0:512] = total(4)
    down[:, 512:1024] = total(5)
    vector[...] = total(6)


def att_scatter(arrays, mlp_a, mlp_b, wait):
    block = (2, 4, 32, 512)
    shapes = [
        shaped(2, 2, 64, 1024),
        shaped(2, 2, 64, 1024, kind=F32),
        shaped(32, 512, kind=F32),
    ]
    shapes += [shaped(9, 32, 512)] * 3 + [shaped(*block)] * 5
    sent, kept, vector, *results = pl.pallas_call(
        back_body,
        out_shape=shapes,
        in_specs=[VMEM] * len(arrays),
        out_specs=[VMEM] * 3 + [ANY] * 8,
        scratch_shapes=[
            pltpu.VMEM((512, 768), BF),
            pltpu.VMEM((512, 1024), BF),
            pltpu.VMEM((2, 4, 4, 32, 512), BF),
            pltpu.VMEM((2, 4, 4, 32, 512), BF),
            pltpu.VMEM((32, 512), BF),
            pltpu.SemaphoreType.DMA((14,)),
        ],
        compiler_params=limit(56),
    )(*arrays)
    near = swap(sent, 1)
    kept_one = kept[:, 0] + near[:, 0].astype(F32)
    came_one = swap((kept[:, 1] + near[:, 1].astype(F32)).astype(BF), 2)
    grad_norm_one = kept_one + came_one.astype(F32)
    came_a = [hop(results[step - 1], "z", step) for step in (1, 2, 3)]
    came_b = [hop(results[2 + step], "x", step) for step in (1, 2, 3)]
    pieces = whole_call(
        second_body,
        (*came_a, results[6], *came_b, results[7], vector, mlp_a, mlp_b),
        [shaped(7, 32, 512)] * 4 + [shaped(6, 32, 512)] * 4,
        40,
        scratch=[pltpu.VMEM(block, BF), pltpu.VMEM(block, BF)],
    )
    came_a = [hop(pieces[step], "x", step) for step in (1, 2, 3)]
    came_b = [hop(pieces[4 + step], "z", step) for step in (1, 2, 3)]
    send, own = whole_call(
        third_body,
        (pieces[0], *came_a, pieces[4], *came_b),
        [shaped(7, 32, 512), shaped(7, 32, 512, kind=F32)],
        40,
    )
    send = after(send, came_one, wait)
    shapes = [(3, 32, 256), (32, 256), (32, 1024), (32, 1024), (32, 512)]
    results = whole_call(
        last_body, (own, hop(send, "y", 1)), [shaped(*shape, kind=F32) for shape in shapes], 40
    )
    return grad_norm_one, *results


def dot(spec, left, right):
    return jnp.einsum(spec, left, right, preferred_element_type=F32)


def local(
    tokens,
    dealt,
    cotangent,
    qkv_weight,
    out_weight,
    up_weight,
    down_weight,
    norm1_gain,
    norm1_bias,
    query_bias,
    value_bias,
    out_bias,
    norm2_gain,
    norm2_bias,
    up_bias,
    down_bias,
):
    tensor = lax.axis_index("tensor")
    rows = tokens.shape[2]
    width = tokens.shape[3]
    count = 8 * rows
    weight_rows = (YH, ZN, XN, 32)

    def own_part(vector, size):
        return lax.dynamic_slice_in_dim(vector[0], tensor * size, size, 0)

    (own,) = move(
        pack_plan,
        (jnp.transpose(qkv_weight[0], (1, 0, 2)), out_weight[0], up_weight[0], down_weight[0]),
        [shaped(32, 3072)],
        6,
    )
    other = hop(own, "y", 1)
    part_a, part_b = whole_call(pair_body, (own, other), [shaped(2, 32, 1536)] * 2, 16)
    pieces_a, pieces_b = near_gather(part_a, "x", part_b, "z")
    shapes = [shaped(2, 4, 32, 1536)] * 2 + [shaped(2, 4, 32, 512)] * 2
    all_a, all_b, att_a, att_b = move(first_plan, pieces_a + pieces_b, shapes, 16)
    att_a, mlp_a = wide_gather(all_a, att_a, "z")
    att_b, mlp_b = wide_gather(all_b, att_b, "x")
    shapes = [shaped(*weight_rows, 512), shaped(*weight_rows, 256), shaped(*weight_rows, 256)]
    qk_w, values_w, out_w = move(att_plan, att_a + att_b, shapes, 12)
    up_w, down_w = move(mlp_plan, mlp_a + mlp_b, [shaped(*weight_rows, 1024)] * 2, 10)
    up_w, down_w = up_w.reshape(width, -1), down_w.reshape(width, -1)

    live = dealt.astype(F32).reshape(2, 1, 1)
    own_tokens = tokens[:, 0]
    grad_own = cotangent[:, 0].astype(F32) * live
    across = swap(own_tokens, 2)
    pair = jnp.stack([own_tokens, across], axis=1)
    hidden = jnp.stack([pair, swap(pair, 1)], axis=1).reshape(count, width)
    grad_low = after(
        grad_own.astype(BF), pieces_a[1], pieces_b[1], pieces_a[3], pieces_b[3]
    )
    grad_across = swap(grad_low, 2)
    grad_pair = jnp.stack([grad_low, grad_across], axis=1)
    grad_beside = swap(grad_pair, 1)
    hidden = after(hidden, grad_beside)
    down_all = jnp.stack([grad_pair, grad_beside]).reshape(count, width)
    unit_one, _ = normalize(hidden.astype(F32))
    normed = (unit_one * norm1_gain[0] + norm1_bias[0]).astype(BF)
    quarter = (2, 2, rows, width)
    joined, mixed, sent, kept = whole_call(
        att_body,
        (normed, qk_w, values_w, out_w, query_bias, value_bias),
        [shaped(count, 768), shaped(count, 256), shaped(*quarter), shaped(*quarter, kind=F32)],
        48,
    )
    half = (kept + swap(sent, 1).astype(F32)).astype(BF)
    normed_pair, middle = whole_call(
        middle_body,
        (half, swap(half, 2), own_tokens, across, out_bias, norm2_gain, norm2_bias),
        [shaped(*quarter), shaped(*quarter, kind=F32)],
        32,
    )
    normed_two = jnp.stack([normed_pair, swap(normed_pair, 1)]).reshape(count, width)
    upward = dot("sd,df->sf", normed_two, up_w) + own_part(up_bias, 1024)
    share = 0.5 * (1.0 + lax.erf(upward * (0.5**0.5)))
    activated = (upward * share).astype(BF)
    slope = share + upward * (jnp.exp(-0.5 * upward * upward) * (0.5 / jnp.pi) ** 0.5)

    grad_up = (dot("se,ef->sf", down_all, down_w) * slope).astype(BF)
    norm_two_part = dot("sf,df->sd", grad_up, up_w).reshape(2, *quarter)
    half = (norm_two_part[0] + swap(norm_two_part[1].astype(BF), 1).astype(F32)).astype(BF)
    up_grad = dot("sd,sf->df", normed_two, grad_up).astype(BF)
    down_grad = dot("se,sf->ef", down_all, activated).astype(BF)
    up_grad, down_grad = lax.optimization_barrier((up_grad, down_grad, half))[:2]
    mlp_a, mlp_b = mlp_scatter(
        up_grad.reshape(*weight_rows, -1), down_grad.reshape(*weight_rows, -1)
    )
    up_b_grad = jnp.sum(grad_up.astype(F32), axis=0, keepdims=True)
    down_b_grad = jnp.sum(grad_own, axis=(0, 1))[None]

    att_pair, grad_middle, gain_two_grad, shift_two_grad, out_b_grad = whole_call(
        middle_back_body,
        (half, swap(half, 2), grad_low, grad_across, middle, norm2_gain),
        [shaped(*quarter), shaped(2, rows, width, kind=F32)] + [shaped(1, width, kind=F32)] * 3,
        32,
    )
    att_beside = swap(att_pair, 1)

    down_part = dot("sf,ef->se", activated, down_w).reshape(2, *quarter)
    near = swap(after(down_part[1].astype(BF), att_beside), 1)
    down_sent = (down_part[0][:, 1] + near[:, 1].astype(F32)).astype(BF)
    down_came = swap(down_sent, 2)
    down_total = down_part[0][:, 0] + near[:, 0].astype(F32) + down_came.astype(F32)
    block_out = ((middle[:, 0] + (down_total + down_bias[0])) * live).astype(BF)[:, None]

    arrays = (
        att_pair,
        att_beside,
        normed,
        mixed,
        joined,
        qk_w,
        values_w,
        out_w,
        hidden,
        gain_two_grad,
        shift_two_grad,
        out_b_grad,
        down_b_grad,
        up_b_grad,
    )
    grad_norm_one, qkv_grad, out_grad, up_grad, down_grad, vector = att_scatter(
        arrays, mlp_a, mlp_b, down_came
    )
    unit_own, scale_own = normalize(own_tokens.astype(F32))
    input_grad = grad_middle + norm_back(grad_norm_one, unit_own, scale_own, norm1_gain[0])
    input_grad = input_grad.astype(BF)[:, None]

    vector = vector + swap(vector, 1) + swap(vector, 2) + swap(vector, 3)
    vector = vector[:24].reshape(1, -1)
    parts = [vector[:, k * width : (k + 1) * width] for k in range(8)]
    return (
        block_out,
        input_grad,
        jnp.transpose(qkv_grad, (1, 0, 2))[None],
        out_grad[None],
        up_grad[None],
        down_grad[None],
        *parts[:7],
        vector[:, 8 * width :],
        parts[7],
    )


def solution(mesh):
    rows = P(None, "fsdp", "tensor", None)
    matrix = P(None, "fsdp", "tensor")
    qkv = P(None, "fsdp", None, "tensor")
    return jax.shard_map(
        local,
        mesh=mesh,
        in_specs=(rows, P(None, "fsdp"), rows, qkv, matrix, matrix, matrix) + (P(),) * 9,
        out_specs=(rows, rows, qkv, matrix, matrix, matrix) + (P(),) * 9,
        check_vma=False,
    )
```

```python
import jax
import jax.numpy as jnp
from jax import lax
from jax.experimental import pallas as pl
from jax.experimental.pallas import tpu as pltpu
from jax.sharding import PartitionSpec as P

HEAD_DIM = 64
EPS_NORM = 1e-06
BF = jnp.bfloat16
F32 = jnp.float32

YH, ZN, XN = 2, 4, 4


def fsdp_perm(dx, dz, dy):
    pairs = []
    for source in range(YH * ZN * XN):
        yh, z, x = source // (ZN * XN), (source // XN) % ZN, source % XN
        target = (((yh + dy) % YH) * ZN + (z + dz) % ZN) * XN + (x + dx) % XN
        pairs.append((source, target))
    return pairs


def hop(array, axis, step):
    move = {"x": (step, 0, 0), "z": (0, step, 0), "y": (0, 0, step)}[axis]
    return lax.ppermute(array, "fsdp", fsdp_perm(*move))


def swap(array, mask):
    return lax.ppermute(array, "tensor", [(i, i ^ mask) for i in range(4)])


def here():
    index = lax.axis_index("fsdp")
    plane = ZN * XN
    return lax.div(index, plane), lax.rem(lax.div(index, XN), ZN), lax.rem(index, XN)


def turn(index, step):
    return lax.rem(index + step, 4)


def shaped(*shape, kind=BF):
    return jax.ShapeDtypeStruct(shape, kind)


def limit(mebibytes):
    return pltpu.CompilerParams(vmem_limit_bytes=mebibytes << 20)


VMEM = pl.BlockSpec(memory_space=pltpu.VMEM)
ANY = pl.BlockSpec(memory_space=pl.ANY)


def move(plan, arrays, shapes, count):
    def body(*refs):
        inputs, outputs, done = refs[: len(arrays)], refs[len(arrays) : -1], refs[-1]
        pairs = plan(inputs, outputs)
        copies = [
            pltpu.make_async_copy(source, target, done.at[spot])
            for spot, (source, target) in enumerate(pairs)
        ]
        for copy in copies:
            copy.start()
        for copy in copies:
            copy.wait()

    size = sum(item.size * 2 for item in shapes)
    return pl.pallas_call(
        body,
        out_shape=shapes,
        in_specs=[ANY] * len(arrays),
        out_specs=[VMEM] * len(shapes),
        scratch_shapes=[pltpu.SemaphoreType.DMA((count,))],
        compiler_params=limit(16),
        cost_estimate=pl.CostEstimate(flops=0, bytes_accessed=2 * size, transcendentals=0),
    )(*arrays)


def whole_call(body, arrays, shapes, mebibytes, scratch=(), cost=None):
    size = sum(item.size * item.dtype.itemsize for item in list(shapes) + list(arrays))
    cost = cost or pl.CostEstimate(flops=0, bytes_accessed=size, transcendentals=0)
    return pl.pallas_call(
        body,
        out_shape=shapes,
        scratch_shapes=scratch,
        compiler_params=limit(mebibytes),
        cost_estimate=cost,
    )(*arrays)


def after(value, *others):
    return lax.optimization_barrier((value,) + others)[0]


def near_gather(block_a, axis_a, block_b, axis_b):
    right_a, right_b = hop(block_a, axis_a, -1), hop(block_b, axis_b, -1)
    left_a, left_b = hop(block_a, axis_a, 1), hop(block_b, axis_b, 1)
    late_a, late_b = lax.optimization_barrier(
        (block_a, block_b, right_a, right_b, left_a, left_b)
    )[:2]
    far_a, far_b = hop(late_a, axis_a, 2), hop(late_b, axis_b, 2)
    return [block_a, right_a, far_a, left_a], [block_b, right_b, far_b, left_b]


def ring_gather(block, axis):
    right, left = hop(block, axis, -1), hop(block, axis, 1)
    low, high = hop(left[0], axis, 1), hop(right[1], axis, -1)
    return [block, right, left, low, high]


def near_scatter(right_a, far_a, left_a, axis_a, right_b, far_b, left_b, axis_b):
    came = [
        hop(right_a, axis_a, 1), hop(right_b, axis_b, 1),
        hop(left_a, axis_a, -1), hop(left_b, axis_b, -1),
    ]
    far_a, far_b = lax.optimization_barrier((far_a, far_b, *came))[:2]
    far_a, far_b = hop(far_a, axis_a, 2), hop(far_b, axis_b, 2)
    return (came[0], far_a, came[2]), (came[1], far_b, came[3])


def pack_plan(inputs, outputs):
    qkv, out, up, down = inputs
    own = outputs[0]
    return [
        (qkv.at[0], own.at[:, 0:256]),
        (qkv.at[1], own.at[:, 256:512]),
        (up, own.at[:, 512:1536]),
        (qkv.at[2], own.at[:, 1536:1792]),
        (out, own.at[:, 1792:2048]),
        (down, own.at[:, 2048:3072]),
    ]


def pair_body(own, other, part_a, part_b):
    yh, _, _ = here()
    part_a[yh] = own[:, :1536]
    part_b[yh] = own[:, 1536:]
    part_a[1 - yh] = other[:, :1536]
    part_b[1 - yh] = other[:, 1536:]


def first_plan(inputs, outputs):
    _, z, x = here()
    all_a, all_b = outputs
    pairs = []
    for step in range(4):
        pairs.append((inputs[step], all_a.at[:, turn(x, step)]))
        pairs.append((inputs[4 + step], all_b.at[:, turn(z, step)]))
    return pairs


def cut_plan(first, last, axis, inputs, target):
    _, z, x = here()
    columns = slice(first, last)

    def spot(step, half):
        if axis == "z":
            return target.at[half, turn(z, step)]
        return target.at[half, :, turn(x, step)]

    whole = slice(0, 2)
    pairs = []
    for piece, step in zip(inputs[:3], (0, 1, 3)):
        pairs.append((piece.at[:, :, :, columns], spot(step, whole)))
    for half in range(2):
        pairs.append((inputs[3 + half].at[:, :, columns], spot(2, half)))
    return pairs


def att_plan(inputs, outputs):
    qk_w, values_w, out_w = outputs
    return (
        cut_plan(0, 512, "z", inputs[:5], qk_w)
        + cut_plan(0, 256, "x", inputs[5:], values_w)
        + cut_plan(256, 512, "x", inputs[5:], out_w)
    )


def mlp_plan(inputs, outputs):
    up_w, down_w = outputs
    return cut_plan(512, 1536, "z", inputs[:5], up_w) + cut_plan(
        512, 1536, "x", inputs[5:], down_w
    )


def far_plan(inputs, outputs):
    _, z, x = here()
    grad_a, grad_b = inputs
    pairs = []
    for half in range(2):
        pairs.append((grad_a.at[half, turn(z, 2)], outputs[half]))
        pairs.append((grad_b.at[half, :, turn(x, 2)], outputs[2 + half]))
    return pairs


def fetch(pairs, done):
    copies = [
        pltpu.make_async_copy(source, target, done.at[spot])
        for spot, (source, target) in enumerate(pairs)
    ]
    for copy in copies:
        copy.start()
    for copy in copies:
        copy.wait()


def pass_body(grad_a, grad_b, low_a, high_a, low_b, high_b, ra, la, rb, lb, held, done):
    _, z, x = here()
    fetch(
        [
            (grad_a.at[:, turn(z, 1)], held.at[0]),
            (grad_a.at[:, turn(z, 3)], held.at[1]),
            (grad_b.at[:, :, turn(x, 1)], held.at[2]),
            (grad_b.at[:, :, turn(x, 3)], held.at[3]),
        ],
        done,
    )
    for spot, (right, left, low, high) in enumerate(
        ((ra, la, low_a, high_a), (rb, lb, low_b, high_b))
    ):
        right[0] = add(held[2 * spot, 0], low[...])
        right[1] = held[2 * spot, 1]
        left[0] = held[2 * spot + 1, 0]
        left[1] = add(held[2 * spot + 1, 1], high[...])


def rest_body(grad_a, grad_b, la, ra, lb, rb, total_a, total_b, held, done):
    _, z, x = here()
    fetch(
        [(grad_a.at[:, turn(z, 0)], held.at[0]), (grad_b.at[:, :, turn(x, 0)], held.at[1])],
        done,
    )
    total_a[...] = add(held[0], la[...], ra[...])
    total_b[...] = add(held[1], lb[...], rb[...])


def held_call(body, whole, arrays, shapes, slots, block, mebibytes):
    size = sum(item.size * 2 for item in shapes) + sum(item.size * 2 for item in arrays)
    return pl.pallas_call(
        body,
        out_shape=shapes,
        in_specs=[ANY] * len(whole) + [VMEM] * len(arrays),
        out_specs=[VMEM] * len(shapes),
        scratch_shapes=[pltpu.VMEM((slots,) + block, BF), pltpu.SemaphoreType.DMA((slots,))],
        compiler_params=limit(mebibytes),
        cost_estimate=pl.CostEstimate(flops=0, bytes_accessed=2 * size, transcendentals=0),
    )(*whole, *arrays)


def mlp_scatter(grad_a, grad_b):
    block = (2, 4, 32, 1024)
    half = shaped(4, 32, 1024)
    low_a, high_a, low_b, high_b = move(far_plan, (grad_a, grad_b), [half] * 4, 4)
    recv = (hop(low_a, "z", 1), hop(high_a, "z", -1), hop(low_b, "x", 1), hop(high_b, "x", -1))
    ra, la, rb, lb = held_call(
        pass_body, (grad_a, grad_b), recv, [shaped(*block)] * 4, 4, block, 40
    )
    return ra, la, rb, lb


def mlp_rest(grad_a, grad_b, ra, la, rb, lb):
    block = (2, 4, 32, 1024)
    recv = (hop(ra, "z", 1), hop(la, "z", -1), hop(rb, "x", 1), hop(lb, "x", -1))
    return held_call(rest_body, (grad_a, grad_b), recv, [shaped(*block)] * 2, 2, block, 40)


def add(*terms):
    total = terms[0].astype(F32)
    for term in terms[1:]:
        total = total + term.astype(F32)
    return total.astype(BF)


def contract(left, right, dims):
    return lax.dot_general(left, right, (dims, ((), ())), preferred_element_type=F32)


ROWS = ((1,), (0,))
BOTH = ((1,), (1,))
TOPS = ((0,), (0,))
SCALE = HEAD_DIM ** (-0.5)


def probabilities(query, keys):
    scores = contract(query, keys, BOTH) * SCALE
    weight = jnp.exp(scores - jnp.max(scores, axis=-1, keepdims=True))
    return weight / jnp.sum(weight, axis=-1, keepdims=True)


def att_body(normed, qk_w, values_w, out_w, query_b, value_b, joined, mixed, sent, kept):
    spot = pl.ds(pl.multiple_of(lax.axis_index("tensor") * 256, 256), 256)
    rows = normed[...]
    mixer = out_w[...].reshape(1024, 256)
    pair = contract(rows, qk_w[...].reshape(1024, 512), ROWS)
    joined[:, 0:256] = (pair[:, 0:256] + query_b[:, spot]).astype(BF)
    joined[:, 256:512] = pair[:, 256:].astype(BF)
    last = contract(rows, values_w[...].reshape(1024, 256), ROWS)
    joined[:, 512:768] = (last + value_b[:, spot]).astype(BF)
    for image in range(2):
        line = slice(image * 256, image * 256 + 256)
        parts = []
        for head in range(4):
            query, keys, values = (
                joined[line, base + head * 64 : base + head * 64 + 64] for base in (0, 256, 512)
            )
            probs = probabilities(query, keys).astype(BF)
            parts.append(contract(probs, values, ROWS).astype(BF))
        whole = jnp.concatenate(parts, axis=1)
        mixed[line, :] = whole
        split_blocks(image, contract(whole, mixer, BOTH), sent, kept)


def split_blocks(image, part, sent, kept):
    for spot in range(2):
        kept[image, spot] = part[spot * 64 : spot * 64 + 64]
        sent[image, spot] = part[128 + spot * 64 : 192 + spot * 64].astype(BF)


def middle_body(half, came, own, across, out_b, gain, shift, normed, middle):
    for image in range(2):
        for spot, piece in enumerate((own, across)):
            total = half[image, spot].astype(F32) + came[image, 1 - spot].astype(F32)
            value = piece[image].astype(F32) + (total + out_b[...])
            middle[image, spot] = value
            unit, _ = normalize(value)
            normed[image, spot] = (unit * gain[...] + shift[...]).astype(BF)


def middle_back_body(
    half, came, own, across, middle, gain, att, grad, gain_grad, shift_grad, out_b_grad
):
    sums = [jnp.zeros((1, 1024), F32) for _ in range(3)]
    for image in range(2):
        for spot, piece in enumerate((own, across)):
            total = half[image, spot].astype(F32) + came[image, 1 - spot].astype(F32)
            unit, scale = normalize(middle[image, spot])
            value = piece[image].astype(F32) + norm_back(total, unit, scale, gain[...])
            low = value.astype(BF)
            att[image, spot] = low
            if spot == 0:
                grad[image] = value
                for place, item in enumerate((total * unit, total, low.astype(F32))):
                    sums[place] = sums[place] + jnp.sum(item, axis=0, keepdims=True)
    gain_grad[...], shift_grad[...], out_b_grad[...] = sums


def collect_far(kept, sent):
    return kept + swap(sent, 2).astype(F32)


def normalize(values):
    center = values - jnp.mean(values, axis=-1, keepdims=True)
    scale = lax.rsqrt(jnp.mean(center * center, axis=-1, keepdims=True) + EPS_NORM)
    return center * scale, scale


def norm_back(grad, unit, scale, gain):
    inner = grad * gain
    first = jnp.mean(inner, axis=-1, keepdims=True)
    second = jnp.mean(inner * unit, axis=-1, keepdims=True)
    return scale * (inner - first - unit * second)


def back_body(
    pair, beside, normed, mixed, joined, qk_w, values_w, out_w, hidden, gain_two, shift_two,
    out_b, down_b, up_b, sent, kept, vector, *rest,
):
    sends_a, sends_b, own_a, own_b = rest[0:3], rest[3:6], rest[6], rest[7]
    grads, att, grad_a, grad_b, low, done = rest[8:]
    tensor = lax.axis_index("tensor")
    for image in range(2):
        for spot, piece in enumerate((pair, beside)):
            first = image * 256 + spot * 128
            att[first : first + 128, :] = piece[image].reshape(128, 1024)
    pair_w = qk_w[...].reshape(1024, 512)
    last_w = values_w[...].reshape(1024, 256)
    mixer = out_w[...].reshape(1024, 256)
    gain = jnp.zeros((1, 1024), F32)
    shift = jnp.zeros((1, 1024), F32)
    for image in range(2):
        line = slice(image * 256, image * 256 + 256)
        grad_mixed = contract(att[line, :], mixer, ROWS).astype(BF)
        parts = ([], [], [])
        for head in range(4):
            query, keys, values = (
                joined[line, base + head * 64 : base + head * 64 + 64] for base in (0, 256, 512)
            )
            grad = grad_mixed[:, head * 64 : head * 64 + 64]
            probs = probabilities(query, keys)
            grad_prob = contract(grad, values, BOTH)
            inner = jnp.sum(grad_prob * probs, axis=-1, keepdims=True)
            score = (probs * (grad_prob - inner)).astype(BF)
            parts[0].append((contract(score, keys, ROWS) * SCALE).astype(BF))
            parts[1].append((contract(score, query, TOPS) * SCALE).astype(BF))
            parts[2].append(contract(probs.astype(BF), grad, TOPS).astype(BF))
        for kind in range(3):
            grads[line, kind * 256 : kind * 256 + 256] = jnp.concatenate(parts[kind], axis=1)
        norm_grad = contract(grads[line, :512], pair_w, BOTH) + contract(
            grads[line, 512:], last_w, BOTH
        )
        unit, _ = normalize(hidden[line, :].astype(F32))
        gain = gain + jnp.sum(norm_grad * unit, axis=0, keepdims=True)
        shift = shift + jnp.sum(norm_grad, axis=0, keepdims=True)
        split_blocks(image, norm_grad, sent, kept)
    vector[...] = jnp.zeros(vector.shape, F32)
    rows = (
        (0, gain), (2, shift), (8, out_b[...]), (10, gain_two[...]), (12, shift_two[...]),
        (14, down_b[...]),
    )
    for row, value in rows:
        vector[row : row + 1, :] = value[:, :512]
        vector[row + 1 : row + 2, :] = value[:, 512:]
    spot = pl.ds(pl.multiple_of(lax.rem(tensor, 2) * 256, 256), 256)
    for row, base in ((4, 0), (6, 512)):
        part = jnp.sum(grads[:, base : base + 256].astype(F32), axis=0, keepdims=True)
        vector[pl.ds(row + lax.div(tensor, 2), 1), spot] = part
    vector[pl.ds(16 + 2 * tensor, 1), :] = up_b[:, :512]
    vector[pl.ds(17 + 2 * tensor, 1), :] = up_b[:, 512:]
    _, z, x = here()
    grad_a[...] = contract(normed[...], grads[:, 0:512], TOPS).astype(BF).reshape(grad_a.shape)
    pairs = [(grad_a.at[:, turn(z, 0)], own_a)]
    low[...] = vector[...].astype(BF)
    for step in range(1, 4):
        target = sends_a[step - 1]
        for half in range(2):
            pairs.append((grad_a.at[half, turn(z, step)], target.at[pl.ds(4 * half, 4)]))
        pairs.append((low, target.at[8]))
    copies = [
        pltpu.make_async_copy(source, target, done.at[spot])
        for spot, (source, target) in enumerate(pairs)
    ]
    for copy in copies:
        copy.start()
    last = contract(normed[...], grads[:, 512:768], TOPS).astype(BF)
    grad_b[:, :, :, :, 0:256] = last.reshape(2, 4, 4, 32, 256)
    last = contract(att[...], mixed[...], TOPS).astype(BF)
    grad_b[:, :, :, :, 256:512] = last.reshape(2, 4, 4, 32, 256)
    others = [(grad_b.at[:, :, turn(x, 0)], own_b)]
    for step in range(1, 4):
        others.append((grad_b.at[:, :, turn(x, step)], sends_b[step - 1]))
    more = [
        pltpu.make_async_copy(source, target, done.at[len(pairs) + spot])
        for spot, (source, target) in enumerate(others)
    ]
    for copy in more:
        copy.start()
    for copy in copies + more:
        copy.wait()


def second_body(*refs):
    a1, a2, a3, own_a, b1, b2, b3, own_b, vector, mlp_a, mlp_b = refs[:11]
    outs_a, outs_b, sum_a, sum_b = refs[11:15], refs[15:19], refs[19], refs[20]
    _, z, x = here()
    for yh in range(2):
        part = slice(4 * yh, 4 * yh + 4)
        sum_a[yh] = add(own_a[yh], a1[part], a2[part], a3[part])
        sum_b[yh] = add(own_b[yh], b1[yh], b2[yh], b3[yh])
    low = add(vector[...], a1[8], a2[8], a3[8])
    for step in range(4):
        for out, total, mlp, index in (
            (outs_a[step], sum_a, mlp_a, turn(x, step)),
            (outs_b[step], sum_b, mlp_b, turn(z, step)),
        ):
            for yh in range(2):
                out[yh] = total[yh, index]
                out[2 + yh] = mlp[yh, index, :, 0:512]
                out[4 + yh] = mlp[yh, index, :, 512:1024]
        outs_a[step][6] = low


def third_body(a0, a1, a2, a3, b0, b1, b2, b3, send, own):
    yh, _, _ = here()
    for spot in range(3):
        for base, pieces in ((0, (a0, a1, a2, a3)), (3, (b0, b1, b2, b3))):
            mine = [piece[2 * spot + yh].astype(F32) for piece in pieces]
            other = [piece[2 * spot + 1 - yh].astype(F32) for piece in pieces]
            own[base + spot] = (mine[0] + mine[1]) + (mine[2] + mine[3])
            send[base + spot] = ((other[0] + other[1]) + (other[2] + other[3])).astype(BF)
    total = [piece[6].astype(F32) for piece in (a0, a1, a2, a3)]
    total = (total[0] + total[1]) + (total[2] + total[3])
    own[6] = total
    send[6] = total.astype(BF)


def last_body(own, came, qkv, out, up, down, vector):
    def total(spot):
        return own[spot] + came[spot].astype(F32)

    att_a, att_b = total(0), total(3)
    qkv[0] = att_a[:, 0:256]
    qkv[1] = att_a[:, 256:512]
    qkv[2] = att_b[:, 0:256]
    out[...] = att_b[:, 256:512]
    up[:, 0:512] = total(1)
    up[:, 512:1024] = total(2)
    down[:, 0:512] = total(4)
    down[:, 512:1024] = total(5)
    vector[...] = total(6)


def att_scatter(arrays, mlp_a, mlp_b, down_part):
    block = (2, 4, 32, 512)
    shapes = [
        shaped(2, 2, 64, 1024),
        shaped(2, 2, 64, 1024, kind=F32),
        shaped(32, 512, kind=F32),
    ]
    shapes += [shaped(9, 32, 512)] * 3 + [shaped(*block)] * 5
    sent, kept, vector, *results = pl.pallas_call(
        back_body,
        out_shape=shapes,
        in_specs=[VMEM] * len(arrays),
        out_specs=[VMEM] * 3 + [ANY] * 8,
        scratch_shapes=[
            pltpu.VMEM((512, 768), BF),
            pltpu.VMEM((512, 1024), BF),
            pltpu.VMEM((2, 4, 4, 32, 512), BF),
            pltpu.VMEM((2, 4, 4, 32, 512), BF),
            pltpu.VMEM((32, 512), BF),
            pltpu.SemaphoreType.DMA((14,)),
        ],
        compiler_params=limit(56),
    )(*arrays)
    near = swap(jnp.stack([sent, down_part[1].astype(BF)]), 1).astype(F32)
    sums = [kept + near[0], down_part[0] + near[1]]
    came = swap(jnp.stack([item[:, 1].astype(BF) for item in sums]), 2)
    totals = [item[:, 0] + came[spot].astype(F32) for spot, item in enumerate(sums)]
    results = lax.optimization_barrier((*results, mlp_a))[:-1]
    came_a, came_b = near_scatter(*results[:3], "z", *results[3:6], "x")
    pieces = whole_call(
        second_body,
        (*came_a, results[6], *came_b, results[7], vector, mlp_a, mlp_b),
        [shaped(7, 32, 512)] * 4 + [shaped(6, 32, 512)] * 4,
        40,
        scratch=[pltpu.VMEM(block, BF), pltpu.VMEM(block, BF)],
    )
    came_a, came_b = near_scatter(*pieces[1:4], "x", *pieces[5:8], "z")
    send, own = whole_call(
        third_body,
        (pieces[0], *came_a, pieces[4], *came_b),
        [shaped(7, 32, 512), shaped(7, 32, 512, kind=F32)],
        40,
    )
    send = after(send, came)
    shapes = [(3, 32, 256), (32, 256), (32, 1024), (32, 1024), (32, 512)]
    results = whole_call(
        last_body, (own, hop(send, "y", 1)), [shaped(*shape, kind=F32) for shape in shapes], 40
    )
    return *totals, *results


def dot(spec, left, right):
    return jnp.einsum(spec, left, right, preferred_element_type=F32)


def local(
    tokens,
    dealt,
    cotangent,
    qkv_weight,
    out_weight,
    up_weight,
    down_weight,
    norm1_gain,
    norm1_bias,
    query_bias,
    value_bias,
    out_bias,
    norm2_gain,
    norm2_bias,
    up_bias,
    down_bias,
):
    tensor = lax.axis_index("tensor")
    rows = tokens.shape[2]
    width = tokens.shape[3]
    count = 8 * rows
    weight_rows = (YH, ZN, XN, 32)

    def own_part(vector, size):
        return lax.dynamic_slice_in_dim(vector[0], tensor * size, size, 0)

    (own,) = move(
        pack_plan,
        (jnp.transpose(qkv_weight[0], (1, 0, 2)), out_weight[0], up_weight[0], down_weight[0]),
        [shaped(32, 3072)],
        6,
    )
    other = hop(own, "y", 1)
    part_a, part_b = whole_call(pair_body, (own, other), [shaped(2, 32, 1536)] * 2, 16)
    pieces_a, pieces_b = near_gather(part_a, "x", part_b, "z")
    all_a, all_b = move(first_plan, pieces_a + pieces_b, [shaped(2, 4, 32, 1536)] * 2, 8)
    ring = ring_gather(all_a, "z") + ring_gather(all_b, "x")
    shapes = [shaped(*weight_rows, 512), shaped(*weight_rows, 256), shaped(*weight_rows, 256)]
    qk_w, values_w, out_w = move(att_plan, ring, shapes, 15)
    up_w, down_w = move(mlp_plan, ring, [shaped(*weight_rows, 1024)] * 2, 10)
    up_w, down_w = up_w.reshape(width, -1), down_w.reshape(width, -1)

    live = dealt.astype(F32).reshape(2, 1, 1)
    own_tokens = tokens[:, 0]
    grad_own = cotangent[:, 0].astype(F32) * live
    grad_low = grad_own.astype(BF)
    both = jnp.stack([own_tokens, grad_low])
    across = swap(both, 2)
    across = after(across, pieces_a[1], pieces_b[1], pieces_a[3], pieces_b[3])
    pair = jnp.stack([both, across], axis=2)
    beside = swap(pair, 1)
    hidden = jnp.stack([pair[0], beside[0]], axis=1).reshape(count, width)
    down_all = jnp.stack([pair[1], beside[1]]).reshape(count, width)
    across, grad_across = across[0], across[1]
    unit_one, _ = normalize(hidden.astype(F32))
    normed = (unit_one * norm1_gain[0] + norm1_bias[0]).astype(BF)
    quarter = (2, 2, rows, width)
    joined, mixed, sent, kept = whole_call(
        att_body,
        (normed, qk_w, values_w, out_w, query_bias, value_bias),
        [shaped(count, 768), shaped(count, 256), shaped(*quarter), shaped(*quarter, kind=F32)],
        48,
    )
    half = (kept + swap(sent, 1).astype(F32)).astype(BF)
    normed_pair, middle = whole_call(
        middle_body,
        (half, swap(half, 2), own_tokens, across, out_bias, norm2_gain, norm2_bias),
        [shaped(*quarter), shaped(*quarter, kind=F32)],
        32,
    )
    normed_two = jnp.stack([normed_pair, swap(normed_pair, 1)]).reshape(count, width)
    upward = dot("sd,df->sf", normed_two, up_w) + own_part(up_bias, 1024)
    share = 0.5 * (1.0 + lax.erf(upward * (0.5**0.5)))
    activated = (upward * share).astype(BF)
    slope = share + upward * (jnp.exp(-0.5 * upward * upward) * (0.5 / jnp.pi) ** 0.5)

    grad_up = (dot("se,ef->sf", down_all, down_w) * slope).astype(BF)
    norm_two_part = dot("sf,df->sd", grad_up, up_w).reshape(2, *quarter)
    half = (norm_two_part[0] + swap(norm_two_part[1].astype(BF), 1).astype(F32)).astype(BF)
    up_grad = dot("sd,sf->df", normed_two, grad_up).astype(BF)
    down_grad = dot("se,sf->ef", down_all, activated).astype(BF)
    up_grad, down_grad = lax.optimization_barrier((up_grad, down_grad, half))[:2]
    up_grad = up_grad.reshape(*weight_rows, -1)
    down_grad = down_grad.reshape(*weight_rows, -1)
    passed = mlp_scatter(up_grad, down_grad)
    mlp_a, mlp_b = mlp_rest(up_grad, down_grad, *passed)
    up_b_grad = jnp.sum(grad_up.astype(F32), axis=0, keepdims=True)
    down_b_grad = jnp.sum(grad_own, axis=(0, 1))[None]

    att_pair, grad_middle, gain_two_grad, shift_two_grad, out_b_grad = whole_call(
        middle_back_body,
        (half, swap(half, 2), grad_low, grad_across, middle, norm2_gain),
        [shaped(*quarter), shaped(2, rows, width, kind=F32)] + [shaped(1, width, kind=F32)] * 3,
        32,
    )
    att_beside = swap(att_pair, 1)
    att_pair = after(att_pair, *passed)

    down_part = dot("sf,ef->se", activated, down_w).reshape(2, *quarter)

    arrays = (
        att_pair,
        att_beside,
        normed,
        mixed,
        joined,
        qk_w,
        values_w,
        out_w,
        hidden,
        gain_two_grad,
        shift_two_grad,
        out_b_grad,
        down_b_grad,
        up_b_grad,
    )
    grad_norm_one, down_total, qkv_grad, out_grad, up_grad, down_grad, vector = att_scatter(
        arrays, mlp_a, mlp_b, down_part
    )
    block_out = ((middle[:, 0] + (down_total + down_bias[0])) * live).astype(BF)[:, None]
    unit_own, scale_own = normalize(own_tokens.astype(F32))
    input_grad = grad_middle + norm_back(grad_norm_one, unit_own, scale_own, norm1_gain[0])
    input_grad = input_grad.astype(BF)[:, None]

    vector = vector + swap(vector, 1) + swap(vector, 2) + swap(vector, 3)
    vector = vector[:24].reshape(1, -1)
    parts = [vector[:, k * width : (k + 1) * width] for k in range(8)]
    return (
        block_out,
        input_grad,
        jnp.transpose(qkv_grad, (1, 0, 2))[None],
        out_grad[None],
        up_grad[None],
        down_grad[None],
        *parts[:7],
        vector[:, 8 * width :],
        parts[7],
    )


def solution(mesh):
    rows = P(None, "fsdp", "tensor", None)
    matrix = P(None, "fsdp", "tensor")
    qkv = P(None, "fsdp", None, "tensor")
    return jax.shard_map(
        local,
        mesh=mesh,
        in_specs=(rows, P(None, "fsdp"), rows, qkv, matrix, matrix, matrix) + (P(),) * 9,
        out_specs=(rows, rows, qkv, matrix, matrix, matrix) + (P(),) * 9,
        check_vma=False,
    )
```

```python
import jax
import jax.numpy as jnp
from jax import lax
from jax.experimental import pallas as pl
from jax.experimental.pallas import tpu as pltpu
from jax.sharding import PartitionSpec as P

HEAD_DIM = 64
EPS_NORM = 1e-06
BF = jnp.bfloat16
F32 = jnp.float32

YH, ZN, XN = 2, 4, 4


def fsdp_perm(dx, dz, dy):
    pairs = []
    for source in range(YH * ZN * XN):
        yh, z, x = source // (ZN * XN), (source // XN) % ZN, source % XN
        target = (((yh + dy) % YH) * ZN + (z + dz) % ZN) * XN + (x + dx) % XN
        pairs.append((source, target))
    return pairs


def hop(array, axis, step):
    move = {"x": (step, 0, 0), "z": (0, step, 0), "y": (0, 0, step)}[axis]
    return lax.ppermute(array, "fsdp", fsdp_perm(*move))


def swap(array, mask):
    return lax.ppermute(array, "tensor", [(i, i ^ mask) for i in range(4)])


def here():
    index = lax.axis_index("fsdp")
    plane = ZN * XN
    return lax.div(index, plane), lax.rem(lax.div(index, XN), ZN), lax.rem(index, XN)


def turn(index, step):
    return lax.rem(index + step, 4)


def shaped(*shape, kind=BF):
    return jax.ShapeDtypeStruct(shape, kind)


def limit(mebibytes):
    return pltpu.CompilerParams(vmem_limit_bytes=mebibytes << 20)


VMEM = pl.BlockSpec(memory_space=pltpu.VMEM)
ANY = pl.BlockSpec(memory_space=pl.ANY)


def move(plan, arrays, shapes, count):
    def body(*refs):
        inputs, outputs, done = refs[: len(arrays)], refs[len(arrays) : -1], refs[-1]
        pairs = plan(inputs, outputs)
        copies = [
            pltpu.make_async_copy(source, target, done.at[spot])
            for spot, (source, target) in enumerate(pairs)
        ]
        for copy in copies:
            copy.start()
        for copy in copies:
            copy.wait()

    size = sum(item.size * 2 for item in shapes)
    return pl.pallas_call(
        body,
        out_shape=shapes,
        in_specs=[ANY] * len(arrays),
        out_specs=[VMEM] * len(shapes),
        scratch_shapes=[pltpu.SemaphoreType.DMA((count,))],
        compiler_params=limit(16),
        cost_estimate=pl.CostEstimate(flops=0, bytes_accessed=2 * size, transcendentals=0),
    )(*arrays)


def whole_call(body, arrays, shapes, mebibytes, scratch=(), cost=None):
    size = sum(item.size * item.dtype.itemsize for item in list(shapes) + list(arrays))
    cost = cost or pl.CostEstimate(flops=0, bytes_accessed=size, transcendentals=0)
    return pl.pallas_call(
        body,
        out_shape=shapes,
        scratch_shapes=scratch,
        compiler_params=limit(mebibytes),
        cost_estimate=cost,
    )(*arrays)


def after(value, *others):
    return lax.optimization_barrier((value,) + others)[0]


def near_gather(block_a, axis_a, block_b, axis_b):
    right_a, right_b = hop(block_a, axis_a, -1), hop(block_b, axis_b, -1)
    left_a, left_b = hop(block_a, axis_a, 1), hop(block_b, axis_b, 1)
    late_a, late_b = lax.optimization_barrier(
        (block_a, block_b, right_a, right_b, left_a, left_b)
    )[:2]
    far_a, far_b = hop(late_a, axis_a, 2), hop(late_b, axis_b, 2)
    return [block_a, right_a, far_a, left_a], [block_b, right_b, far_b, left_b]


def ring_gather(block, axis):
    right, left = hop(block, axis, -1), hop(block, axis, 1)
    low, high = hop(left[0], axis, 1), hop(right[1], axis, -1)
    return [block, right, left, low, high]


def near_scatter(right_a, far_a, left_a, axis_a, right_b, far_b, left_b, axis_b):
    came = [
        hop(right_a, axis_a, 1), hop(right_b, axis_b, 1),
        hop(left_a, axis_a, -1), hop(left_b, axis_b, -1),
    ]
    far_a, far_b = lax.optimization_barrier((far_a, far_b, *came))[:2]
    far_a, far_b = hop(far_a, axis_a, 2), hop(far_b, axis_b, 2)
    return (came[0], far_a, came[2]), (came[1], far_b, came[3])


def pack_plan(inputs, outputs):
    qkv, out, up, down = inputs
    own = outputs[0]
    return [
        (qkv.at[0], own.at[:, 0:256]),
        (qkv.at[1], own.at[:, 256:512]),
        (up, own.at[:, 512:1536]),
        (qkv.at[2], own.at[:, 1536:1792]),
        (out, own.at[:, 1792:2048]),
        (down, own.at[:, 2048:3072]),
    ]


def pair_body(own, other, part_a, part_b):
    yh, _, _ = here()
    part_a[yh] = own[:, :1536]
    part_b[yh] = own[:, 1536:]
    part_a[1 - yh] = other[:, :1536]
    part_b[1 - yh] = other[:, 1536:]


def first_plan(inputs, outputs):
    _, z, x = here()
    all_a, all_b = outputs
    pairs = []
    for step in range(4):
        pairs.append((inputs[step], all_a.at[:, turn(x, step)]))
        pairs.append((inputs[4 + step], all_b.at[:, turn(z, step)]))
    return pairs


def cut_plan(first, last, axis, inputs, target):
    _, z, x = here()
    columns = slice(first, last)

    def spot(step, half):
        if axis == "z":
            return target.at[half, turn(z, step)]
        return target.at[half, :, turn(x, step)]

    whole = slice(0, 2)
    pairs = []
    for piece, step in zip(inputs[:3], (0, 1, 3)):
        pairs.append((piece.at[:, :, :, columns], spot(step, whole)))
    for half in range(2):
        pairs.append((inputs[3 + half].at[:, :, columns], spot(2, half)))
    return pairs


def att_plan(inputs, outputs):
    qk_w, values_w, out_w = outputs
    return (
        cut_plan(0, 512, "z", inputs[:5], qk_w)
        + cut_plan(0, 256, "x", inputs[5:], values_w)
        + cut_plan(256, 512, "x", inputs[5:], out_w)
    )


def mlp_plan(inputs, outputs):
    up_w, down_w = outputs
    return cut_plan(512, 1536, "z", inputs[:5], up_w) + cut_plan(
        512, 1536, "x", inputs[5:], down_w
    )


def far_plan(inputs, outputs):
    _, z, x = here()
    grad_a, grad_b = inputs
    pairs = []
    for half in range(2):
        pairs.append((grad_a.at[half, turn(z, 2)], outputs[half]))
        pairs.append((grad_b.at[half, :, turn(x, 2)], outputs[2 + half]))
    return pairs


def fetch(pairs, done):
    copies = [
        pltpu.make_async_copy(source, target, done.at[spot])
        for spot, (source, target) in enumerate(pairs)
    ]
    for copy in copies:
        copy.start()
    for copy in copies:
        copy.wait()


def pass_body(grad_a, grad_b, low_a, high_a, low_b, high_b, ra, la, rb, lb, held, done):
    _, z, x = here()
    fetch(
        [
            (grad_a.at[:, turn(z, 1)], held.at[0]),
            (grad_a.at[:, turn(z, 3)], held.at[1]),
            (grad_b.at[:, :, turn(x, 1)], held.at[2]),
            (grad_b.at[:, :, turn(x, 3)], held.at[3]),
        ],
        done,
    )
    for spot, (right, left, low, high) in enumerate(
        ((ra, la, low_a, high_a), (rb, lb, low_b, high_b))
    ):
        right[0] = add(held[2 * spot, 0], low[...])
        right[1] = held[2 * spot, 1]
        left[0] = held[2 * spot + 1, 0]
        left[1] = add(held[2 * spot + 1, 1], high[...])


def rest_body(grad_a, grad_b, la, ra, lb, rb, total_a, total_b, held, done):
    _, z, x = here()
    fetch(
        [(grad_a.at[:, turn(z, 0)], held.at[0]), (grad_b.at[:, :, turn(x, 0)], held.at[1])],
        done,
    )
    total_a[...] = add(held[0], la[...], ra[...])
    total_b[...] = add(held[1], lb[...], rb[...])


def held_call(body, whole, arrays, shapes, slots, block, mebibytes):
    size = sum(item.size * 2 for item in shapes) + sum(item.size * 2 for item in arrays)
    return pl.pallas_call(
        body,
        out_shape=shapes,
        in_specs=[ANY] * len(whole) + [VMEM] * len(arrays),
        out_specs=[VMEM] * len(shapes),
        scratch_shapes=[pltpu.VMEM((slots,) + block, BF), pltpu.SemaphoreType.DMA((slots,))],
        compiler_params=limit(mebibytes),
        cost_estimate=pl.CostEstimate(flops=0, bytes_accessed=2 * size, transcendentals=0),
    )(*whole, *arrays)


def mlp_far(grad_a, grad_b):
    halves = move(far_plan, (grad_a, grad_b), [shaped(4, 32, 1024)] * 4, 4)
    low_a, high_a, low_b, high_b = halves
    return hop(low_a, "z", 1), hop(high_a, "z", -1), hop(low_b, "x", 1), hop(high_b, "x", -1)


def mlp_pass(grad_a, grad_b, *recv):
    block = (2, 4, 32, 1024)
    return held_call(pass_body, (grad_a, grad_b), recv, [shaped(*block)] * 4, 4, block, 40)


def mlp_rest(grad_a, grad_b, ra, la, rb, lb):
    block = (2, 4, 32, 1024)
    recv = (hop(ra, "z", 1), hop(la, "z", -1), hop(rb, "x", 1), hop(lb, "x", -1))
    return held_call(rest_body, (grad_a, grad_b), recv, [shaped(*block)] * 2, 2, block, 40)


def add(*terms):
    total = terms[0].astype(F32)
    for term in terms[1:]:
        total = total + term.astype(F32)
    return total.astype(BF)


def contract(left, right, dims):
    return lax.dot_general(left, right, (dims, ((), ())), preferred_element_type=F32)


ROWS = ((1,), (0,))
BOTH = ((1,), (1,))
TOPS = ((0,), (0,))
SCALE = HEAD_DIM ** (-0.5)


def probabilities(query, keys):
    scores = contract(query, keys, BOTH) * SCALE
    weight = jnp.exp(scores - jnp.max(scores, axis=-1, keepdims=True))
    return weight / jnp.sum(weight, axis=-1, keepdims=True)


def att_body(normed, qk_w, values_w, out_w, query_b, value_b, joined, mixed, sent, kept):
    spot = pl.ds(pl.multiple_of(lax.axis_index("tensor") * 256, 256), 256)
    rows = normed[...]
    mixer = out_w[...].reshape(1024, 256)
    pair = contract(rows, qk_w[...].reshape(1024, 512), ROWS)
    joined[:, 0:256] = (pair[:, 0:256] + query_b[:, spot]).astype(BF)
    joined[:, 256:512] = pair[:, 256:].astype(BF)
    last = contract(rows, values_w[...].reshape(1024, 256), ROWS)
    joined[:, 512:768] = (last + value_b[:, spot]).astype(BF)
    for image in range(2):
        line = slice(image * 256, image * 256 + 256)
        parts = []
        for head in range(4):
            query, keys, values = (
                joined[line, base + head * 64 : base + head * 64 + 64] for base in (0, 256, 512)
            )
            probs = probabilities(query, keys).astype(BF)
            parts.append(contract(probs, values, ROWS).astype(BF))
        whole = jnp.concatenate(parts, axis=1)
        mixed[line, :] = whole
        split_blocks(image, contract(whole, mixer, BOTH), sent, kept)


def split_blocks(image, part, sent, kept):
    for spot in range(2):
        kept[image, spot] = part[spot * 64 : spot * 64 + 64]
        sent[image, spot] = part[128 + spot * 64 : 192 + spot * 64].astype(BF)


def middle_body(half, came, own, across, out_b, gain, shift, normed, middle):
    for image in range(2):
        for spot, piece in enumerate((own, across)):
            total = half[image, spot].astype(F32) + came[image, 1 - spot].astype(F32)
            value = piece[image].astype(F32) + (total + out_b[...])
            middle[image, spot] = value
            unit, _ = normalize(value)
            normed[image, spot] = (unit * gain[...] + shift[...]).astype(BF)


def middle_back_body(
    half, came, own, across, middle, gain, att, grad, gain_grad, shift_grad, out_b_grad
):
    sums = [jnp.zeros((1, 1024), F32) for _ in range(3)]
    for image in range(2):
        for spot, piece in enumerate((own, across)):
            total = half[image, spot].astype(F32) + came[image, 1 - spot].astype(F32)
            unit, scale = normalize(middle[image, spot])
            value = piece[image].astype(F32) + norm_back(total, unit, scale, gain[...])
            low = value.astype(BF)
            att[image, spot] = low
            if spot == 0:
                grad[image] = value
                for place, item in enumerate((total * unit, total, low.astype(F32))):
                    sums[place] = sums[place] + jnp.sum(item, axis=0, keepdims=True)
    gain_grad[...], shift_grad[...], out_b_grad[...] = sums


def collect_far(kept, sent):
    return kept + swap(sent, 2).astype(F32)


def normalize(values):
    center = values - jnp.mean(values, axis=-1, keepdims=True)
    scale = lax.rsqrt(jnp.mean(center * center, axis=-1, keepdims=True) + EPS_NORM)
    return center * scale, scale


def norm_back(grad, unit, scale, gain):
    inner = grad * gain
    first = jnp.mean(inner, axis=-1, keepdims=True)
    second = jnp.mean(inner * unit, axis=-1, keepdims=True)
    return scale * (inner - first - unit * second)


def back_body(
    pair, beside, normed, mixed, joined, qk_w, values_w, out_w, hidden, gain_two, shift_two,
    out_b, down_b, up_b, sent, kept, vector, *rest,
):
    sends_a, sends_b, own_a, own_b = rest[0:3], rest[3:6], rest[6], rest[7]
    grads, att, grad_a, grad_b, low, done = rest[8:]
    tensor = lax.axis_index("tensor")
    for image in range(2):
        for spot, piece in enumerate((pair, beside)):
            first = image * 256 + spot * 128
            att[first : first + 128, :] = piece[image].reshape(128, 1024)
    pair_w = qk_w[...].reshape(1024, 512)
    last_w = values_w[...].reshape(1024, 256)
    mixer = out_w[...].reshape(1024, 256)
    gain = jnp.zeros((1, 1024), F32)
    shift = jnp.zeros((1, 1024), F32)
    for image in range(2):
        line = slice(image * 256, image * 256 + 256)
        grad_mixed = contract(att[line, :], mixer, ROWS).astype(BF)
        parts = ([], [], [])
        for head in range(4):
            query, keys, values = (
                joined[line, base + head * 64 : base + head * 64 + 64] for base in (0, 256, 512)
            )
            grad = grad_mixed[:, head * 64 : head * 64 + 64]
            probs = probabilities(query, keys)
            grad_prob = contract(grad, values, BOTH)
            inner = jnp.sum(grad_prob * probs, axis=-1, keepdims=True)
            score = (probs * (grad_prob - inner)).astype(BF)
            parts[0].append((contract(score, keys, ROWS) * SCALE).astype(BF))
            parts[1].append((contract(score, query, TOPS) * SCALE).astype(BF))
            parts[2].append(contract(probs.astype(BF), grad, TOPS).astype(BF))
        for kind in range(3):
            grads[line, kind * 256 : kind * 256 + 256] = jnp.concatenate(parts[kind], axis=1)
        norm_grad = contract(grads[line, :512], pair_w, BOTH) + contract(
            grads[line, 512:], last_w, BOTH
        )
        unit, _ = normalize(hidden[line, :].astype(F32))
        gain = gain + jnp.sum(norm_grad * unit, axis=0, keepdims=True)
        shift = shift + jnp.sum(norm_grad, axis=0, keepdims=True)
        split_blocks(image, norm_grad, sent, kept)
    vector[...] = jnp.zeros(vector.shape, F32)
    rows = (
        (0, gain), (2, shift), (8, out_b[...]), (10, gain_two[...]), (12, shift_two[...]),
        (14, down_b[...]),
    )
    for row, value in rows:
        vector[row : row + 1, :] = value[:, :512]
        vector[row + 1 : row + 2, :] = value[:, 512:]
    spot = pl.ds(pl.multiple_of(lax.rem(tensor, 2) * 256, 256), 256)
    for row, base in ((4, 0), (6, 512)):
        part = jnp.sum(grads[:, base : base + 256].astype(F32), axis=0, keepdims=True)
        vector[pl.ds(row + lax.div(tensor, 2), 1), spot] = part
    vector[pl.ds(16 + 2 * tensor, 1), :] = up_b[:, :512]
    vector[pl.ds(17 + 2 * tensor, 1), :] = up_b[:, 512:]
    _, z, x = here()
    grad_a[...] = contract(normed[...], grads[:, 0:512], TOPS).astype(BF).reshape(grad_a.shape)
    pairs = [(grad_a.at[:, turn(z, 0)], own_a)]
    low[...] = vector[...].astype(BF)
    for step in range(1, 4):
        target = sends_a[step - 1]
        for half in range(2):
            pairs.append((grad_a.at[half, turn(z, step)], target.at[pl.ds(4 * half, 4)]))
        pairs.append((low, target.at[8]))
    copies = [
        pltpu.make_async_copy(source, target, done.at[spot])
        for spot, (source, target) in enumerate(pairs)
    ]
    for copy in copies:
        copy.start()
    last = contract(normed[...], grads[:, 512:768], TOPS).astype(BF)
    grad_b[:, :, :, :, 0:256] = last.reshape(2, 4, 4, 32, 256)
    last = contract(att[...], mixed[...], TOPS).astype(BF)
    grad_b[:, :, :, :, 256:512] = last.reshape(2, 4, 4, 32, 256)
    others = [(grad_b.at[:, :, turn(x, 0)], own_b)]
    for step in range(1, 4):
        others.append((grad_b.at[:, :, turn(x, step)], sends_b[step - 1]))
    more = [
        pltpu.make_async_copy(source, target, done.at[len(pairs) + spot])
        for spot, (source, target) in enumerate(others)
    ]
    for copy in more:
        copy.start()
    for copy in copies + more:
        copy.wait()


def second_body(*refs):
    a1, a2, a3, own_a, b1, b2, b3, own_b, vector, mlp_a, mlp_b = refs[:11]
    outs_a, outs_b, sum_a, sum_b = refs[11:15], refs[15:19], refs[19], refs[20]
    _, z, x = here()
    for yh in range(2):
        part = slice(4 * yh, 4 * yh + 4)
        sum_a[yh] = add(own_a[yh], a1[part], a2[part], a3[part])
        sum_b[yh] = add(own_b[yh], b1[yh], b2[yh], b3[yh])
    low = add(vector[...], a1[8], a2[8], a3[8])
    for step in range(4):
        for out, total, mlp, index in (
            (outs_a[step], sum_a, mlp_a, turn(x, step)),
            (outs_b[step], sum_b, mlp_b, turn(z, step)),
        ):
            for yh in range(2):
                out[yh] = total[yh, index]
                out[2 + yh] = mlp[yh, index, :, 0:512]
                out[4 + yh] = mlp[yh, index, :, 512:1024]
        outs_a[step][6] = low


def third_body(a0, a1, a2, a3, b0, b1, b2, b3, send, own):
    yh, _, _ = here()
    for spot in range(3):
        for base, pieces in ((0, (a0, a1, a2, a3)), (3, (b0, b1, b2, b3))):
            mine = [piece[2 * spot + yh].astype(F32) for piece in pieces]
            other = [piece[2 * spot + 1 - yh].astype(F32) for piece in pieces]
            own[base + spot] = (mine[0] + mine[1]) + (mine[2] + mine[3])
            send[base + spot] = ((other[0] + other[1]) + (other[2] + other[3])).astype(BF)
    total = [piece[6].astype(F32) for piece in (a0, a1, a2, a3)]
    total = (total[0] + total[1]) + (total[2] + total[3])
    own[6] = total
    send[6] = total.astype(BF)


def last_body(own, came, qkv, out, up, down, vector):
    def total(spot):
        return own[spot] + came[spot].astype(F32)

    att_a, att_b = total(0), total(3)
    qkv[0] = att_a[:, 0:256]
    qkv[1] = att_a[:, 256:512]
    qkv[2] = att_b[:, 0:256]
    out[...] = att_b[:, 256:512]
    up[:, 0:512] = total(1)
    up[:, 512:1024] = total(2)
    down[:, 0:512] = total(4)
    down[:, 512:1024] = total(5)
    vector[...] = total(6)


def att_scatter(arrays, mlp_a, mlp_b, down_part):
    block = (2, 4, 32, 512)
    shapes = [
        shaped(2, 2, 64, 1024),
        shaped(2, 2, 64, 1024, kind=F32),
        shaped(32, 512, kind=F32),
    ]
    shapes += [shaped(9, 32, 512)] * 3 + [shaped(*block)] * 5
    sent, kept, vector, *results = pl.pallas_call(
        back_body,
        out_shape=shapes,
        in_specs=[VMEM] * len(arrays),
        out_specs=[VMEM] * 3 + [ANY] * 8,
        scratch_shapes=[
            pltpu.VMEM((512, 768), BF),
            pltpu.VMEM((512, 1024), BF),
            pltpu.VMEM((2, 4, 4, 32, 512), BF),
            pltpu.VMEM((2, 4, 4, 32, 512), BF),
            pltpu.VMEM((32, 512), BF),
            pltpu.SemaphoreType.DMA((14,)),
        ],
        compiler_params=limit(56),
    )(*arrays)
    near = swap(jnp.stack([sent, down_part[1].astype(BF)]), 1).astype(F32)
    sums = [kept + near[0], down_part[0] + near[1]]
    came = swap(jnp.stack([item[:, 1].astype(BF) for item in sums]), 2)
    totals = [item[:, 0] + came[spot].astype(F32) for spot, item in enumerate(sums)]
    results = lax.optimization_barrier((*results, mlp_a))[:-1]
    came_a, came_b = near_scatter(*results[:3], "z", *results[3:6], "x")
    pieces = whole_call(
        second_body,
        (*came_a, results[6], *came_b, results[7], vector, mlp_a, mlp_b),
        [shaped(7, 32, 512)] * 4 + [shaped(6, 32, 512)] * 4,
        40,
        scratch=[pltpu.VMEM(block, BF), pltpu.VMEM(block, BF)],
    )
    came_a, came_b = near_scatter(*pieces[1:4], "x", *pieces[5:8], "z")
    send, own = whole_call(
        third_body,
        (pieces[0], *came_a, pieces[4], *came_b),
        [shaped(7, 32, 512), shaped(7, 32, 512, kind=F32)],
        40,
    )
    send = after(send, came)
    shapes = [(3, 32, 256), (32, 256), (32, 1024), (32, 1024), (32, 512)]
    results = whole_call(
        last_body, (own, hop(send, "y", 1)), [shaped(*shape, kind=F32) for shape in shapes], 40
    )
    return *totals, *results


def dot(spec, left, right):
    return jnp.einsum(spec, left, right, preferred_element_type=F32)


def local(
    tokens,
    dealt,
    cotangent,
    qkv_weight,
    out_weight,
    up_weight,
    down_weight,
    norm1_gain,
    norm1_bias,
    query_bias,
    value_bias,
    out_bias,
    norm2_gain,
    norm2_bias,
    up_bias,
    down_bias,
):
    tensor = lax.axis_index("tensor")
    rows = tokens.shape[2]
    width = tokens.shape[3]
    count = 8 * rows
    weight_rows = (YH, ZN, XN, 32)

    def own_part(vector, size):
        return lax.dynamic_slice_in_dim(vector[0], tensor * size, size, 0)

    (own,) = move(
        pack_plan,
        (jnp.transpose(qkv_weight[0], (1, 0, 2)), out_weight[0], up_weight[0], down_weight[0]),
        [shaped(32, 3072)],
        6,
    )
    other = hop(own, "y", 1)
    part_a, part_b = whole_call(pair_body, (own, other), [shaped(2, 32, 1536)] * 2, 16)
    pieces_a, pieces_b = near_gather(part_a, "x", part_b, "z")
    all_a, all_b = move(first_plan, pieces_a + pieces_b, [shaped(2, 4, 32, 1536)] * 2, 8)
    ring = ring_gather(all_a, "z") + ring_gather(all_b, "x")
    shapes = [shaped(*weight_rows, 512), shaped(*weight_rows, 256), shaped(*weight_rows, 256)]
    qk_w, values_w, out_w = move(att_plan, ring, shapes, 15)
    up_w, down_w = move(mlp_plan, ring, [shaped(*weight_rows, 1024)] * 2, 10)
    up_w, down_w = up_w.reshape(width, -1), down_w.reshape(width, -1)

    live = dealt.astype(F32).reshape(2, 1, 1)
    own_tokens = tokens[:, 0]
    grad_own = cotangent[:, 0].astype(F32) * live
    grad_low = grad_own.astype(BF)
    both = jnp.stack([own_tokens, grad_low])
    across = swap(both, 2)
    across = after(across, ring[1], ring[2], ring[6], ring[7])
    pair = jnp.stack([both, across], axis=2)
    beside = swap(pair, 1)
    hidden = jnp.stack([pair[0], beside[0]], axis=1).reshape(count, width)
    down_all = jnp.stack([pair[1], beside[1]]).reshape(count, width)
    across, grad_across = across[0], across[1]
    unit_one, _ = normalize(hidden.astype(F32))
    normed = (unit_one * norm1_gain[0] + norm1_bias[0]).astype(BF)
    quarter = (2, 2, rows, width)
    joined, mixed, sent, kept = whole_call(
        att_body,
        (normed, qk_w, values_w, out_w, query_bias, value_bias),
        [shaped(count, 768), shaped(count, 256), shaped(*quarter), shaped(*quarter, kind=F32)],
        48,
    )
    half = (kept + swap(sent, 1).astype(F32)).astype(BF)
    normed_pair, middle = whole_call(
        middle_body,
        (half, swap(half, 2), own_tokens, across, out_bias, norm2_gain, norm2_bias),
        [shaped(*quarter), shaped(*quarter, kind=F32)],
        32,
    )
    normed_two = jnp.stack([normed_pair, swap(normed_pair, 1)]).reshape(count, width)
    upward = dot("sd,df->sf", normed_two, up_w) + own_part(up_bias, 1024)
    share = 0.5 * (1.0 + lax.erf(upward * (0.5**0.5)))
    activated = (upward * share).astype(BF)
    slope = share + upward * (jnp.exp(-0.5 * upward * upward) * (0.5 / jnp.pi) ** 0.5)

    grad_up = (dot("se,ef->sf", down_all, down_w) * slope).astype(BF)
    norm_two_part = dot("sf,df->sd", grad_up, up_w).reshape(2, *quarter)
    half = (norm_two_part[0] + swap(norm_two_part[1].astype(BF), 1).astype(F32)).astype(BF)
    up_grad = dot("sd,sf->df", normed_two, grad_up).astype(BF)
    down_grad = dot("se,sf->ef", down_all, activated).astype(BF)
    up_grad, down_grad = lax.optimization_barrier((up_grad, down_grad, half))[:2]
    up_grad = up_grad.reshape(*weight_rows, -1)
    down_grad = down_grad.reshape(*weight_rows, -1)
    far = mlp_far(up_grad, down_grad)
    passed = mlp_pass(up_grad, down_grad, *far)
    mlp_a, mlp_b = mlp_rest(up_grad, down_grad, *passed)
    up_b_grad = jnp.sum(grad_up.astype(F32), axis=0, keepdims=True)
    down_b_grad = jnp.sum(grad_own, axis=(0, 1))[None]

    att_pair, grad_middle, gain_two_grad, shift_two_grad, out_b_grad = whole_call(
        middle_back_body,
        (half, swap(half, 2), after(grad_low, *far), grad_across, middle, norm2_gain),
        [shaped(*quarter), shaped(2, rows, width, kind=F32)] + [shaped(1, width, kind=F32)] * 3,
        32,
    )
    att_beside = swap(att_pair, 1)
    att_pair = after(att_pair, *passed)

    down_part = dot("sf,ef->se", activated, down_w).reshape(2, *quarter)

    arrays = (
        att_pair,
        att_beside,
        normed,
        mixed,
        joined,
        qk_w,
        values_w,
        out_w,
        hidden,
        gain_two_grad,
        shift_two_grad,
        out_b_grad,
        down_b_grad,
        up_b_grad,
    )
    grad_norm_one, down_total, qkv_grad, out_grad, up_grad, down_grad, vector = att_scatter(
        arrays, mlp_a, mlp_b, down_part
    )
    block_out = ((middle[:, 0] + (down_total + down_bias[0])) * live).astype(BF)[:, None]
    unit_own, scale_own = normalize(own_tokens.astype(F32))
    input_grad = grad_middle + norm_back(grad_norm_one, unit_own, scale_own, norm1_gain[0])
    input_grad = input_grad.astype(BF)[:, None]

    vector = vector + swap(vector, 1) + swap(vector, 2) + swap(vector, 3)
    vector = vector[:24].reshape(1, -1)
    parts = [vector[:, k * width : (k + 1) * width] for k in range(8)]
    return (
        block_out,
        input_grad,
        jnp.transpose(qkv_grad, (1, 0, 2))[None],
        out_grad[None],
        up_grad[None],
        down_grad[None],
        *parts[:7],
        vector[:, 8 * width :],
        parts[7],
    )


def solution(mesh):
    rows = P(None, "fsdp", "tensor", None)
    matrix = P(None, "fsdp", "tensor")
    qkv = P(None, "fsdp", None, "tensor")
    return jax.shard_map(
        local,
        mesh=mesh,
        in_specs=(rows, P(None, "fsdp"), rows, qkv, matrix, matrix, matrix) + (P(),) * 9,
        out_specs=(rows, rows, qkv, matrix, matrix, matrix) + (P(),) * 9,
        check_vma=False,
    )
```

```python
import jax
import jax.numpy as jnp
from jax import lax
from jax.experimental import pallas as pl
from jax.experimental.pallas import tpu as pltpu
from jax.sharding import PartitionSpec as P

HEAD_DIM = 64
EPS_NORM = 1e-06
BF = jnp.bfloat16
F32 = jnp.float32

YH, ZN, XN = 2, 4, 4


def fsdp_perm(dx, dz, dy):
    pairs = []
    for source in range(YH * ZN * XN):
        yh, z, x = source // (ZN * XN), (source // XN) % ZN, source % XN
        target = (((yh + dy) % YH) * ZN + (z + dz) % ZN) * XN + (x + dx) % XN
        pairs.append((source, target))
    return pairs


def hop(array, axis, step):
    move = {"x": (step, 0, 0), "z": (0, step, 0), "y": (0, 0, step)}[axis]
    return lax.ppermute(array, "fsdp", fsdp_perm(*move))


def swap(array, mask):
    return lax.ppermute(array, "tensor", [(i, i ^ mask) for i in range(4)])


def here():
    index = lax.axis_index("fsdp")
    plane = ZN * XN
    return lax.div(index, plane), lax.rem(lax.div(index, XN), ZN), lax.rem(index, XN)


def turn(index, step):
    return lax.rem(index + step, 4)


def shaped(*shape, kind=BF):
    return jax.ShapeDtypeStruct(shape, kind)


def limit(mebibytes):
    return pltpu.CompilerParams(vmem_limit_bytes=mebibytes << 20)


VMEM = pl.BlockSpec(memory_space=pltpu.VMEM)
ANY = pl.BlockSpec(memory_space=pl.ANY)


def move(plan, arrays, shapes, count):
    def body(*refs):
        inputs, outputs, done = refs[: len(arrays)], refs[len(arrays) : -1], refs[-1]
        pairs = plan(inputs, outputs)
        copies = [
            pltpu.make_async_copy(source, target, done.at[spot])
            for spot, (source, target) in enumerate(pairs)
        ]
        for copy in copies:
            copy.start()
        for copy in copies:
            copy.wait()

    size = sum(item.size * 2 for item in shapes)
    return pl.pallas_call(
        body,
        out_shape=shapes,
        in_specs=[ANY] * len(arrays),
        out_specs=[VMEM] * len(shapes),
        scratch_shapes=[pltpu.SemaphoreType.DMA((count,))],
        compiler_params=limit(16),
        cost_estimate=pl.CostEstimate(flops=0, bytes_accessed=2 * size, transcendentals=0),
    )(*arrays)


def whole_call(body, arrays, shapes, mebibytes, scratch=(), cost=None):
    size = sum(item.size * item.dtype.itemsize for item in list(shapes) + list(arrays))
    cost = cost or pl.CostEstimate(flops=0, bytes_accessed=size, transcendentals=0)
    return pl.pallas_call(
        body,
        out_shape=shapes,
        scratch_shapes=scratch,
        compiler_params=limit(mebibytes),
        cost_estimate=cost,
    )(*arrays)


def after(value, *others):
    return lax.optimization_barrier((value,) + others)[0]


def near_gather(block_a, axis_a, block_b, axis_b):
    right_a, right_b = hop(block_a, axis_a, -1), hop(block_b, axis_b, -1)
    left_a, left_b = hop(block_a, axis_a, 1), hop(block_b, axis_b, 1)
    late_a, late_b = lax.optimization_barrier(
        (block_a, block_b, right_a, right_b, left_a, left_b)
    )[:2]
    far_a, far_b = hop(late_a, axis_a, 2), hop(late_b, axis_b, 2)
    return [block_a, right_a, far_a, left_a], [block_b, right_b, far_b, left_b]


def ring_gather(block, axis):
    right, left = hop(block, axis, -1), hop(block, axis, 1)
    low, high = hop(left[0], axis, 1), hop(right[1], axis, -1)
    return [block, right, left, low, high]


def near_scatter(right_a, far_a, left_a, axis_a, right_b, far_b, left_b, axis_b):
    came = [
        hop(right_a, axis_a, 1), hop(right_b, axis_b, 1),
        hop(left_a, axis_a, -1), hop(left_b, axis_b, -1),
    ]
    far_a, far_b = lax.optimization_barrier((far_a, far_b, *came))[:2]
    far_a, far_b = hop(far_a, axis_a, 2), hop(far_b, axis_b, 2)
    return (came[0], far_a, came[2]), (came[1], far_b, came[3])


def pack_plan(inputs, outputs):
    qkv, out, up, down = inputs
    own = outputs[0]
    return [
        (qkv.at[0], own.at[:, 0:256]),
        (qkv.at[1], own.at[:, 256:512]),
        (up, own.at[:, 512:1536]),
        (qkv.at[2], own.at[:, 1536:1792]),
        (out, own.at[:, 1792:2048]),
        (down, own.at[:, 2048:3072]),
    ]


def pair_body(own, other, part_a, part_b):
    yh, _, _ = here()
    part_a[yh] = own[:, :1536]
    part_b[yh] = own[:, 1536:]
    part_a[1 - yh] = other[:, :1536]
    part_b[1 - yh] = other[:, 1536:]


def first_plan(inputs, outputs):
    _, z, x = here()
    all_a, all_b = outputs
    pairs = []
    for step in range(4):
        pairs.append((inputs[step], all_a.at[:, turn(x, step)]))
        pairs.append((inputs[4 + step], all_b.at[:, turn(z, step)]))
    return pairs


def cut_plan(first, last, axis, inputs, target):
    _, z, x = here()
    columns = slice(first, last)

    def spot(step, half):
        if axis == "z":
            return target.at[half, turn(z, step)]
        return target.at[half, :, turn(x, step)]

    whole = slice(0, 2)
    pairs = []
    for piece, step in zip(inputs[:3], (0, 1, 3)):
        pairs.append((piece.at[:, :, :, columns], spot(step, whole)))
    for half in range(2):
        pairs.append((inputs[3 + half].at[:, :, columns], spot(2, half)))
    return pairs


def att_plan(inputs, outputs):
    qk_w, values_w, out_w = outputs
    return (
        cut_plan(0, 512, "z", inputs[:5], qk_w)
        + cut_plan(0, 256, "x", inputs[5:], values_w)
        + cut_plan(256, 512, "x", inputs[5:], out_w)
    )


def mlp_plan(inputs, outputs):
    up_w, down_w = outputs
    return cut_plan(512, 1536, "z", inputs[:5], up_w) + cut_plan(
        512, 1536, "x", inputs[5:], down_w
    )


def far_plan(inputs, outputs):
    _, z, x = here()
    grad_a, grad_b = inputs
    pairs = []
    for half in range(2):
        pairs.append((grad_a.at[half, turn(z, 2)], outputs[half]))
        pairs.append((grad_b.at[half, :, turn(x, 2)], outputs[2 + half]))
    return pairs


def fetch(pairs, done):
    copies = [
        pltpu.make_async_copy(source, target, done.at[spot])
        for spot, (source, target) in enumerate(pairs)
    ]
    for copy in copies:
        copy.start()
    for copy in copies:
        copy.wait()


def pass_body(grad_a, grad_b, low_a, high_a, low_b, high_b, ra, la, rb, lb, held, done):
    _, z, x = here()
    fetch(
        [
            (grad_a.at[:, turn(z, 1)], held.at[0]),
            (grad_a.at[:, turn(z, 3)], held.at[1]),
            (grad_b.at[:, :, turn(x, 1)], held.at[2]),
            (grad_b.at[:, :, turn(x, 3)], held.at[3]),
        ],
        done,
    )
    for spot, (right, left, low, high) in enumerate(
        ((ra, la, low_a, high_a), (rb, lb, low_b, high_b))
    ):
        right[0] = add(held[2 * spot, 0], low[...])
        right[1] = held[2 * spot, 1]
        left[0] = held[2 * spot + 1, 0]
        left[1] = add(held[2 * spot + 1, 1], high[...])


def rest_body(grad_a, grad_b, la, ra, lb, rb, total_a, total_b, held, done):
    _, z, x = here()
    fetch(
        [(grad_a.at[:, turn(z, 0)], held.at[0]), (grad_b.at[:, :, turn(x, 0)], held.at[1])],
        done,
    )
    total_a[...] = add(held[0], la[...], ra[...])
    total_b[...] = add(held[1], lb[...], rb[...])


def held_call(body, whole, arrays, shapes, slots, block, mebibytes):
    size = sum(item.size * 2 for item in shapes) + sum(item.size * 2 for item in arrays)
    return pl.pallas_call(
        body,
        out_shape=shapes,
        in_specs=[ANY] * len(whole) + [VMEM] * len(arrays),
        out_specs=[VMEM] * len(shapes),
        scratch_shapes=[pltpu.VMEM((slots,) + block, BF), pltpu.SemaphoreType.DMA((slots,))],
        compiler_params=limit(mebibytes),
        cost_estimate=pl.CostEstimate(flops=0, bytes_accessed=2 * size, transcendentals=0),
    )(*whole, *arrays)


def mlp_far(grad_a, grad_b):
    halves = move(far_plan, (grad_a, grad_b), [shaped(4, 32, 1024)] * 4, 4)
    low_a, high_a, low_b, high_b = halves
    return hop(low_a, "z", 1), hop(high_a, "z", -1), hop(low_b, "x", 1), hop(high_b, "x", -1)


def mlp_pass(grad_a, grad_b, *recv):
    block = (2, 4, 32, 1024)
    return held_call(pass_body, (grad_a, grad_b), recv, [shaped(*block)] * 4, 4, block, 40)


def mlp_rest(grad_a, grad_b, ra, la, rb, lb):
    block = (2, 4, 32, 1024)
    recv = (hop(ra, "z", 1), hop(la, "z", -1), hop(rb, "x", 1), hop(lb, "x", -1))
    return held_call(rest_body, (grad_a, grad_b), recv, [shaped(*block)] * 2, 2, block, 40)


def add(*terms):
    total = terms[0].astype(F32)
    for term in terms[1:]:
        total = total + term.astype(F32)
    return total.astype(BF)


def contract(left, right, dims):
    return lax.dot_general(left, right, (dims, ((), ())), preferred_element_type=F32)


ROWS = ((1,), (0,))
BOTH = ((1,), (1,))
TOPS = ((0,), (0,))
SCALE = HEAD_DIM ** (-0.5)


def probabilities(query, keys):
    scores = contract(query, keys, BOTH) * SCALE
    weight = jnp.exp(scores - jnp.max(scores, axis=-1, keepdims=True))
    return weight / jnp.sum(weight, axis=-1, keepdims=True)


def att_body(normed, qk_w, values_w, out_w, query_b, value_b, joined, mixed, sent, kept):
    spot = pl.ds(pl.multiple_of(lax.axis_index("tensor") * 256, 256), 256)
    rows = normed[...]
    mixer = out_w[...].reshape(1024, 256)
    pair = contract(rows, qk_w[...].reshape(1024, 512), ROWS)
    joined[:, 0:256] = (pair[:, 0:256] + query_b[:, spot]).astype(BF)
    joined[:, 256:512] = pair[:, 256:].astype(BF)
    last = contract(rows, values_w[...].reshape(1024, 256), ROWS)
    joined[:, 512:768] = (last + value_b[:, spot]).astype(BF)
    for image in range(2):
        line = slice(image * 256, image * 256 + 256)
        parts = []
        for head in range(4):
            query, keys, values = (
                joined[line, base + head * 64 : base + head * 64 + 64] for base in (0, 256, 512)
            )
            probs = probabilities(query, keys).astype(BF)
            parts.append(contract(probs, values, ROWS).astype(BF))
        whole = jnp.concatenate(parts, axis=1)
        mixed[line, :] = whole
        split_blocks(image, contract(whole, mixer, BOTH), sent, kept)


def split_blocks(image, part, sent, kept):
    for spot in range(2):
        kept[image, spot] = part[spot * 64 : spot * 64 + 64]
        sent[image, spot] = part[128 + spot * 64 : 192 + spot * 64].astype(BF)


def middle_body(half, came, own, across, out_b, gain, shift, normed, middle):
    for image in range(2):
        for spot, piece in enumerate((own, across)):
            total = half[image, spot].astype(F32) + came[image, 1 - spot].astype(F32)
            value = piece[image].astype(F32) + (total + out_b[...])
            middle[image, spot] = value
            unit, _ = normalize(value)
            normed[image, spot] = (unit * gain[...] + shift[...]).astype(BF)


def middle_back_body(
    half, came, own, across, middle, gain, att, grad, gain_grad, shift_grad, out_b_grad
):
    sums = [jnp.zeros((1, 1024), F32) for _ in range(3)]
    for image in range(2):
        for spot, piece in enumerate((own, across)):
            total = half[image, spot].astype(F32) + came[image, 1 - spot].astype(F32)
            unit, scale = normalize(middle[image, spot])
            value = piece[image].astype(F32) + norm_back(total, unit, scale, gain[...])
            low = value.astype(BF)
            att[image, spot] = low
            if spot == 0:
                grad[image] = value
                for place, item in enumerate((total * unit, total, low.astype(F32))):
                    sums[place] = sums[place] + jnp.sum(item, axis=0, keepdims=True)
    gain_grad[...], shift_grad[...], out_b_grad[...] = sums


def collect_far(kept, sent):
    return kept + swap(sent, 2).astype(F32)


def normalize(values):
    center = values - jnp.mean(values, axis=-1, keepdims=True)
    scale = lax.rsqrt(jnp.mean(center * center, axis=-1, keepdims=True) + EPS_NORM)
    return center * scale, scale


def norm_back(grad, unit, scale, gain):
    inner = grad * gain
    first = jnp.mean(inner, axis=-1, keepdims=True)
    second = jnp.mean(inner * unit, axis=-1, keepdims=True)
    return scale * (inner - first - unit * second)


def back_body(
    pair, beside, normed, mixed, joined, qk_w, values_w, out_w, hidden, gain_two, shift_two,
    out_b, down_b, up_b, sent, kept, vector, *rest,
):
    sends_a, sends_b, own_a, own_b = rest[0:3], rest[3:6], rest[6], rest[7]
    grads, att, grad_a, grad_b, low, done = rest[8:]
    tensor = lax.axis_index("tensor")
    for image in range(2):
        for spot, piece in enumerate((pair, beside)):
            first = image * 256 + spot * 128
            att[first : first + 128, :] = piece[image].reshape(128, 1024)
    pair_w = qk_w[...].reshape(1024, 512)
    last_w = values_w[...].reshape(1024, 256)
    mixer = out_w[...].reshape(1024, 256)
    gain = jnp.zeros((1, 1024), F32)
    shift = jnp.zeros((1, 1024), F32)
    for image in range(2):
        line = slice(image * 256, image * 256 + 256)
        grad_mixed = contract(att[line, :], mixer, ROWS).astype(BF)
        parts = ([], [], [])
        for head in range(4):
            query, keys, values = (
                joined[line, base + head * 64 : base + head * 64 + 64] for base in (0, 256, 512)
            )
            grad = grad_mixed[:, head * 64 : head * 64 + 64]
            probs = probabilities(query, keys)
            grad_prob = contract(grad, values, BOTH)
            inner = jnp.sum(grad_prob * probs, axis=-1, keepdims=True)
            score = (probs * (grad_prob - inner)).astype(BF)
            parts[0].append((contract(score, keys, ROWS) * SCALE).astype(BF))
            parts[1].append((contract(score, query, TOPS) * SCALE).astype(BF))
            parts[2].append(contract(probs.astype(BF), grad, TOPS).astype(BF))
        for kind in range(3):
            grads[line, kind * 256 : kind * 256 + 256] = jnp.concatenate(parts[kind], axis=1)
        norm_grad = contract(grads[line, :512], pair_w, BOTH) + contract(
            grads[line, 512:], last_w, BOTH
        )
        unit, _ = normalize(hidden[line, :].astype(F32))
        gain = gain + jnp.sum(norm_grad * unit, axis=0, keepdims=True)
        shift = shift + jnp.sum(norm_grad, axis=0, keepdims=True)
        split_blocks(image, norm_grad, sent, kept)
    vector[...] = jnp.zeros(vector.shape, F32)
    rows = (
        (0, gain), (2, shift), (8, out_b[...]), (10, gain_two[...]), (12, shift_two[...]),
        (14, down_b[...]),
    )
    for row, value in rows:
        vector[row : row + 1, :] = value[:, :512]
        vector[row + 1 : row + 2, :] = value[:, 512:]
    spot = pl.ds(pl.multiple_of(lax.rem(tensor, 2) * 256, 256), 256)
    for row, base in ((4, 0), (6, 512)):
        part = jnp.sum(grads[:, base : base + 256].astype(F32), axis=0, keepdims=True)
        vector[pl.ds(row + lax.div(tensor, 2), 1), spot] = part
    vector[pl.ds(16 + 2 * tensor, 1), :] = up_b[:, :512]
    vector[pl.ds(17 + 2 * tensor, 1), :] = up_b[:, 512:]
    _, z, x = here()
    grad_a[...] = contract(normed[...], grads[:, 0:512], TOPS).astype(BF).reshape(grad_a.shape)
    pairs = [(grad_a.at[:, turn(z, 0)], own_a)]
    low[...] = vector[...].astype(BF)
    for step in range(1, 4):
        target = sends_a[step - 1]
        for half in range(2):
            pairs.append((grad_a.at[half, turn(z, step)], target.at[pl.ds(4 * half, 4)]))
        pairs.append((low, target.at[8]))
    copies = [
        pltpu.make_async_copy(source, target, done.at[spot])
        for spot, (source, target) in enumerate(pairs)
    ]
    for copy in copies:
        copy.start()
    last = contract(normed[...], grads[:, 512:768], TOPS).astype(BF)
    grad_b[:, :, :, :, 0:256] = last.reshape(2, 4, 4, 32, 256)
    last = contract(att[...], mixed[...], TOPS).astype(BF)
    grad_b[:, :, :, :, 256:512] = last.reshape(2, 4, 4, 32, 256)
    others = [(grad_b.at[:, :, turn(x, 0)], own_b)]
    for step in range(1, 4):
        others.append((grad_b.at[:, :, turn(x, step)], sends_b[step - 1]))
    more = [
        pltpu.make_async_copy(source, target, done.at[len(pairs) + spot])
        for spot, (source, target) in enumerate(others)
    ]
    for copy in more:
        copy.start()
    for copy in copies + more:
        copy.wait()


def second_body(*refs):
    a1, a2, a3, own_a, b1, b2, b3, own_b, vector, mlp_a, mlp_b = refs[:11]
    outs_a, outs_b, sum_a, sum_b = refs[11:15], refs[15:19], refs[19], refs[20]
    _, z, x = here()
    for yh in range(2):
        part = slice(4 * yh, 4 * yh + 4)
        sum_a[yh] = add(own_a[yh], a1[part], a2[part], a3[part])
        sum_b[yh] = add(own_b[yh], b1[yh], b2[yh], b3[yh])
    low = add(vector[...], a1[8], a2[8], a3[8])
    for step in range(4):
        for out, total, mlp, index in (
            (outs_a[step], sum_a, mlp_a, turn(x, step)),
            (outs_b[step], sum_b, mlp_b, turn(z, step)),
        ):
            for yh in range(2):
                out[yh] = total[yh, index]
                out[2 + yh] = mlp[yh, index, :, 0:512]
                out[4 + yh] = mlp[yh, index, :, 512:1024]
        outs_a[step][6] = low


def third_body(a0, a1, a2, a3, b0, b1, b2, b3, send, own):
    yh, _, _ = here()
    for spot in range(3):
        for base, pieces in ((0, (a0, a1, a2, a3)), (3, (b0, b1, b2, b3))):
            mine = [piece[2 * spot + yh].astype(F32) for piece in pieces]
            other = [piece[2 * spot + 1 - yh].astype(F32) for piece in pieces]
            own[base + spot] = (mine[0] + mine[1]) + (mine[2] + mine[3])
            send[base + spot] = ((other[0] + other[1]) + (other[2] + other[3])).astype(BF)
    total = [piece[6].astype(F32) for piece in (a0, a1, a2, a3)]
    total = (total[0] + total[1]) + (total[2] + total[3])
    own[6] = total
    send[6] = total.astype(BF)


def last_body(own, came, qkv, out, up, down, vector):
    def total(spot):
        return own[spot] + came[spot].astype(F32)

    att_a, att_b = total(0), total(3)
    qkv[0] = att_a[:, 0:256]
    qkv[1] = att_a[:, 256:512]
    qkv[2] = att_b[:, 0:256]
    out[...] = att_b[:, 256:512]
    up[:, 0:512] = total(1)
    up[:, 512:1024] = total(2)
    down[:, 0:512] = total(4)
    down[:, 512:1024] = total(5)
    vector[...] = total(6)


def att_scatter(arrays, mlp_a, mlp_b, down_part):
    block = (2, 4, 32, 512)
    shapes = [
        shaped(2, 2, 64, 1024),
        shaped(2, 2, 64, 1024, kind=F32),
        shaped(32, 512, kind=F32),
    ]
    shapes += [shaped(9, 32, 512)] * 3 + [shaped(*block)] * 5
    sent, kept, vector, *results = pl.pallas_call(
        back_body,
        out_shape=shapes,
        in_specs=[VMEM] * len(arrays),
        out_specs=[VMEM] * 3 + [ANY] * 8,
        scratch_shapes=[
            pltpu.VMEM((512, 768), BF),
            pltpu.VMEM((512, 1024), BF),
            pltpu.VMEM((2, 4, 4, 32, 512), BF),
            pltpu.VMEM((2, 4, 4, 32, 512), BF),
            pltpu.VMEM((32, 512), BF),
            pltpu.SemaphoreType.DMA((14,)),
        ],
        compiler_params=limit(56),
    )(*arrays)
    near = swap(jnp.stack([sent, down_part[1].astype(BF)]), 1).astype(F32)
    sums = [kept + near[0], down_part[0] + near[1]]
    came = swap(jnp.stack([item[:, 1].astype(BF) for item in sums]), 2)
    totals = [item[:, 0] + came[spot].astype(F32) for spot, item in enumerate(sums)]
    results = lax.optimization_barrier((*results, mlp_a))[:-1]
    came_a, came_b = near_scatter(*results[:3], "z", *results[3:6], "x")
    pieces = whole_call(
        second_body,
        (*came_a, results[6], *came_b, results[7], vector, mlp_a, mlp_b),
        [shaped(7, 32, 512)] * 4 + [shaped(6, 32, 512)] * 4,
        40,
        scratch=[pltpu.VMEM(block, BF), pltpu.VMEM(block, BF)],
    )
    came_a, came_b = near_scatter(*pieces[1:4], "x", *pieces[5:8], "z")
    send, own = whole_call(
        third_body,
        (pieces[0], *came_a, pieces[4], *came_b),
        [shaped(7, 32, 512), shaped(7, 32, 512, kind=F32)],
        40,
    )
    send = after(send, came)
    shapes = [(3, 32, 256), (32, 256), (32, 1024), (32, 1024), (32, 512)]
    results = whole_call(
        last_body, (own, hop(send, "y", 1)), [shaped(*shape, kind=F32) for shape in shapes], 40
    )
    return *totals, *results


def dot(spec, left, right):
    return jnp.einsum(spec, left, right, preferred_element_type=F32)


def local(
    tokens,
    dealt,
    cotangent,
    qkv_weight,
    out_weight,
    up_weight,
    down_weight,
    norm1_gain,
    norm1_bias,
    query_bias,
    value_bias,
    out_bias,
    norm2_gain,
    norm2_bias,
    up_bias,
    down_bias,
):
    tensor = lax.axis_index("tensor")
    rows = tokens.shape[2]
    width = tokens.shape[3]
    count = 8 * rows
    weight_rows = (YH, ZN, XN, 32)

    def own_part(vector, size):
        return lax.dynamic_slice_in_dim(vector[0], tensor * size, size, 0)

    (own,) = move(
        pack_plan,
        (jnp.transpose(qkv_weight[0], (1, 0, 2)), out_weight[0], up_weight[0], down_weight[0]),
        [shaped(32, 3072)],
        6,
    )
    other = hop(own, "y", 1)
    part_a, part_b = whole_call(pair_body, (own, other), [shaped(2, 32, 1536)] * 2, 16)
    pieces_a, pieces_b = near_gather(part_a, "x", part_b, "z")
    all_a, all_b = move(first_plan, pieces_a + pieces_b, [shaped(2, 4, 32, 1536)] * 2, 8)
    ring = ring_gather(all_a, "z") + ring_gather(all_b, "x")
    shapes = [shaped(*weight_rows, 512), shaped(*weight_rows, 256), shaped(*weight_rows, 256)]
    qk_w, values_w, out_w = move(att_plan, ring, shapes, 15)
    up_w, down_w = move(mlp_plan, ring, [shaped(*weight_rows, 1024)] * 2, 10)
    up_w, down_w = up_w.reshape(width, -1), down_w.reshape(width, -1)

    live = dealt.astype(F32).reshape(2, 1, 1)
    own_tokens = tokens[:, 0]
    grad_own = cotangent[:, 0].astype(F32) * live
    grad_low = grad_own.astype(BF)
    both = jnp.stack([own_tokens, grad_low])
    across = swap(both, 2)
    across = after(across, ring[1], ring[2])
    pair = jnp.stack([both, across], axis=2)
    beside = swap(pair, 1)
    hidden = jnp.stack([pair[0], beside[0]], axis=1).reshape(count, width)
    down_all = jnp.stack([pair[1], beside[1]]).reshape(count, width)
    across, grad_across = across[0], across[1]
    unit_one, _ = normalize(hidden.astype(F32))
    normed = (unit_one * norm1_gain[0] + norm1_bias[0]).astype(BF)
    quarter = (2, 2, rows, width)
    joined, mixed, sent, kept = whole_call(
        att_body,
        (normed, qk_w, values_w, out_w, query_bias, value_bias),
        [shaped(count, 768), shaped(count, 256), shaped(*quarter), shaped(*quarter, kind=F32)],
        48,
    )
    half = (kept + swap(sent, 1).astype(F32)).astype(BF)
    normed_pair, middle = whole_call(
        middle_body,
        (half, swap(half, 2), own_tokens, across, out_bias, norm2_gain, norm2_bias),
        [shaped(*quarter), shaped(*quarter, kind=F32)],
        32,
    )
    normed_two = jnp.stack([normed_pair, swap(normed_pair, 1)]).reshape(count, width)
    upward = dot("sd,df->sf", normed_two, up_w) + own_part(up_bias, 1024)
    share = 0.5 * (1.0 + lax.erf(upward * (0.5**0.5)))
    activated = (upward * share).astype(BF)
    slope = share + upward * (jnp.exp(-0.5 * upward * upward) * (0.5 / jnp.pi) ** 0.5)

    grad_up = (dot("se,ef->sf", down_all, down_w) * slope).astype(BF)
    norm_two_part = dot("sf,df->sd", grad_up, up_w).reshape(2, *quarter)
    half = (norm_two_part[0] + swap(norm_two_part[1].astype(BF), 1).astype(F32)).astype(BF)
    up_grad = dot("sd,sf->df", normed_two, grad_up).astype(BF)
    down_grad = dot("se,sf->ef", down_all, activated).astype(BF)
    up_grad, down_grad = lax.optimization_barrier((up_grad, down_grad, half))[:2]
    up_grad = up_grad.reshape(*weight_rows, -1)
    down_grad = down_grad.reshape(*weight_rows, -1)
    far = mlp_far(up_grad, down_grad)
    passed = mlp_pass(up_grad, down_grad, *far)
    mlp_a, mlp_b = mlp_rest(up_grad, down_grad, *passed)
    up_b_grad = jnp.sum(grad_up.astype(F32), axis=0, keepdims=True)
    down_b_grad = jnp.sum(grad_own, axis=(0, 1))[None]

    att_pair, grad_middle, gain_two_grad, shift_two_grad, out_b_grad = whole_call(
        middle_back_body,
        (half, swap(half, 2), after(grad_low, *far), grad_across, middle, norm2_gain),
        [shaped(*quarter), shaped(2, rows, width, kind=F32)] + [shaped(1, width, kind=F32)] * 3,
        32,
    )
    att_beside = swap(att_pair, 1)
    att_pair = after(att_pair, *passed)

    down_part = dot("sf,ef->se", activated, down_w).reshape(2, *quarter)

    arrays = (
        att_pair,
        att_beside,
        normed,
        mixed,
        joined,
        qk_w,
        values_w,
        out_w,
        hidden,
        gain_two_grad,
        shift_two_grad,
        out_b_grad,
        down_b_grad,
        up_b_grad,
    )
    grad_norm_one, down_total, qkv_grad, out_grad, up_grad, down_grad, vector = att_scatter(
        arrays, mlp_a, mlp_b, down_part
    )
    block_out = ((middle[:, 0] + (down_total + down_bias[0])) * live).astype(BF)[:, None]
    unit_own, scale_own = normalize(own_tokens.astype(F32))
    input_grad = grad_middle + norm_back(grad_norm_one, unit_own, scale_own, norm1_gain[0])
    input_grad = input_grad.astype(BF)[:, None]

    vector = vector + swap(vector, 1) + swap(vector, 2) + swap(vector, 3)
    vector = vector[:24].reshape(1, -1)
    parts = [vector[:, k * width : (k + 1) * width] for k in range(8)]
    return (
        block_out,
        input_grad,
        jnp.transpose(qkv_grad, (1, 0, 2))[None],
        out_grad[None],
        up_grad[None],
        down_grad[None],
        *parts[:7],
        vector[:, 8 * width :],
        parts[7],
    )


def solution(mesh):
    rows = P(None, "fsdp", "tensor", None)
    matrix = P(None, "fsdp", "tensor")
    qkv = P(None, "fsdp", None, "tensor")
    return jax.shard_map(
        local,
        mesh=mesh,
        in_specs=(rows, P(None, "fsdp"), rows, qkv, matrix, matrix, matrix) + (P(),) * 9,
        out_specs=(rows, rows, qkv, matrix, matrix, matrix) + (P(),) * 9,
        check_vma=False,
    )
```
